32 devices in a mesh: dp: 16 (over z, y, x), tm: 2 (over core).
Axes of the slice: x: 2, y: 2, z: 4, core: 2. Of those that a mesh axis runs over, the one named last changes fastest.
Arguments:
- frames: bfloat16 [8192, 1024], P(('dp', 'tm')), may hold values from -6 to 6
- clip_lengths: int32 [16, 3], P('dp'), may hold values from 1 to 384, as said below
- cotangent: bfloat16 [8192, 1024], P(('dp', 'tm')), may hold values from -6 to 6
- attend_in: float32 [1024, 3072], P(('dp', 'tm')), may hold values from -0.1875 to 0.1875
- attend_out: float32 [1024, 1024], P(('dp', 'tm')), may hold values from -1.5 to 1.5
- expand: float32 [1024, 8192], P(('dp', 'tm')), may hold values from -0.1875 to 0.1875
- contract: float32 [1024, 4096], P(('dp', 'tm')), may hold values from -0.09375 to 0.09375
- gains: float32 [6, 1024], P(None, ('dp', 'tm'))
- prior_mean_attend_in: float32 [1024, 3072], P(('dp', 'tm')), may hold values from -0.00015258789 to 0.00015258789
- prior_mean_attend_out: float32 [1024, 1024], P(('dp', 'tm')), may hold values from -0.00015258789 to 0.00015258789
- prior_mean_expand: float32 [1024, 8192], P(('dp', 'tm')), may hold values from -0.00015258789 to 0.00015258789
- prior_mean_contract: float32 [1024, 4096], P(('dp', 'tm')), may hold values from -0.00015258789 to 0.00015258789
- prior_mean_gains: float32 [6, 1024], P(None, ('dp', 'tm')), may hold values from -0.00061035156 to 0.00061035156
- prior_square_attend_in: float32 [1024, 3072], P(('dp', 'tm')), may hold values from 8.937424e-11 to 3.5749695e-10
- prior_square_attend_out: float32 [1024, 1024], P(('dp', 'tm')), may hold values from 8.937424e-11 to 3.5749695e-10
- prior_square_expand: float32 [1024, 8192], P(('dp', 'tm')), may hold values from 8.937424e-11 to 3.5749695e-10
- prior_square_contract: float32 [1024, 4096], P(('dp', 'tm')), may hold values from 8.937424e-11 to 3.5749695e-10
- prior_square_gains: float32 [6, 1024], P(None, ('dp', 'tm')), may hold values from 1.4299878e-09 to 5.719951e-09
Outputs:
- out_frames: bfloat16 [8192, 1024], P(('dp', 'tm'))
- frames_grad: float32 [8192, 1024], P(('dp', 'tm'))
- grad_norm: float32 [], replicated
- mean_attend_in: float32 [1024, 3072], P(('dp', 'tm'))
- square_attend_in: float32 [1024, 3072], P(('dp', 'tm'))
- moved_attend_in: float32 [1024, 3072], P(('dp', 'tm'))
- lowered_attend_in: bfloat16 [1024, 3072], P(('dp', 'tm'))
- mean_attend_out: float32 [1024, 1024], P(('dp', 'tm'))
- square_attend_out: float32 [1024, 1024], P(('dp', 'tm'))
- moved_attend_out: float32 [1024, 1024], P(('dp', 'tm'))
- lowered_attend_out: bfloat16 [1024, 1024], P(('dp', 'tm'))
- mean_expand: float32 [1024, 8192], P(('dp', 'tm'))
- square_expand: float32 [1024, 8192], P(('dp', 'tm'))
- moved_expand: float32 [1024, 8192], P(('dp', 'tm'))
- lowered_expand: bfloat16 [1024, 8192], P(('dp', 'tm'))
- mean_contract: float32 [1024, 4096], P(('dp', 'tm'))
- square_contract: float32 [1024, 4096], P(('dp', 'tm'))
- moved_contract: float32 [1024, 4096], P(('dp', 'tm'))
- lowered_contract: bfloat16 [1024, 4096], P(('dp', 'tm'))
- mean_gains: float32 [6, 1024], P(None, ('dp', 'tm'))
- square_gains: float32 [6, 1024], P(None, ('dp', 'tm'))
- moved_gains: float32 [6, 1024], P(None, ('dp', 'tm'))
- lowered_gains: bfloat16 [6, 1024], P(None, ('dp', 'tm'))
The draws below stay inside these ranges and needn't reach their ends.
Inputs may be any that keep to these rules, and one draw needn't show every extreme that they name: `clip_lengths`: row g lists in order the lengths of the clips of group g; they sum to 512. Each row holds three clips: one shorter clip, then the longest of exactly 384 frames (a window of a longer recording), then one more shorter clip.
All inputs are finite; a program needn't handle non-finite values.
Results may differ from the reference program's by a relative error of at most 0.013.
The reference program's roundings to bfloat16 on the way count: a program that leaves them out, or rounds other values in their place, can miss the bound.
Values may be sent and summed in bfloat16 or wider, within the bound.
No kernel may reach another device: no remote copies, remote signals or barrier semaphores. Data moves between devices by JAX's collectives and lax.ppermute only.
A program may use at most 320 MiB of HBM per device.

```python
import math
import jax
import jax.numpy as jnp
import numpy as np
from jax import lax

D = 1024
HEADS = 16
HEAD = 64
FF = 4096
WINDOW = 128
STEP = 10
TOK_DEV = 256
GROUP = 512
FRAMES = 8192
PIECES = 1
N_DP = 16


def draw_clip_lengths(key, part):
    key = jax.random.fold_in(key, 11)
    shift = jax.random.randint(key, (N_DP,), TOK_DEV // 8, 3 * TOK_DEV // 8 + 1).astype(jnp.int32)
    after = (TOK_DEV // 2 - shift).astype(jnp.int32)
    index = jnp.arange(PIECES, dtype=jnp.int32)

    def split_even(total):
        base = total[:, None] // PIECES
        extra = (index[None, :] < total[:, None] % PIECES).astype(jnp.int32)
        return (base + extra).astype(jnp.int32)
    longest = jnp.full((N_DP, 1), GROUP - TOK_DEV // 2, jnp.int32)
    return jnp.concatenate([split_even(shift), longest, split_even(after)], axis=1)


def draw_gains(key, part):
    key = jax.random.fold_in(key, 23)
    rough_key, shift_key = jax.random.split(key, 2)
    place = jnp.arange(D, dtype=jnp.float32) / (D - 1)
    low_end = 0.55
    high_end = 1.65
    trend = low_end * (high_end / low_end) ** place
    rough = jax.random.uniform(rough_key, (4, D), jnp.float32, 0.75, 1.5)
    scales = trend[None, :] * rough
    shifts = 0.3 * jax.random.normal(shift_key, (2, D), jnp.float32)
    return jnp.stack([scales[0], shifts[0], scales[1], shifts[1], scales[2], scales[3]], axis=0)


def block_levels(stream_key, shape, cuts, smallest, largest):
    factor_of = 1.0
    for dim, shards_of in cuts:
        draws = jax.random.uniform(jax.random.fold_in(jax.random.fold_in(stream_key, 6), dim), (shards_of,), jnp.float32, smallest / len(cuts), largest / len(cuts))
        factor_of = factor_of * jnp.repeat(jnp.exp(draws), shape[dim] // shards_of).reshape((-1,) + (1,) * (len(shape) - 1 - dim))
    return factor_of


def gaussian(own_key, dims, width, limit, cuts=(), kind=jnp.bfloat16):
    level = block_levels(own_key, dims, cuts, -0.22, 0.18) if cuts else 1.0
    array = jax.random.normal(own_key, dims, jnp.float32) * width * level
    return jnp.minimum(jnp.maximum(array, -limit), limit).astype(kind)


def setup_inputs(seed: int = 0) -> dict:
    keys = jax.random.split(jax.random.key(seed), 19)
    frames = gaussian(keys[0], (FRAMES, D), 1.0, 6.0, ((0, 32),))
    clip_lengths = draw_clip_lengths(jax.random.fold_in(keys[18], 71), 0)
    cotangent = gaussian(keys[2], (FRAMES, D), 1.0, 6.0, ((0, 32),))
    attend_in = gaussian(keys[3], (D, 3 * D), D ** -0.5, 0.1875, ((0, 32),), jnp.float32)
    attend_out = gaussian(keys[4], (D, D), (D // 64) ** -0.5, 1.5, ((0, 32),), jnp.float32)
    expand = gaussian(keys[5], (D, 2 * FF), D ** -0.5, 0.1875, ((0, 32),), jnp.float32)
    contract = gaussian(keys[6], (D, FF), FF ** -0.5, 0.09375, ((0, 32),), jnp.float32)
    gains = draw_gains(jax.random.fold_in(keys[18], 71), 0)
    prior_mean_attend_in = gaussian(keys[8], (D, 3 * D), (0.111 / (4 * D * D + 3 * D * FF + 6 * D) ** 0.5), 0.00015258789, ((0, 32),), jnp.float32)
    prior_mean_attend_out = gaussian(keys[9], (D, D), (0.111 / (4 * D * D + 3 * D * FF + 6 * D) ** 0.5), 0.00015258789, ((0, 32),), jnp.float32)
    prior_mean_expand = gaussian(keys[10], (D, 2 * FF), (0.111 / (4 * D * D + 3 * D * FF + 6 * D) ** 0.5), 0.00015258789, ((0, 32),), jnp.float32)
    prior_mean_contract = gaussian(keys[11], (D, FF), (0.111 / (4 * D * D + 3 * D * FF + 6 * D) ** 0.5), 0.00015258789, ((0, 32),), jnp.float32)
    prior_mean_gains = gaussian(keys[12], (6, D), (0.444 / (4 * D * D + 3 * D * FF + 6 * D) ** 0.5), 0.00061035156, ((1, 32),), jnp.float32)
    prior_square_attend_in = jnp.clip(jnp.exp(math.log(3.574969487107893e-10) - 1.3862944 * jax.random.uniform(keys[13], (D, 3 * D), jnp.float32) ** block_levels(keys[13], (D, 3 * D), ((0, 32),), -0.2, 0.2)), 8.937423717769732e-11, 3.574969487107893e-10)
    prior_square_attend_out = jnp.clip(jnp.exp(math.log(3.574969487107893e-10) - 1.3862944 * jax.random.uniform(keys[14], (D, D), jnp.float32) ** block_levels(keys[14], (D, D), ((0, 32),), -0.2, 0.2)), 8.937423717769732e-11, 3.574969487107893e-10)
    prior_square_expand = jnp.clip(jnp.exp(math.log(3.574969487107893e-10) - 1.3862944 * jax.random.uniform(keys[15], (D, 2 * FF), jnp.float32) ** block_levels(keys[15], (D, 2 * FF), ((0, 32),), -0.2, 0.2)), 8.937423717769732e-11, 3.574969487107893e-10)
    prior_square_contract = jnp.clip(jnp.exp(math.log(3.574969487107893e-10) - 1.3862944 * jax.random.uniform(keys[16], (D, FF), jnp.float32) ** block_levels(keys[16], (D, FF), ((0, 32),), -0.2, 0.2)), 8.937423717769732e-11, 3.574969487107893e-10)
    prior_square_gains = jnp.clip(jnp.exp(math.log(5.719951179372629e-09) - 1.3862944 * jax.random.uniform(keys[17], (6, D), jnp.float32) ** block_levels(keys[17], (6, D), ((1, 32),), -0.2, 0.2)), 1.4299877948431572e-09, 5.719951179372629e-09)
    return {"frames": frames, "clip_lengths": clip_lengths, "cotangent": cotangent, "attend_in": attend_in, "attend_out": attend_out, "expand": expand, "contract": contract, "gains": gains, "prior_mean_attend_in": prior_mean_attend_in, "prior_mean_attend_out": prior_mean_attend_out, "prior_mean_expand": prior_mean_expand, "prior_mean_contract": prior_mean_contract, "prior_mean_gains": prior_mean_gains, "prior_square_attend_in": prior_square_attend_in, "prior_square_attend_out": prior_square_attend_out, "prior_square_expand": prior_square_expand, "prior_square_contract": prior_square_contract, "prior_square_gains": prior_square_gains}


@jax.custom_vjp
def low(v):
    return lax.optimization_barrier(v.astype(jnp.bfloat16)).astype(jnp.float32)

@jax.custom_vjp
def low_back(v):
    return v

def low_keep(v):
    return (low(v), None)

def low_pass(kept, grad):
    return (grad,)

def back_keep(v):
    return (v, None)

def back_low(kept, grad):
    return (low(grad),)
low.defvjp(low_keep, low_pass)
low_back.defvjp(back_keep, back_low)
EPS_NORM = 1e-05
NEG_FILL = -1e+30
SCORE_SCALE = 0.125
BETA_ONE = 0.9
BETA_TWO = 0.999
ADAM_EPS = 1e-08
DECAY = 0.1
RATE = 3.0
VECTOR_RATE = 0.6
CLIP_NORM = 1.0
PRECISE = lax.Precision.HIGHEST

def clip_index(lengths, places):
    ends = jnp.cumsum(lengths).astype(jnp.int32)
    ids = lax.optimization_barrier(jnp.sum((places[:, None] >= ends[None, :]).astype(jnp.int32), axis=1)).astype(jnp.int32)
    return jnp.where(places < 0, -1, ids).astype(jnp.int32)

def clip_offsets(lengths, places):
    ends = jnp.cumsum(lengths).astype(jnp.int32)
    starts = (ends - lengths).astype(jnp.int32)
    begin = lax.optimization_barrier(jnp.max(jnp.where(starts[None, :] <= places[:, None], starts[None, :], 0), axis=1))
    return (places - begin).astype(jnp.int32)

def rotary_table(offsets):
    freqs = jnp.asarray(np.power(10000.0, -2.0 * np.arange(HEAD // 2) / HEAD), dtype=jnp.float32)
    angles = offsets.astype(jnp.float32)[:, None] * freqs[None, :]
    return (jnp.cos(angles)[:, None, :], jnp.sin(angles)[:, None, :])

def rotate(values, cosines, sine_values):
    first_half = values[..., :HEAD // 2]
    second_half = values[..., HEAD // 2:]
    return jnp.concatenate([first_half * cosines - second_half * sine_values, first_half * sine_values + second_half * cosines], axis=-1)

def layer_norm(values, gain_row, bias_row):
    centered = values - lax.optimization_barrier(jnp.mean(values, axis=-1, keepdims=True))
    scaling = lax.rsqrt(lax.optimization_barrier(jnp.mean(centered * centered, axis=-1, keepdims=True)) + EPS_NORM)
    return centered * scaling * gain_row + bias_row

def product(left_side, right_side):
    return jnp.dot(left_side, right_side, precision=PRECISE, preferred_element_type=jnp.float32)

def group_layer(weights, source, lengths):
    attend_in, attend_out, expand, contract, gains = weights
    vectors = low(gains)
    places = jnp.arange(GROUP, dtype=jnp.int32)
    clip_ids = clip_index(lengths, places)
    cosines, sine_values = rotary_table(clip_offsets(lengths, places))
    normed_one = low(layer_norm(source, vectors[0], vectors[1]))
    joint = low_back(product(normed_one, low(attend_in)))
    query_rows = low(rotate(joint[:, :D].reshape(GROUP, HEADS, HEAD), cosines, sine_values))
    key_rows = low(rotate(joint[:, D:2 * D].reshape(GROUP, HEADS, HEAD), cosines, sine_values))
    value_rows = low(joint[:, 2 * D:].reshape(GROUP, HEADS, HEAD))
    scores = low_back(jnp.einsum('qhd,khd->hqk', query_rows, key_rows, precision=PRECISE) * SCORE_SCALE)
    allowed = (clip_ids[:, None] == clip_ids[None, :]) & (jnp.abs(places[:, None] - places[None, :]) <= WINDOW)
    scores = jnp.where(allowed[None], scores, NEG_FILL)
    row_top = lax.optimization_barrier(jnp.max(scores, axis=-1, keepdims=True))
    exponent = jnp.exp(scores - row_top)
    probability = low(exponent / lax.optimization_barrier(jnp.sum(exponent, axis=-1, keepdims=True)))
    mixed_heads = low(low_back(jnp.einsum('hqk,khd->qhd', probability, value_rows, precision=PRECISE))).reshape(GROUP, D)
    attend_part = low_back(product(mixed_heads, low(attend_out).T))
    hidden = source + vectors[4] * attend_part
    normed_two = low(layer_norm(hidden, vectors[2], vectors[3]))
    gate_up = low_back(product(normed_two, low(expand)))
    inner_act = low(jax.nn.silu(gate_up[:, :FF]) * gate_up[:, FF:])
    branch = low_back(product(inner_act, low(contract).T))
    return hidden + vectors[5] * branch

def adam_step(weight, mean_old, square_old, gradient, factor, step_rate):
    clipped = gradient * factor
    mean_new = BETA_ONE * mean_old + (1.0 - BETA_ONE) * clipped
    square_new = BETA_TWO * square_old + (1.0 - BETA_TWO) * clipped * clipped
    mean_hat = mean_new / (1.0 - BETA_ONE ** STEP)
    square_hat = square_new / (1.0 - BETA_TWO ** STEP)
    moved = weight - step_rate * (mean_hat / (jnp.sqrt(square_hat) + ADAM_EPS) + DECAY * weight)
    return (mean_new, square_new, moved)

def reference(frames, clip_lengths, cotangent, attend_in, attend_out, expand, contract, gains, prior_mean_attend_in, prior_mean_attend_out, prior_mean_expand, prior_mean_contract, prior_mean_gains, prior_square_attend_in, prior_square_attend_out, prior_square_expand, prior_square_contract, prior_square_gains):
    weights = (attend_in, attend_out, expand, contract, gains)
    groups = frames.astype(jnp.float32).reshape(N_DP, GROUP, D)
    pulls = cotangent.astype(jnp.float32).reshape(N_DP, GROUP, D)

    def whole(weight_set, group_set):

        def one_group(item):
            return group_layer(weight_set, item[0], item[1])
        return lax.map(jax.checkpoint(one_group), (group_set, clip_lengths))
    result, backward = jax.vjp(whole, weights, groups)
    grads, frames_grad = backward(pulls)
    square_total = jnp.sum(grads[0] * grads[0])
    for gradient in grads[1:]:
        square_total = square_total + jnp.sum(gradient * gradient)
    grad_norm = jnp.sqrt(square_total)
    factor = CLIP_NORM / jnp.maximum(grad_norm, CLIP_NORM)
    rates = (RATE / math.sqrt(D), RATE / math.sqrt(D // 64), RATE / math.sqrt(D), RATE / math.sqrt(FF), VECTOR_RATE)
    means = (prior_mean_attend_in, prior_mean_attend_out, prior_mean_expand, prior_mean_contract, prior_mean_gains)
    squares = (prior_square_attend_in, prior_square_attend_out, prior_square_expand, prior_square_contract, prior_square_gains)
    news = []
    for weight, mean_old, square_old, gradient, step_rate in zip(weights, means, squares, grads, rates):
        mean_new, square_new, moved = adam_step(weight, mean_old, square_old, gradient, factor, step_rate)
        news.append((mean_new, square_new, moved, moved.astype(jnp.bfloat16)))
    out_frames = result.reshape(FRAMES, D).astype(jnp.bfloat16)
    return (out_frames, frames_grad.reshape(FRAMES, D), grad_norm, news[0][0], news[0][1], news[0][2], news[0][3], news[1][0], news[1][1], news[1][2], news[1][3], news[2][0], news[2][1], news[2][2], news[2][3], news[3][0], news[3][1], news[3][2], news[3][3], news[4][0], news[4][1], news[4][2], news[4][3])
```

```python
import math

import jax
import jax.numpy as jnp
import numpy as np
from jax import lax
from jax.sharding import Mesh
from jax.sharding import PartitionSpec as P

D = 1024
HEADS = 16
HEAD = 64
FF = 4096
WINDOW = 128
STEP = 10

EPS_NORM = 1e-05
NEG_FILL = -1e30
SCORE_SCALE = 0.125
BETA_ONE = 0.9
BETA_TWO = 0.999
ADAM_EPS = 1e-08
DECAY = 0.1
RATE = 3.0
VECTOR_RATE = 0.6
CLIP_NORM = 1.0

TEAM = 4
CORES = 2
SLOTS = TEAM * CORES
ALL = ("rep", "team", "tm")
MEMBERS = ("team", "tm")
HEADS_DEV = HEADS // SLOTS
WIDTH_DEV = HEADS_DEV * HEAD
FF_DEV = FF // SLOTS


def swap_pairs(count, bit):
    return [(a, a ^ bit) for a in range(count)]


def other_core(x):
    return lax.ppermute(x, "tm", swap_pairs(CORES, 1))


def to_mate(x, bit):
    return lax.ppermute(x, "team", swap_pairs(TEAM, bit))


def gather_team(x):
    blocks = [x] + [to_mate(x, k) for k in range(1, TEAM)]
    parts = []
    for block in blocks:
        parts += [block, other_core(block)]
    return jnp.stack(parts)


def scatter_team(x):
    mine = x[:, 0] + other_core(x[:, 1].astype(jnp.bfloat16)).astype(jnp.float32)
    total = mine[0]
    low = mine[1:].astype(jnp.bfloat16)
    for k in range(1, TEAM):
        total = total + to_mate(low[k - 1], k).astype(jnp.float32)
    return total


def exchange_team(x):
    parts = []
    for k in range(TEAM):
        for j in range(CORES):
            block = x[k * CORES + j]
            if k == 0 and j == 1:
                block = other_core(block)
            elif k > 0:
                pairs = [(a, ((a // CORES) ^ k) * CORES + ((a % CORES) ^ j)) for a in range(SLOTS)]
                block = lax.ppermute(block, MEMBERS, pairs)
            parts.append(block)
    return jnp.stack(parts)


def gather_reps(x):
    count = lax.axis_size("rep")
    if count > 4:
        return lax.all_gather(x, "rep", axis=0, tiled=False)
    place = lax.axis_index("rep")
    out = jnp.zeros((count,) + x.shape, x.dtype)
    out = lax.dynamic_update_slice_in_dim(out, x[None], place, 0)
    for k in range(1, count):
        got = lax.ppermute(x, "rep", swap_pairs(count, k))
        out = lax.dynamic_update_slice_in_dim(out, got[None], place ^ k, 0)
    return out


def scatter_reps(x):
    count = lax.axis_size("rep")
    if count > 4:
        return lax.psum_scatter(x.astype(jnp.bfloat16), "rep", scatter_dimension=0, tiled=False).astype(
            jnp.float32
        )
    place = lax.axis_index("rep")
    total = lax.dynamic_index_in_dim(x, place, 0, keepdims=False)
    for k in range(1, count):
        block = lax.dynamic_index_in_dim(x, place ^ k, 0, keepdims=False).astype(jnp.bfloat16)
        total = total + lax.ppermute(block, "rep", swap_pairs(count, k)).astype(jnp.float32)
    return total


def spread_all(block):
    count = lax.axis_size("rep") * SLOTS
    whole = jnp.broadcast_to(block[None], (count,) + block.shape)
    return lax.all_to_all(whole, ALL, 0, 0, tiled=True)


def norm_parts(values):
    centered = values - jnp.mean(values, axis=-1, keepdims=True)
    scaling = lax.rsqrt(jnp.mean(centered * centered, axis=-1, keepdims=True) + EPS_NORM)
    return (centered * scaling, scaling)


def norm_back(gradient, unit_rows, scaling, gain_row):
    scaled = gradient * gain_row
    return scaling * (
        scaled
        - jnp.mean(scaled, axis=-1, keepdims=True)
        - unit_rows * jnp.mean(scaled * unit_rows, axis=-1, keepdims=True)
    )


def dot_rows(left_side, right_side):
    return lax.dot_general(
        left_side, right_side, (((0,), (0,)), ((), ())), preferred_element_type=jnp.float32
    )


def dot_last(left_side, right_side):
    return lax.dot_general(
        left_side, right_side, (((1,), (1,)), ((), ())), preferred_element_type=jnp.float32
    )


def dot(left_side, right_side):
    return jnp.dot(left_side, right_side, preferred_element_type=jnp.float32)


def rotate(values, cosines, sines):
    first = values[..., : HEAD // 2]
    second = values[..., HEAD // 2 :]
    return jnp.concatenate(
        [first * cosines - second * sines, first * sines + second * cosines], axis=-1
    )


def unrotate(values, cosines, sines):
    first = values[..., : HEAD // 2]
    second = values[..., HEAD // 2 :]
    return jnp.concatenate(
        [first * cosines + second * sines, second * cosines - first * sines], axis=-1
    )


def adam_step(weight, mean_old, square_old, gradient, factor, step_rate):
    clipped = gradient * factor
    mean_new = BETA_ONE * mean_old + (1.0 - BETA_ONE) * clipped
    square_new = BETA_TWO * square_old + (1.0 - BETA_TWO) * clipped * clipped
    mean_hat = mean_new / (1.0 - BETA_ONE**STEP)
    square_hat = square_new / (1.0 - BETA_TWO**STEP)
    moved = weight - step_rate * (mean_hat / (jnp.sqrt(square_hat) + ADAM_EPS) + DECAY * weight)
    return (mean_new, square_new, moved)


def per_device(
    frames,
    clip_lengths,
    cotangent,
    attend_in,
    attend_out,
    expand,
    contract,
    gains,
    prior_mean_attend_in,
    prior_mean_attend_out,
    prior_mean_expand,
    prior_mean_contract,
    prior_mean_gains,
    prior_square_attend_in,
    prior_square_attend_out,
    prior_square_expand,
    prior_square_contract,
    prior_square_gains,
):
    bf16 = jnp.bfloat16
    f32 = jnp.float32
    tokens = frames.shape[0]
    group = tokens * CORES
    rows = attend_in.shape[0]
    gain_width = gains.shape[1]
    reps = lax.axis_size("rep")
    devices = reps * SLOTS
    rep = lax.axis_index("rep")
    team = lax.axis_index("team")
    core = lax.axis_index("tm")

    small = jnp.zeros((8, 128), f32)
    small = small.at[:6, :gain_width].set(gains)
    small = small.at[6, :3].set(clip_lengths[0].astype(f32))
    spread = spread_all(small)
    vectors = spread[:, :6, :gain_width].transpose(1, 0, 2).reshape(6, D)
    vectors = lax.reduce_precision(vectors, 8, 7)
    lengths_team = lax.dynamic_index_in_dim(
        spread[:, 6, :3].reshape(reps, TEAM, CORES, 3)[:, :, 0], rep, 0, keepdims=False
    ).astype(jnp.int32)
    slot_lengths = jnp.take(lengths_team, team ^ jnp.arange(TEAM), axis=0)

    frames_team = gather_team(frames)

    attend_pack = jnp.concatenate(
        [
            attend_in.astype(bf16).reshape(rows, 3, SLOTS, WIDTH_DEV).transpose(2, 0, 1, 3).reshape(
                SLOTS, rows, 3 * WIDTH_DEV
            ),
            attend_out.astype(bf16).reshape(rows, SLOTS, WIDTH_DEV).transpose(1, 0, 2),
        ],
        axis=2,
    )
    attend_cols = gather_reps(lax.all_to_all(attend_pack, MEMBERS, 0, 0, tiled=True)).reshape(
        D, 4 * WIDTH_DEV
    )
    part_in = attend_cols[:, : 3 * WIDTH_DEV]
    part_out = attend_cols[:, 3 * WIDTH_DEV :]
    full_out = gather_team(part_out).transpose(1, 0, 2).reshape(D, D)

    mlp_pack = jnp.concatenate(
        [
            expand.astype(bf16).reshape(rows, 2, SLOTS, FF_DEV).transpose(2, 0, 1, 3).reshape(
                SLOTS, rows, 2 * FF_DEV
            ),
            contract.astype(bf16).reshape(rows, SLOTS, FF_DEV).transpose(1, 0, 2),
        ],
        axis=2,
    )
    mlp_cols = gather_reps(lax.all_to_all(mlp_pack, MEMBERS, 0, 0, tiled=True)).reshape(
        D, 3 * FF_DEV
    )
    part_expand = mlp_cols[:, : 2 * FF_DEV]
    part_contract = mlp_cols[:, 2 * FF_DEV :]
    cotangent_team = gather_team(cotangent)

    wide = frames_team.reshape(SLOTS * tokens, D).astype(f32)
    unit_wide, _ = norm_parts(wide)
    normed_one = (unit_wide * vectors[0] + vectors[1]).astype(bf16)
    joint = dot(normed_one, part_in).reshape(TEAM, group, 3, HEADS_DEV, HEAD)
    index = jnp.arange(group, dtype=jnp.int32)
    places = jnp.where(index < tokens, core, 1 - core) * tokens + index % tokens
    ends = jnp.cumsum(slot_lengths, axis=1)
    starts = ends - slot_lengths
    clip_ids = jnp.sum((places[None, :, None] >= ends[:, None, :]).astype(jnp.int32), axis=2)
    begin = jnp.max(
        jnp.where(starts[:, None, :] <= places[None, :, None], starts[:, None, :], 0), axis=2
    )
    offsets = (places[None] - begin).astype(f32)
    freqs = jnp.asarray(np.power(10000.0, -2.0 * np.arange(HEAD // 2) / HEAD), dtype=f32)
    angles = offsets[:, :, None] * freqs
    cosines = jnp.cos(angles)[:, :, None, :]
    sines = jnp.sin(angles)[:, :, None, :]
    query = rotate(joint[:, :, 0], cosines, sines).astype(bf16)
    key = rotate(joint[:, :, 1], cosines, sines).astype(bf16)
    value = joint[:, :, 2].astype(bf16)
    allowed = (clip_ids[:, :, None] == clip_ids[:, None, :]) & (
        jnp.abs(places[:, None] - places[None, :]) <= WINDOW
    )[None]
    scores = jnp.einsum("gqhd,gkhd->ghqk", query, key, preferred_element_type=f32) * SCORE_SCALE
    scores = jnp.where(allowed[:, None], scores, NEG_FILL)
    exponent = jnp.exp(scores - jnp.max(scores, axis=-1, keepdims=True))
    probability = exponent / jnp.sum(exponent, axis=-1, keepdims=True)
    probability_low = probability.astype(bf16)
    mixed = jnp.einsum("ghqk,gkhd->gqhd", probability_low, value, preferred_element_type=f32)
    mixed = mixed.astype(bf16).reshape(SLOTS, tokens, WIDTH_DEV)
    mixed_own = exchange_team(mixed).transpose(1, 0, 2).reshape(tokens, D)

    source = frames.astype(f32)
    attend_part = dot_last(mixed_own, full_out)
    hidden = source + vectors[4] * attend_part
    unit_two, scaling_two = norm_parts(hidden)
    normed_two = (unit_two * vectors[2] + vectors[3]).astype(bf16)

    normed_wide = gather_team(normed_two).reshape(SLOTS * tokens, D)
    grad_branch = (cotangent_team.astype(f32) * vectors[5]).astype(bf16).reshape(SLOTS * tokens, D)
    gate_up = dot(normed_wide, part_expand)
    gate_part = gate_up[:, :FF_DEV]
    up_part = gate_up[:, FF_DEV:]
    sigmoid_gate = jax.nn.sigmoid(gate_part)
    silu_gate = gate_part * sigmoid_gate
    inner_act = (silu_gate * up_part).astype(bf16)
    grad_inner = dot(grad_branch, part_contract)
    grad_gate = grad_inner * up_part * sigmoid_gate * (1.0 + gate_part * (1.0 - sigmoid_gate))
    grad_up = grad_inner * silu_gate
    grad_gate_up = jnp.concatenate([grad_gate, grad_up], axis=1).astype(bf16)
    back_partial = dot_last(grad_gate_up, part_expand).reshape(TEAM, CORES, tokens, D)
    grad_normed_two = scatter_team(back_partial)
    branch_partial = dot_last(inner_act, part_contract).reshape(TEAM, CORES, tokens, D)
    branch = scatter_team(branch_partial)
    term_mlp = jnp.concatenate(
        [dot_rows(normed_wide, grad_gate_up), dot_rows(grad_branch, inner_act)], axis=1
    )
    mlp_sum = scatter_reps(term_mlp.reshape(reps, SLOTS * rows, 3 * FF_DEV))

    pull = cotangent.astype(f32)
    out_frames = (hidden + vectors[5] * branch).astype(bf16)
    grad_hidden = pull + norm_back(grad_normed_two, unit_two, scaling_two, vectors[2])
    grad_attend = (grad_hidden * vectors[4]).astype(bf16)
    grad_mixed_own = dot(grad_attend, full_out).astype(bf16)
    grad_mixed = exchange_team(grad_mixed_own.reshape(tokens, SLOTS, WIDTH_DEV).transpose(1, 0, 2))
    term_out = dot_rows(grad_attend, mixed_own)
    out_partial = term_out.reshape(D, TEAM, CORES, WIDTH_DEV).transpose(1, 2, 0, 3)
    out_sum = scatter_reps(scatter_team(out_partial).reshape(reps, SLOTS * rows, WIDTH_DEV))

    grad_mixed = grad_mixed.reshape(TEAM, group, HEADS_DEV, HEAD)
    grad_probability = jnp.einsum("gqhd,gkhd->ghqk", grad_mixed, value, preferred_element_type=f32)
    row_delta = jnp.sum(probability * grad_probability, axis=-1, keepdims=True)
    grad_scores = (probability * (grad_probability - row_delta)).astype(bf16)
    grad_query = (
        jnp.einsum("ghqk,gkhd->gqhd", grad_scores, key, preferred_element_type=f32) * SCORE_SCALE
    )
    grad_key = (
        jnp.einsum("ghqk,gqhd->gkhd", grad_scores, query, preferred_element_type=f32) * SCORE_SCALE
    )
    grad_value = jnp.einsum(
        "ghqk,gqhd->gkhd", probability_low, grad_mixed, preferred_element_type=f32
    )
    grad_joint = (
        jnp.stack(
            [unrotate(grad_query, cosines, sines), unrotate(grad_key, cosines, sines), grad_value],
            axis=2,
        )
        .astype(bf16)
        .reshape(SLOTS * tokens, 3 * WIDTH_DEV)
    )
    term_in = dot_rows(normed_one, grad_joint)
    back_wide = dot_last(grad_joint, part_in)
    term_gains = jnp.stack(
        [
            jnp.sum(back_wide * unit_wide, axis=0),
            jnp.sum(back_wide, axis=0),
            jnp.sum(grad_normed_two * unit_two, axis=0),
            jnp.sum(grad_normed_two, axis=0),
            jnp.sum(grad_hidden * attend_part, axis=0),
            jnp.sum(pull * branch, axis=0),
        ]
    )
    gains_block = jnp.zeros((devices, 8, 128), f32)
    gains_block = gains_block.at[:, :6, :gain_width].set(
        term_gains.reshape(6, devices, gain_width).transpose(1, 0, 2)
    )
    owned_gains = jnp.sum(lax.all_to_all(gains_block, ALL, 0, 0, tiled=True), axis=0)[
        :6, :gain_width
    ]
    in_blocks = lax.all_to_all(
        term_in.astype(bf16).reshape(devices, rows, 3 * WIDTH_DEV), ALL, 0, 0, tiled=True
    )
    in_sum = jnp.sum(in_blocks.reshape(reps, SLOTS, rows, 3, WIDTH_DEV).astype(f32), axis=0)
    owned_in = in_sum.transpose(1, 2, 0, 3).reshape(rows, 3 * D)

    late = lax.all_to_all(
        jnp.concatenate([mlp_sum, out_sum], axis=1).astype(bf16).reshape(SLOTS, rows, -1),
        MEMBERS,
        0,
        0,
        tiled=True,
    ).astype(f32)
    owned_expand = (
        late[:, :, : 2 * FF_DEV].reshape(SLOTS, rows, 2, FF_DEV).transpose(1, 2, 0, 3)
    ).reshape(rows, 2 * FF)
    owned_contract = late[:, :, 2 * FF_DEV : 3 * FF_DEV].transpose(1, 0, 2).reshape(rows, FF)
    owned_out = late[:, :, 3 * FF_DEV :].transpose(1, 0, 2).reshape(rows, D)

    unit_one, scaling_one = norm_parts(source)
    grad_normed_one = scatter_team(back_wide.reshape(TEAM, CORES, tokens, D))
    frames_grad = grad_hidden + norm_back(grad_normed_one, unit_one, scaling_one, vectors[0])

    square_part = jnp.zeros((), f32)
    for owned in (owned_in, owned_out, owned_expand, owned_contract, owned_gains):
        square_part = square_part + jnp.sum(owned * owned)
    square_total = jnp.sum(spread_all(jnp.full((8, 128), square_part))[:, 0, 0])
    grad_norm = jnp.sqrt(square_total)
    factor = CLIP_NORM / jnp.maximum(grad_norm, CLIP_NORM)
    weights = (attend_in, attend_out, expand, contract, gains)
    grads = (owned_in, owned_out, owned_expand, owned_contract, owned_gains)
    means = (
        prior_mean_attend_in,
        prior_mean_attend_out,
        prior_mean_expand,
        prior_mean_contract,
        prior_mean_gains,
    )
    squares = (
        prior_square_attend_in,
        prior_square_attend_out,
        prior_square_expand,
        prior_square_contract,
        prior_square_gains,
    )
    rates = (
        RATE / math.sqrt(D),
        RATE / math.sqrt(D // 64),
        RATE / math.sqrt(D),
        RATE / math.sqrt(FF),
        VECTOR_RATE,
    )
    news = []
    for weight, mean_old, square_old, gradient, step_rate in zip(
        weights, means, squares, grads, rates
    ):
        mean_new, square_new, moved = adam_step(
            weight, mean_old, square_old, gradient, factor, step_rate
        )
        news += [mean_new, square_new, moved, moved.astype(bf16)]
    return (out_frames, frames_grad, grad_norm, *news)


def solution(mesh):
    teams = Mesh(
        mesh.devices.reshape(mesh.shape["dp"] // TEAM, TEAM, mesh.shape["tm"]), ALL
    )
    by_row = P(ALL, None)
    by_column = P(None, ALL)
    per_group = P(("rep", "team"), None)
    weights = (by_row, by_row, by_row, by_row, by_column)
    return jax.shard_map(
        per_device,
        mesh=teams,
        in_specs=(by_row, per_group, by_row) + weights * 3,
        out_specs=(by_row, by_row, P()) + (by_row,) * 16 + (by_column,) * 4,
        check_vma=False,
    )
```

```python
import math

import jax
import jax.numpy as jnp
import numpy as np
from jax import lax
from jax.experimental import pallas as pl
from jax.experimental.pallas import tpu as pltpu
from jax.sharding import Mesh
from jax.sharding import PartitionSpec as P

D = 1024
HEADS = 16
HEAD = 64
FF = 4096
WINDOW = 128
STEP = 10

EPS_NORM = 1e-05
NEG_FILL = -1e30
SCORE_SCALE = 0.125
BETA_ONE = 0.9
BETA_TWO = 0.999
ADAM_EPS = 1e-08
DECAY = 0.1
RATE = 3.0
VECTOR_RATE = 0.6
CLIP_NORM = 1.0

TEAM = 4
CORES = 2
SLOTS = TEAM * CORES
ALL = ("rep", "team", "tm")
MEMBERS = ("team", "tm")
ANY_SPEC = pl.BlockSpec(memory_space=pl.ANY)
SMEM_SPEC = pl.BlockSpec(memory_space=pltpu.SMEM)
VMEM_SPEC = pl.BlockSpec(memory_space=pltpu.VMEM)
MIB = 1 << 20
HEADS_DEV = HEADS // SLOTS
WIDTH_DEV = HEADS_DEV * HEAD
FF_DEV = FF // SLOTS


def swap_pairs(count, bit):
    return [(a, a ^ bit) for a in range(count)]


def other_core(x):
    return lax.ppermute(x, "tm", swap_pairs(CORES, 1))


def to_mate(x, bit):
    return lax.ppermute(x, "team", swap_pairs(TEAM, bit))


def gather_team(x):
    blocks = [x] + [to_mate(x, k) for k in range(1, TEAM)]
    parts = []
    for block in blocks:
        parts += [block, other_core(block)]
    return parts


def split_mates(sends):
    own, mates = other_core(sends[0]), other_core(sends[1])
    return [own] + [mates[k] for k in range(TEAM - 1)]


def scatter_team(keep, got):
    pieces = [keep[0], got[0]]
    for k in range(1, TEAM):
        chip = (keep[k] + got[k].astype(jnp.float32)).astype(jnp.bfloat16)
        pieces.append(to_mate(chip, k))
    return pieces


def exchange_team(x):
    return lax.all_to_all(x, MEMBERS, 0, 0, tiled=True)


def rep_blocks(x):
    count = lax.axis_size("rep")
    if count > 4:
        return [lax.all_gather(x, "rep", axis=0, tiled=True)]
    return [x] + [lax.ppermute(x, "rep", swap_pairs(count, k)) for k in range(1, count)]


def spread_all(block):
    count = lax.axis_size("rep") * SLOTS
    whole = jnp.broadcast_to(block[None], (count,) + block.shape)
    return lax.all_to_all(whole, ALL, 0, 0, tiled=True)


def norm_parts(values):
    centered = values - jnp.mean(values, axis=-1, keepdims=True)
    scaling = lax.rsqrt(jnp.mean(centered * centered, axis=-1, keepdims=True) + EPS_NORM)
    return (centered * scaling, scaling)


def norm_back(gradient, unit_rows, scaling, gain_row):
    scaled = gradient * gain_row
    return scaling * (
        scaled
        - jnp.mean(scaled, axis=-1, keepdims=True)
        - unit_rows * jnp.mean(scaled * unit_rows, axis=-1, keepdims=True)
    )


def dot_rows(left_side, right_side):
    return lax.dot_general(
        left_side, right_side, (((0,), (0,)), ((), ())), preferred_element_type=jnp.float32
    )


def dot_last(left_side, right_side):
    return lax.dot_general(
        left_side, right_side, (((1,), (1,)), ((), ())), preferred_element_type=jnp.float32
    )


def dot(left_side, right_side):
    return jnp.dot(left_side, right_side, preferred_element_type=jnp.float32)


def call_kernel(kernel, ins, outs, scratch=(), specs=None, vmem=32, name=None):
    return pl.pallas_call(
        kernel,
        out_shape=[jax.ShapeDtypeStruct(shape, dtype) for shape, dtype in outs],
        in_specs=specs or [VMEM_SPEC] * len(ins),
        out_specs=[VMEM_SPEC] * len(outs),
        scratch_shapes=list(scratch),
        compiler_params=pltpu.CompilerParams(vmem_limit_bytes=vmem * MIB),
        name=name,
    )(*ins)


def row_chunks(count, size, body):
    def step(i, carry):
        body(pl.ds(pl.multiple_of(i * size, size), size))
        return carry

    lax.fori_loop(0, count // size, step, 0)


def half_swap(x):
    width = x.shape[-1]
    lane = lax.broadcasted_iota(jnp.int32, x.shape, x.ndim - 1)
    half = HEAD // 2
    return jnp.where(
        lane % HEAD < half,
        pltpu.roll(x, width - half, x.ndim - 1),
        pltpu.roll(x, half, x.ndim - 1),
    )


def key_span(block, group):
    return max(0, (block - 1) * WINDOW), min(group, (block + 2) * WINDOW)


def span_mask(info, slot, block, group):
    low, high = key_span(block, group)
    first = info[3 * slot]
    second = first + info[3 * slot + 1]
    third = second + info[3 * slot + 2]
    place = block * WINDOW + lax.broadcasted_iota(jnp.int32, (WINDOW, 1), 0)
    start = jnp.where(
        place >= third,
        third,
        jnp.where(place >= second, second, jnp.where(place >= first, first, 0)),
    )
    end = jnp.where(
        place < first, first, jnp.where(place < second, second, jnp.where(place < third, third, group))
    )
    least = jnp.maximum(start, place - WINDOW)
    most = jnp.minimum(end, place + WINDOW + 1)
    key_place = low + lax.broadcasted_iota(jnp.int32, (1, high - low), 1)
    return (key_place >= least) & (key_place < most)


def head_lanes(x, head):
    lane = lax.broadcasted_iota(jnp.int32, x.shape, 1)
    return jnp.where(lane // HEAD == head, x, jnp.zeros_like(x))


def pick_heads(parts):
    lane = lax.broadcasted_iota(jnp.int32, parts[0].shape, 1)
    out = parts[0]
    for head in range(1, len(parts)):
        out = jnp.where(lane // HEAD >= head, parts[head], out)
    return out


def block_probability(query, keys, allowed):
    scores = jnp.where(allowed, dot_last(query, keys) * SCORE_SCALE, NEG_FILL)
    exponent = jnp.exp(scores - jnp.max(scores, axis=-1, keepdims=True))
    return exponent * (1.0 / jnp.sum(exponent, axis=-1, keepdims=True))


def attend_forward(info, *refs):
    frames = refs[:SLOTS]
    vec, cosines, sines = refs[SLOTS : SLOTS + 3]
    blocks = refs[SLOTS + 3 : -5]
    normed, rows_out, win, mixed_out, mixed = refs[-5:]
    tokens = frames[0].shape[0]
    group = CORES * tokens
    core, team, rep = info[3 * TEAM], info[3 * TEAM + 1], info[3 * TEAM + 2]
    width = WIDTH_DEV
    size = blocks[0].shape[0]
    for k, block in enumerate(blocks):
        begin = (rep ^ k) * size if len(blocks) > 1 else 0
        win[pl.ds(pl.multiple_of(begin, size), size), :] = block[...]

    def place_of(j):
        return pl.ds(pl.multiple_of((core ^ j) * tokens, tokens), tokens)

    for k in range(TEAM):
        for j in range(CORES):
            s = k * CORES + j

            def norm_rows(chunk, s=s):
                unit, _ = norm_parts(frames[s][chunk, :].astype(jnp.float32))
                normed[s, chunk, :] = (unit * vec[0:1, :] + vec[1:2, :]).astype(jnp.bfloat16)

            row_chunks(tokens, 32, norm_rows)
            joint = dot(normed[s], win[...])
            cos_rows = cosines[k, place_of(j), :]
            sin_rows = sines[k, place_of(j), :]
            for part in range(2):
                x = joint[:, part * width : (part + 1) * width]
                rows_out[k, place_of(j), part * width : (part + 1) * width] = (
                    x * cos_rows + half_swap(x) * sin_rows
                ).astype(jnp.bfloat16)
            rows_out[k, place_of(j), 2 * width :] = joint[:, 2 * width :].astype(jnp.bfloat16)

    def one_group(k, carry):
        for block in range(group // WINDOW):
            low, high = key_span(block, group)
            allowed = span_mask(info, k, block, group)
            query = rows_out[k, block * WINDOW : (block + 1) * WINDOW, :width]
            keys = rows_out[k, low:high, width : 2 * width]
            values = rows_out[k, low:high, 2 * width :]
            outs = []
            for head in range(HEADS_DEV):
                probability = block_probability(head_lanes(query, head), keys, allowed)
                outs.append(dot(probability.astype(jnp.bfloat16), values))
            mixed[k, block * WINDOW : (block + 1) * WINDOW, :] = pick_heads(outs).astype(jnp.bfloat16)
        return carry

    lax.fori_loop(0, TEAM, one_group, 0)
    for k in range(TEAM):
        for half in range(CORES):
            mixed_out[(team ^ k) * CORES + half] = mixed[k, half * tokens : (half + 1) * tokens, :]


def attend_finish(mixed, weight, frames, vec, part_out, normed, mixed_out):
    for p in range(SLOTS):
        mixed_out[:, p * WIDTH_DEV : (p + 1) * WIDTH_DEV] = mixed[p]
    part_out[...] = dot_last(mixed_out[...], weight[...])

    def rows(chunk):
        hidden = frames[chunk, :].astype(jnp.float32) + vec[4:5, :] * part_out[chunk, :]
        unit, _ = norm_parts(hidden)
        normed[chunk, :] = (unit * vec[2:3, :] + vec[3:4, :]).astype(jnp.bfloat16)

    row_chunks(frames.shape[0], 32, rows)


def feed_forward(n0, n1, c0, c1, vec, weight, inner, grads, pulls, keep, send):
    tokens = n0.shape[0]
    half = FF_DEV // 2
    for j, (normed, cot) in enumerate(((n0, c0), (n1, c1))):
        rows = slice(j * tokens, (j + 1) * tokens)
        pulls[rows, :] = (cot[...].astype(jnp.float32) * vec[5:6, :]).astype(jnp.bfloat16)
        for f in range(2):
            gate_cols = slice(f * half, (f + 1) * half)
            up_cols = slice(FF_DEV + f * half, FF_DEV + (f + 1) * half)
            out_cols = slice(2 * FF_DEV + f * half, 2 * FF_DEV + (f + 1) * half)
            gate = dot(normed[...], weight[:, gate_cols])
            up = dot(normed[...], weight[:, up_cols])
            grad_inner = dot(pulls[rows, :], weight[:, out_cols])
            sigmoid = jax.nn.sigmoid(gate)
            silu = gate * sigmoid
            inner[rows, gate_cols] = (silu * up).astype(jnp.bfloat16)
            grads[rows, gate_cols] = (
                grad_inner * up * sigmoid * (1.0 + gate * (1.0 - sigmoid))
            ).astype(jnp.bfloat16)
            grads[rows, up_cols] = (grad_inner * silu).astype(jnp.bfloat16)
        back = dot_last(grads[rows, :], weight[:, : 2 * FF_DEV])
        if j == 0:
            keep[...] = back
        else:
            send[...] = back.astype(jnp.bfloat16)


def feed_branch(i0, i1, i2, i3, weight, k0, k1, k2, k3, send, send_mates):
    tokens = k0.shape[0]
    for k, (inner, keep) in enumerate(((i0, k0), (i1, k1), (i2, k2), (i3, k3))):
        keep[...] = dot_last(inner[:tokens, :], weight[:, 2 * FF_DEV :])
        part = dot_last(inner[tokens:, :], weight[:, 2 * FF_DEV :]).astype(jnp.bfloat16)
        if k == 0:
            send[...] = part
        else:
            send_mates[k - 1] = part


def feed_terms(*refs):
    normed, grads = refs[:SLOTS], refs[SLOTS : SLOTS + TEAM]
    pulls, inner = refs[SLOTS + TEAM : SLOTS + 2 * TEAM], refs[SLOTS + 2 * TEAM : SLOTS + 3 * TEAM]
    out = refs[-1]
    step = 256
    for r in range(D // step):
        rows = slice(r * step, (r + 1) * step)
        left = jnp.concatenate([ref[:, rows] for ref in normed], axis=0)
        right = jnp.concatenate([ref[...] for ref in grads], axis=0)
        out[rows, : 2 * FF_DEV] = dot_rows(left, right).astype(jnp.bfloat16)
        left = jnp.concatenate([ref[:, rows] for ref in pulls], axis=0)
        right = jnp.concatenate([ref[...] for ref in inner], axis=0)
        out[rows, 2 * FF_DEV :] = dot_rows(left, right).astype(jnp.bfloat16)


def attend_back_start(*refs):
    pieces = refs[: TEAM + 1]
    part_out, frames, cotangent, vec, weight, mixed = refs[TEAM + 1 : TEAM + 7]
    grad_hidden, sums = refs[TEAM + 7 : TEAM + 9]
    grad_mixed, term, grad_attend = refs[TEAM + 9 :]
    sums[...] = jnp.zeros_like(sums)

    def rows(chunk):
        grad_normed = pieces[0][chunk, :]
        for piece in pieces[1:]:
            grad_normed = grad_normed + piece[chunk, :].astype(jnp.float32)
        attended = part_out[chunk, :]
        unit, scaling = norm_parts(frames[chunk, :].astype(jnp.float32) + vec[4:5, :] * attended)
        grad = cotangent[chunk, :].astype(jnp.float32) + norm_back(
            grad_normed, unit, scaling, vec[2:3, :]
        )
        grad_hidden[chunk, :] = grad
        grad_attend[chunk, :] = (grad * vec[4:5, :]).astype(jnp.bfloat16)
        sums[0:1, :] += jnp.sum(grad_normed * unit, axis=0, keepdims=True)
        sums[1:2, :] += jnp.sum(grad_normed, axis=0, keepdims=True)
        sums[2:3, :] += jnp.sum(grad * attended, axis=0, keepdims=True)

    row_chunks(frames.shape[0], 32, rows)
    grads = dot(grad_attend[...], weight[...]).astype(jnp.bfloat16)
    terms = dot_rows(grad_attend[...], mixed[...]).astype(jnp.bfloat16)
    for p in range(SLOTS):
        grad_mixed[p] = grads[:, p * WIDTH_DEV : (p + 1) * WIDTH_DEV]
        term[p] = terms[:, p * WIDTH_DEV : (p + 1) * WIDTH_DEV]


def attend_backward(info, *refs):
    grad_mixed, frames = refs[0], refs[1 : SLOTS + 1]
    normed, rows_in, win, cosines, sines = refs[SLOTS + 1 : SLOTS + 6]
    term, sums = refs[SLOTS + 6 : SLOTS + 8]
    keep = refs[SLOTS + 8 : SLOTS + 8 + TEAM]
    send, send_mates, mixed, joint, key_total, value_total, back = refs[SLOTS + 8 + TEAM :]
    tokens = frames[0].shape[0]
    group = CORES * tokens
    core, team = info[3 * TEAM], info[3 * TEAM + 1]
    width = WIDTH_DEV
    for k in range(TEAM):
        for j in range(CORES):
            place = pl.ds(pl.multiple_of(j * tokens, tokens), tokens)
            mixed[k, place, :] = grad_mixed[(team ^ k) * CORES + j]

    def one_group(k, carry):
        key_total[...] = jnp.zeros_like(key_total)
        value_total[...] = jnp.zeros_like(value_total)

        def own_rows(half):
            return pl.ds(pl.multiple_of((k * CORES + (core ^ half)) * tokens, tokens), tokens)

        def unrotated(x, half):
            rows = slice(half * tokens, (half + 1) * tokens)
            return (x * cosines[k, rows, :] - half_swap(x) * sines[k, rows, :]).astype(jnp.bfloat16)

        query_parts = []
        for block in range(group // WINDOW):
            low, high = key_span(block, group)
            allowed = span_mask(info, k, block, group)
            rows = slice(block * WINDOW, (block + 1) * WINDOW)
            query = rows_in[k, rows, :width]
            keys = rows_in[k, low:high, width : 2 * width]
            values = rows_in[k, low:high, 2 * width :]
            grad = mixed[k, rows, :]
            outs = []
            for head in range(HEADS_DEV):
                query_head = head_lanes(query, head)
                grad_head = head_lanes(grad, head)
                probability = block_probability(query_head, keys, allowed)
                grad_probability = dot_last(grad_head, values)
                delta = jnp.sum(probability * grad_probability, axis=-1, keepdims=True)
                grad_scores = (probability * (grad_probability - delta)).astype(jnp.bfloat16)
                outs.append(dot(grad_scores, keys))
                key_total[low:high, :] += dot_rows(grad_scores, query_head)
                value_total[low:high, :] += dot_rows(probability.astype(jnp.bfloat16), grad_head)
            query_parts.append(pick_heads(outs) * SCORE_SCALE)
        per_half = tokens // WINDOW
        for half in range(CORES):
            rows = slice(half * tokens, (half + 1) * tokens)
            grad_query = jnp.concatenate(query_parts[half * per_half : (half + 1) * per_half], axis=0)
            joint[own_rows(half), :width] = unrotated(grad_query, half)
            joint[own_rows(half), width : 2 * width] = unrotated(
                key_total[rows, :] * SCORE_SCALE, half
            )
            joint[own_rows(half), 2 * width :] = value_total[rows, :].astype(jnp.bfloat16)
        return carry

    lax.fori_loop(0, TEAM, one_group, 0)
    term[...] = dot_rows(normed[...], joint[...]).astype(jnp.bfloat16)
    sums[...] = jnp.zeros_like(sums)
    for k in range(TEAM):
        for j in range(CORES):
            s = k * CORES + j
            back[...] = dot_last(joint[s * tokens : (s + 1) * tokens, :], win[...])

            def rows(chunk, s=s, k=k, j=j):
                part = back[chunk, :]
                unit, _ = norm_parts(frames[s][chunk, :].astype(jnp.float32))
                sums[0:1, :] += jnp.sum(part * unit, axis=0, keepdims=True)
                sums[1:2, :] += jnp.sum(part, axis=0, keepdims=True)
                if j == 0:
                    keep[k][chunk, :] = part
                elif k == 0:
                    send[chunk, :] = part.astype(jnp.bfloat16)
                else:
                    send_mates[k - 1, chunk, :] = part.astype(jnp.bfloat16)

            row_chunks(tokens, 32, rows)


def frames_back(*refs):
    pieces = refs[: TEAM + 1]
    frames, grad_hidden, vec, out = refs[TEAM + 1 :]

    def rows(chunk):
        grad_normed = pieces[0][chunk, :]
        for piece in pieces[1:]:
            grad_normed = grad_normed + piece[chunk, :].astype(jnp.float32)
        unit, scaling = norm_parts(frames[chunk, :].astype(jnp.float32))
        out[chunk, :] = grad_hidden[chunk, :] + norm_back(grad_normed, unit, scaling, vec[0:1, :])

    row_chunks(frames.shape[0], 32, rows)


def frames_out(*refs):
    pieces = refs[: TEAM + 1]
    frames, part_out, cotangent, vec, out, sums = refs[TEAM + 1 :]
    sums[...] = jnp.zeros_like(sums)

    def rows(chunk):
        branch = pieces[0][chunk, :]
        for piece in pieces[1:]:
            branch = branch + piece[chunk, :].astype(jnp.float32)
        hidden = frames[chunk, :].astype(jnp.float32) + vec[4:5, :] * part_out[chunk, :]
        out[chunk, :] = (hidden + vec[5:6, :] * branch).astype(jnp.bfloat16)
        sums[0:1, :] += jnp.sum(
            cotangent[chunk, :].astype(jnp.float32) * branch, axis=0, keepdims=True
        )

    row_chunks(frames.shape[0], 32, rows)


def adam_step(weight, mean_old, square_old, gradient, factor, step_rate):
    clipped = gradient * factor
    mean_new = BETA_ONE * mean_old + (1.0 - BETA_ONE) * clipped
    square_new = BETA_TWO * square_old + (1.0 - BETA_TWO) * clipped * clipped
    mean_hat = mean_new / (1.0 - BETA_ONE**STEP)
    square_hat = square_new / (1.0 - BETA_TWO**STEP)
    moved = weight - step_rate * (mean_hat / (jnp.sqrt(square_hat) + ADAM_EPS) + DECAY * weight)
    return (mean_new, square_new, moved)


def per_device(
    frames,
    clip_lengths,
    cotangent,
    attend_in,
    attend_out,
    expand,
    contract,
    gains,
    prior_mean_attend_in,
    prior_mean_attend_out,
    prior_mean_expand,
    prior_mean_contract,
    prior_mean_gains,
    prior_square_attend_in,
    prior_square_attend_out,
    prior_square_expand,
    prior_square_contract,
    prior_square_gains,
):
    bf16 = jnp.bfloat16
    f32 = jnp.float32
    tokens = frames.shape[0]
    group = tokens * CORES
    rows = attend_in.shape[0]
    gain_width = gains.shape[1]
    reps = lax.axis_size("rep")
    devices = reps * SLOTS
    rep = lax.axis_index("rep")
    team = lax.axis_index("team")
    core = lax.axis_index("tm")

    small = jnp.zeros((8, 128), f32)
    small = small.at[:6, :gain_width].set(gains)
    small = small.at[6, :3].set(clip_lengths[0].astype(f32))
    spread = spread_all(small)
    vectors = spread[:, :6, :gain_width].transpose(1, 0, 2).reshape(6, D)
    vectors = jnp.pad(lax.reduce_precision(vectors, 8, 7), ((0, 2), (0, 0)))
    lengths_team = lax.dynamic_index_in_dim(
        spread[:, 6, :3].reshape(reps, TEAM, CORES, 3)[:, :, 0], rep, 0, keepdims=False
    ).astype(jnp.int32)
    slot_lengths = jnp.take(lengths_team, team ^ jnp.arange(TEAM), axis=0)
    info = jnp.concatenate([slot_lengths.reshape(-1), jnp.stack([core, team, rep])])

    frames_team = gather_team(frames)

    in_pack = (
        attend_in.astype(bf16)
        .reshape(rows, 3, SLOTS, WIDTH_DEV)
        .transpose(2, 0, 1, 3)
        .reshape(SLOTS, rows, 3 * WIDTH_DEV)
    )
    in_blocks = rep_blocks(exchange_team(in_pack).reshape(SLOTS * rows, 3 * WIDTH_DEV))
    full_out = lax.all_gather(attend_out.astype(bf16), ALL, axis=0, tiled=True)
    mlp_pack = jnp.concatenate(
        [
            expand.astype(bf16).reshape(rows, 2, SLOTS, FF_DEV).transpose(2, 0, 1, 3).reshape(
                SLOTS, rows, 2 * FF_DEV
            ),
            contract.astype(bf16).reshape(rows, SLOTS, FF_DEV).transpose(1, 0, 2),
        ],
        axis=2,
    )
    mlp_weight = lax.all_gather(
        exchange_team(mlp_pack).reshape(SLOTS * rows, 3 * FF_DEV), "rep", axis=0, tiled=True
    )
    cotangent_team = gather_team(cotangent)

    places = jnp.arange(group, dtype=jnp.int32)
    ends = jnp.cumsum(slot_lengths, axis=1)
    starts = ends - slot_lengths
    begin = jnp.max(
        jnp.where(starts[:, None, :] <= places[None, :, None], starts[:, None, :], 0), axis=2
    )
    offsets = (places[None] - begin).astype(f32)
    freqs = np.power(10000.0, -2.0 * np.arange(HEAD // 2) / HEAD)
    lane_freqs = jnp.asarray(np.tile(freqs, WIDTH_DEV // (HEAD // 2)), dtype=f32)
    angles = offsets[:, :, None] * lane_freqs
    signs = jnp.asarray(np.where(np.arange(WIDTH_DEV) % HEAD < HEAD // 2, -1.0, 1.0), dtype=f32)
    cosines = jnp.cos(angles)
    sines = jnp.sin(angles) * signs

    normed_one, attend_rows, part_in, mixed = call_kernel(
        attend_forward,
        [info, *frames_team, vectors, cosines, sines, *in_blocks],
        [
            ((SLOTS, tokens, D), bf16),
            ((TEAM, group, 3 * WIDTH_DEV), bf16),
            ((D, 3 * WIDTH_DEV), bf16),
            ((SLOTS, tokens, WIDTH_DEV), bf16),
        ],
        scratch=[pltpu.VMEM((TEAM, group, WIDTH_DEV), bf16)],
        specs=[SMEM_SPEC] + [VMEM_SPEC] * (SLOTS + 3 + len(in_blocks)),
        name="attend_forward",
    )

    attend_part, normed_two, mixed_flat = call_kernel(
        attend_finish,
        [exchange_team(mixed), full_out, frames, vectors],
        [((tokens, D), f32), ((tokens, D), bf16), ((tokens, D), bf16)],
        name="attend_finish",
    )

    normed_team = gather_team(normed_two)
    inner, grads_up, pulls, keeps, sends = [], [], [], [], []
    for k in range(TEAM):
        pair = slice(k * CORES, (k + 1) * CORES)
        out = call_kernel(
            feed_forward,
            [*normed_team[pair], *cotangent_team[pair], vectors, mlp_weight],
            [
                ((group, FF_DEV), bf16),
                ((group, 2 * FF_DEV), bf16),
                ((group, D), bf16),
                ((tokens, D), f32),
                ((tokens, D), bf16),
            ],
            name="feed_forward",
        )
        for kept, item in zip((inner, grads_up, pulls, keeps, sends), out):
            kept.append(item)
    back_pieces = scatter_team(keeps, [other_core(x) for x in sends])
    (term_mlp,) = call_kernel(
        feed_terms,
        [*normed_team, *grads_up, *pulls, *inner],
        [((D, 3 * FF_DEV), bf16)],
        vmem=40,
        name="feed_terms",
    )
    mlp_sum = lax.psum_scatter(term_mlp, "rep", scatter_dimension=0, tiled=True)
    out = call_kernel(
        feed_branch,
        [*inner, mlp_weight],
        [((tokens, D), f32)] * TEAM + [((tokens, D), bf16), ((TEAM - 1, tokens, D), bf16)],
        name="feed_branch",
    )
    branch_pieces = scatter_team(out[:TEAM], split_mates(out[TEAM:]))

    grad_hidden, sums_two, grad_mixed, term_out = call_kernel(
        attend_back_start,
        [*back_pieces, attend_part, frames, cotangent, vectors, full_out, mixed_flat],
        [
            ((tokens, D), f32),
            ((8, D), f32),
            ((SLOTS, tokens, WIDTH_DEV), bf16),
            ((SLOTS, D, WIDTH_DEV), bf16),
        ],
        scratch=[pltpu.VMEM((tokens, D), bf16)],
        name="attend_back_start",
    )
    grad_mixed = exchange_team(grad_mixed)
    out_sum = jnp.sum(exchange_team(term_out).astype(f32), axis=0).astype(bf16)

    out_frames, sums_out = call_kernel(
        frames_out,
        [*branch_pieces, frames, attend_part, cotangent, vectors],
        [((tokens, D), bf16), ((8, D), f32)],
        name="frames_out",
    )

    out = call_kernel(
        attend_backward,
        [info, grad_mixed, *frames_team, normed_one.reshape(SLOTS * tokens, D), attend_rows]
        + [part_in, cosines, sines],
        [
            ((D, 3 * WIDTH_DEV), bf16),
            ((8, D), f32),
            *[((tokens, D), f32)] * TEAM,
            ((tokens, D), bf16),
            ((TEAM - 1, tokens, D), bf16),
        ],
        scratch=[
            pltpu.VMEM((TEAM, group, WIDTH_DEV), bf16),
            pltpu.VMEM((SLOTS * tokens, 3 * WIDTH_DEV), bf16),
            pltpu.VMEM((group, WIDTH_DEV), f32),
            pltpu.VMEM((group, WIDTH_DEV), f32),
            pltpu.VMEM((tokens, D), f32),
        ],
        specs=[SMEM_SPEC] + [VMEM_SPEC] * (SLOTS + 6),
        vmem=48,
        name="attend_backward",
    )
    term_in, sums_one = out[:2]
    one_pieces = scatter_team(out[2 : 2 + TEAM], split_mates(out[2 + TEAM :]))

    term_gains = jnp.concatenate([sums_one[:2], sums_two[:3], sums_out[:1]])
    gains_block = jnp.zeros((devices, 8, 4 * WIDTH_DEV), bf16)
    gains_block = gains_block.at[:, :6, :gain_width].set(
        term_gains.astype(bf16).reshape(6, devices, gain_width).transpose(1, 0, 2)
    )
    last = lax.all_to_all(
        jnp.concatenate(
            [
                jnp.concatenate([term_in, out_sum], axis=1).reshape(devices, rows, 4 * WIDTH_DEV),
                gains_block,
            ],
            axis=1,
        ),
        ALL,
        0,
        0,
        tiled=True,
    )
    owned_gains = jnp.sum(last[:, rows : rows + 6, :gain_width].astype(f32), axis=0)
    last_sum = jnp.sum(
        last[:, :rows].reshape(reps, SLOTS, rows, 4, WIDTH_DEV).astype(f32), axis=0
    )
    owned_in = last_sum[:, :, :3].transpose(1, 2, 0, 3).reshape(rows, 3 * D)
    owned_out = last_sum[:, :, 3].transpose(1, 0, 2).reshape(rows, D)

    late = exchange_team(mlp_sum.reshape(SLOTS, rows, 3 * FF_DEV)).astype(f32)
    owned_expand = (
        late[:, :, : 2 * FF_DEV].reshape(SLOTS, rows, 2, FF_DEV).transpose(1, 2, 0, 3)
    ).reshape(rows, 2 * FF)
    owned_contract = late[:, :, 2 * FF_DEV :].transpose(1, 0, 2).reshape(rows, FF)

    (frames_grad,) = call_kernel(
        frames_back,
        [*one_pieces, frames, grad_hidden, vectors],
        [((tokens, D), f32)],
        name="frames_back",
    )

    square_part = jnp.zeros((), f32)
    for owned in (owned_in, owned_out, owned_expand, owned_contract, owned_gains):
        square_part = square_part + jnp.sum(owned * owned)
    square_total = jnp.sum(spread_all(jnp.full((8, 128), square_part))[:, 0, 0])
    grad_norm = jnp.sqrt(square_total)
    factor = CLIP_NORM / jnp.maximum(grad_norm, CLIP_NORM)
    weights = (attend_in, attend_out, expand, contract, gains)
    grads = (owned_in, owned_out, owned_expand, owned_contract, owned_gains)
    means = (
        prior_mean_attend_in,
        prior_mean_attend_out,
        prior_mean_expand,
        prior_mean_contract,
        prior_mean_gains,
    )
    squares = (
        prior_square_attend_in,
        prior_square_attend_out,
        prior_square_expand,
        prior_square_contract,
        prior_square_gains,
    )
    rates = (
        RATE / math.sqrt(D),
        RATE / math.sqrt(D // 64),
        RATE / math.sqrt(D),
        RATE / math.sqrt(FF),
        VECTOR_RATE,
    )
    news = []
    for weight, mean_old, square_old, gradient, step_rate in zip(
        weights, means, squares, grads, rates
    ):
        mean_new, square_new, moved = adam_step(
            weight, mean_old, square_old, gradient, factor, step_rate
        )
        news += [mean_new, square_new, moved, moved.astype(bf16)]
    return (out_frames, frames_grad, grad_norm, *news)


def solution(mesh):
    teams = Mesh(
        mesh.devices.reshape(mesh.shape["dp"] // TEAM, TEAM, mesh.shape["tm"]), ALL
    )
    by_row = P(ALL, None)
    by_column = P(None, ALL)
    per_group = P(("rep", "team"), None)
    weights = (by_row, by_row, by_row, by_row, by_column)
    return jax.shard_map(
        per_device,
        mesh=teams,
        in_specs=(by_row, per_group, by_row) + weights * 3,
        out_specs=(by_row, by_row, P()) + (by_row,) * 16 + (by_column,) * 4,
        check_vma=False,
    )
```

```python
import functools
import math

import jax
import jax.numpy as jnp
import numpy as np
from jax import lax
from jax.experimental import pallas as pl
from jax.experimental.pallas import tpu as pltpu
from jax.sharding import Mesh
from jax.sharding import PartitionSpec as P

D = 1024
HEADS = 16
HEAD = 64
FF = 4096
WINDOW = 128
STEP = 10

EPS_NORM = 1e-05
NEG_FILL = -1e30
SCORE_SCALE = 0.125
BETA_ONE = 0.9
BETA_TWO = 0.999
ADAM_EPS = 1e-08
DECAY = 0.1
RATE = 3.0
VECTOR_RATE = 0.6
CLIP_NORM = 1.0

TEAM = 4
CORES = 2
SLOTS = TEAM * CORES
ALL = ("rep", "team", "tm")
MEMBERS = ("team", "tm")
ANY_SPEC = pl.BlockSpec(memory_space=pl.ANY)
SMEM_SPEC = pl.BlockSpec(memory_space=pltpu.SMEM)
VMEM_SPEC = pl.BlockSpec(memory_space=pltpu.VMEM)
MIB = 1 << 20
PLAIN, HBM_OUT = range(2)
HBM_SPEC = pl.BlockSpec(memory_space=pltpu.HBM)
LOG2_E = math.log2(math.e)
HEADS_DEV = HEADS // SLOTS
WIDTH_DEV = HEADS_DEV * HEAD
FF_DEV = FF // SLOTS


def swap_pairs(count, bit):
    return [(a, a ^ bit) for a in range(count)]


def other_core(x):
    return lax.ppermute(x, "tm", swap_pairs(CORES, 1))


def to_mate(x, bit):
    return lax.ppermute(x, "team", swap_pairs(TEAM, bit))


def gather_team(x):
    blocks = [x] + [to_mate(x, k) for k in range(1, TEAM)]
    parts = []
    for block in blocks:
        parts += [block, other_core(block)]
    return parts


def chip_sums(keep, got):
    return [
        (keep[k] + got[k].astype(jnp.float32)).astype(jnp.bfloat16) for k in range(1, TEAM)
    ]


def send_mates(chips):
    return [to_mate(chip, k + 1) for k, chip in enumerate(chips)]


def exchange_team(x):
    return lax.all_to_all(x, MEMBERS, 0, 0, tiled=True)


def after(x, *tokens):
    return pl.pallas_call(
        lambda *refs: None,
        out_shape=jax.ShapeDtypeStruct(x.shape, x.dtype),
        in_specs=[ANY_SPEC] * (1 + len(tokens)),
        out_specs=ANY_SPEC,
        input_output_aliases={0: 0},
        name="after",
    )(x, *tokens)


def norm_parts(values):
    centered = values - jnp.mean(values, axis=-1, keepdims=True)
    scaling = lax.rsqrt(jnp.mean(centered * centered, axis=-1, keepdims=True) + EPS_NORM)
    return (centered * scaling, scaling)


def norm_back(gradient, unit_rows, scaling, gain_row):
    scaled = gradient * gain_row
    return scaling * (
        scaled
        - jnp.mean(scaled, axis=-1, keepdims=True)
        - unit_rows * jnp.mean(scaled * unit_rows, axis=-1, keepdims=True)
    )


def dot_rows(left_side, right_side):
    return lax.dot_general(
        left_side, right_side, (((0,), (0,)), ((), ())), preferred_element_type=jnp.float32
    )


def dot_last(left_side, right_side):
    return lax.dot_general(
        left_side, right_side, (((1,), (1,)), ((), ())), preferred_element_type=jnp.float32
    )


def dot(left_side, right_side):
    return jnp.dot(left_side, right_side, preferred_element_type=jnp.float32)


def adam_step(weight, mean_old, square_old, gradient, factor, step_rate):
    clipped = gradient * factor
    mean_new = BETA_ONE * mean_old + (1.0 - BETA_ONE) * clipped
    square_new = BETA_TWO * square_old + (1.0 - BETA_TWO) * clipped * clipped
    mean_hat = mean_new / (1.0 - BETA_ONE**STEP)
    square_hat = square_new / (1.0 - BETA_TWO**STEP)
    moved = weight - step_rate * (mean_hat / (jnp.sqrt(square_hat) + ADAM_EPS) + DECAY * weight)
    return (mean_new, square_new, moved)


def in_hbm(x):
    return pltpu.with_memory_space_constraint(x, pltpu.HBM)


def cost(micros):
    return pl.CostEstimate(flops=int(micros * 1e9), transcendentals=0, bytes_accessed=int(micros * 1e6))


def call_kernel(
    kernel, ins, outs, scratch=(), specs=None, far=(), vmem=16, name=None, micros=2
):
    specs = list(specs or [VMEM_SPEC] * len(ins))
    ins = list(ins)
    buffers = [pltpu.VMEM(ins[i].shape, ins[i].dtype) for i in far]
    for i in far:
        specs[i] = HBM_SPEC

    def loaded(*refs):
        refs = list(refs)
        if far:
            near, sems = refs[-1 - len(far) : -1], refs[-1]
            refs = refs[: -1 - len(far)]
            copies = [
                pltpu.make_async_copy(refs[i], b, sems.at[n]) for n, (i, b) in enumerate(zip(far, near))
            ]
            for copy in copies:
                copy.start()
            for copy in copies:
                copy.wait()
            for i, b in zip(far, near):
                refs[i] = b
        kernel(*refs)

    return pl.pallas_call(
        loaded,
        out_shape=[
            (pltpu.HBM if mode else jax.ShapeDtypeStruct)(shape, dtype) for shape, dtype, *mode in outs
        ],
        in_specs=specs,
        out_specs=[VMEM_SPEC] * len(outs),
        scratch_shapes=[
            *scratch,
            *buffers,
            *([pltpu.SemaphoreType.DMA((len(far),))] if far else []),
        ],
        compiler_params=pltpu.CompilerParams(vmem_limit_bytes=vmem * MIB),
        cost_estimate=cost(micros),
        name=name,
    )(*ins)


def call_terms(normed, grads, pulls, inner):
    count, tokens, _ = normed.shape
    step = 256
    by_rows = pl.BlockSpec((count, tokens, step), lambda r: (0, 0, r))

    def whole(x):
        return pl.BlockSpec(x.shape, lambda r: (0, 0, 0), pipeline_mode=pl.Buffered(1))

    return pl.pallas_call(
        feed_terms,
        grid=(D // step,),
        in_specs=[by_rows, whole(grads), by_rows, whole(inner)],
        out_specs=[pl.BlockSpec((step, 3 * FF_DEV), lambda r: (r, 0))] * 2,
        out_shape=[
            pltpu.HBM((D, 3 * FF_DEV), jnp.bfloat16),
            jax.ShapeDtypeStruct((D, 3 * FF_DEV), jnp.bfloat16),
        ],
        compiler_params=pltpu.CompilerParams(vmem_limit_bytes=24 * MIB),
        cost_estimate=cost(8),
        name="feed_terms",
    )(in_hbm(normed), in_hbm(grads), in_hbm(pulls), in_hbm(inner))


def call_groups(
    kernel, info, ins, outs, scratch=(), vmem=24, name=None, micros=20, mates=None, steps=TEAM
):
    def spec(shape, block, out):
        rest = (0,) * (len(shape) - 1)
        if block is None:
            return pl.BlockSpec(
                shape, lambda g, info: (0, *rest), pipeline_mode=None if out else pl.Buffered(1)
            )
        if mates and not out:
            return pl.BlockSpec(block, lambda g, info: (info[3 * TEAM + 1] ^ (mates[0] + g), *rest))
        return pl.BlockSpec(block, lambda g, info: (g, *rest))

    return pl.pallas_call(
        functools.partial(kernel, mates[0] if mates else 0),
        grid_spec=pltpu.PrefetchScalarGridSpec(
            num_scalar_prefetch=1,
            grid=(mates[1] if mates else steps,),
            in_specs=[spec(x.shape, block, False) for x, block in ins],
            out_specs=[spec(shape, block, True) for shape, _, block, _ in outs],
            scratch_shapes=list(scratch),
        ),
        out_shape=[
            jax.ShapeDtypeStruct(shape, dtype) if mode == PLAIN else pltpu.HBM(shape, dtype)
            for shape, dtype, _, mode in outs
        ],
        compiler_params=pltpu.CompilerParams(vmem_limit_bytes=vmem * MIB),
        cost_estimate=cost(micros),
        name=name,
    )(info, *[x for x, _ in ins])


def row_chunks(count, size, body):
    def step(i, carry):
        body(pl.ds(pl.multiple_of(i * size, size), size))
        return carry

    lax.fori_loop(0, count // size, step, 0)


def half_swap(x):
    width = x.shape[-1]
    lane = lax.broadcasted_iota(jnp.int32, x.shape, x.ndim - 1)
    half = HEAD // 2
    return jnp.where(
        lane % HEAD < half,
        pltpu.roll(x, width - half, x.ndim - 1),
        pltpu.roll(x, half, x.ndim - 1),
    )


def key_span(block, group):
    return max(0, (block - 1) * WINDOW), min(group, (block + 2) * WINDOW)


def span_mask(info, slot, block, group):
    low, high = key_span(block, group)
    first = info[3 * slot]
    second = first + info[3 * slot + 1]
    third = second + info[3 * slot + 2]
    place = block * WINDOW + lax.broadcasted_iota(jnp.int32, (WINDOW, 1), 0)
    start = jnp.where(
        place >= third,
        third,
        jnp.where(place >= second, second, jnp.where(place >= first, first, 0)),
    )
    end = jnp.where(
        place < first, first, jnp.where(place < second, second, jnp.where(place < third, third, group))
    )
    least = jnp.maximum(start, place - WINDOW)
    most = jnp.minimum(end, place + WINDOW + 1)
    key_place = low + lax.broadcasted_iota(jnp.int32, (1, high - low), 1)
    return (key_place >= least) & (key_place < most)


def head_lanes(x, head):
    lane = lax.broadcasted_iota(jnp.int32, x.shape, 1)
    return jnp.where(lane // HEAD == head, x, jnp.zeros_like(x))


def pick_heads(parts):
    lane = lax.broadcasted_iota(jnp.int32, parts[0].shape, 1)
    out = parts[0]
    for head in range(1, len(parts)):
        out = jnp.where(lane // HEAD >= head, parts[head], out)
    return out


def softmax_rows(products, allowed):
    scores = jnp.where(allowed, products * (SCORE_SCALE * LOG2_E), NEG_FILL)
    exponent = jnp.exp2(scores - jnp.max(scores, axis=-1, keepdims=True))
    return exponent * (1.0 / jnp.sum(exponent, axis=-1, keepdims=True))


def attend_forward(_, info, frames, vec, win, cosines, sines, normed, rows_out, mixed):
    k = pl.program_id(0)
    tokens = frames.shape[1]
    group = CORES * tokens
    width = WIDTH_DEV
    for half in range(CORES):
        rows = slice(half * tokens, (half + 1) * tokens)

        def norm_rows(chunk, half=half):
            unit, _ = norm_parts(frames[half, chunk, :].astype(jnp.float32))
            normed[half, chunk, :] = (unit * vec[0:1, :] + vec[1:2, :]).astype(jnp.bfloat16)

        row_chunks(tokens, 256, norm_rows)
        joint = dot(normed[half], win[...])
        for part in range(2):
            x = joint[:, part * width : (part + 1) * width]
            rows_out[0, rows, part * width : (part + 1) * width] = (
                x * cosines[0, rows, :] + half_swap(x) * sines[0, rows, :]
            ).astype(jnp.bfloat16)
        rows_out[0, rows, 2 * width :] = joint[:, 2 * width :].astype(jnp.bfloat16)

    blocks = range(group // WINDOW)
    tiles = [(block, head) for block in blocks for head in range(HEADS_DEV)]
    masks = [span_mask(info, k, block, group) for block in blocks]

    def product(block, head):
        low, high = key_span(block, group)
        query = head_lanes(rows_out[0, block * WINDOW : (block + 1) * WINDOW, :width], head)
        return dot_last(query, rows_out[0, low:high, width : 2 * width])

    ahead = product(*tiles[0])
    outs = []
    for i, (block, head) in enumerate(tiles):
        now = ahead
        if i + 1 < len(tiles):
            ahead = product(*tiles[i + 1])
        low, high = key_span(block, group)
        probability = softmax_rows(now, masks[block]).astype(jnp.bfloat16)
        outs.append(dot(probability, rows_out[0, low:high, 2 * width :]))
        if head == HEADS_DEV - 1:
            half, begin = divmod(block * WINDOW, tokens)
            mixed[half, begin : begin + WINDOW, :] = pick_heads(outs).astype(jnp.bfloat16)
            outs = []


def attend_finish(info, mixed, *refs):
    outs = refs[:SLOTS]
    frames, vec, part_out, normed, weight, mixed_out = refs[SLOTS:]
    core, team = info[3 * TEAM], info[3 * TEAM + 1]
    for k in range(TEAM):
        for j in range(CORES):
            s = k * CORES + j
            columns = slice(s * WIDTH_DEV, (s + 1) * WIDTH_DEV)
            weight[:, columns] = outs[s][...]
            mixed_out[:, columns] = mixed[(team ^ k) * CORES + (core ^ j)]
    part_out[...] = dot_last(mixed_out[...], weight[...])

    def rows(chunk):
        hidden = frames[chunk, :].astype(jnp.float32) + vec[4:5, :] * part_out[chunk, :]
        unit, _ = norm_parts(hidden)
        low = (unit * vec[2:3, :] + vec[3:4, :]).astype(jnp.bfloat16)
        for k in range(TEAM):
            normed[k, chunk, :] = low

    row_chunks(frames.shape[0], 256, rows)


def feed_forward(_, info, normed, cots, vec, own, other, inner, grads, pulls, back):
    count, tokens, _ = normed.shape
    half = FF_DEV // 2

    def flat(ref):
        return jnp.concatenate([ref[g] for g in range(count)], axis=0)

    def spread(ref, columns, value):
        low = value.astype(jnp.bfloat16)
        for g in range(count):
            ref[g, :, columns] = low[g * tokens : (g + 1) * tokens]

    for g in range(count):
        pulls[g] = (cots[g].astype(jnp.float32) * vec[5:6, :]).astype(jnp.bfloat16)
    for w, weight in enumerate((own, other)):
        for f in range(2):
            begin = f * half
            gate_cols = slice(begin, begin + half)
            up_cols = slice(FF_DEV + begin, FF_DEV + begin + half)
            out_cols = slice(2 * FF_DEV + begin, 2 * FF_DEV + begin + half)
            gate = dot(flat(normed), weight[:, gate_cols])
            up = dot(flat(normed), weight[:, up_cols])
            grad_inner = dot(flat(pulls), weight[:, out_cols])
            sigmoid = jax.nn.sigmoid(gate)
            silu = gate * sigmoid
            inner_cols = slice(w * FF_DEV + begin, w * FF_DEV + begin + half)
            spread(inner, inner_cols, silu * up)
            slope = grad_inner * up * sigmoid * (1.0 + gate * (1.0 - sigmoid))
            shift = 2 * w * FF_DEV
            spread(grads, slice(shift + begin, shift + begin + half), slope)
            begin += shift + FF_DEV
            spread(grads, slice(begin, begin + half), grad_inner * silu)
    width = 2 * FF_DEV
    total = dot_last(
        jnp.concatenate([grads[g, :, :width] for g in range(count)], axis=0), own[:, :width]
    ) + dot_last(
        jnp.concatenate([grads[g, :, width:] for g in range(count)], axis=0), other[:, :width]
    )
    spread(back, slice(None), total)


def feed_branch(info, inner, cots, own, other, _, keep, send1, send2, send3, sums, part):
    team = info[3 * TEAM + 1]
    tokens = keep.shape[0]
    sums[...] = jnp.zeros_like(sums)
    for k, out in enumerate((keep, send1, send2, send3)):
        part[...] = dot_last(inner[team ^ k, :, :FF_DEV], own[:, 2 * FF_DEV :]) + dot_last(
            inner[team ^ k, :, FF_DEV:], other[:, 2 * FF_DEV :]
        )

        def rows(chunk, k=k, out=out):
            piece = part[chunk, :]
            cot = cots[team ^ k, chunk, :].astype(jnp.float32)
            sums[0:1, :] += jnp.sum(piece * cot, axis=0, keepdims=True)
            out[chunk, :] = piece.astype(out.dtype)

        row_chunks(tokens, 256, rows)


def feed_terms(normed, grads, pulls, inner, own, other):
    def flat(ref, columns):
        return jnp.concatenate([ref[g, :, columns] for g in range(ref.shape[0])], axis=0)

    left, pull = flat(normed, slice(None)), flat(pulls, slice(None))
    for w, out in enumerate((own, other)):
        columns = slice(2 * w * FF_DEV, 2 * (w + 1) * FF_DEV)
        out[:, : 2 * FF_DEV] = dot_rows(left, flat(grads, columns)).astype(jnp.bfloat16)
        columns = slice(w * FF_DEV, (w + 1) * FF_DEV)
        out[:, 2 * FF_DEV :] = dot_rows(pull, flat(inner, columns)).astype(jnp.bfloat16)


def add_pieces(pieces, chunk):
    total = pieces[0][chunk, :]
    for piece in pieces[1:]:
        total = total + piece[chunk, :].astype(jnp.float32)
    return total


def attend_back_start(info, back_sum, vec, part_out, frames, cotangent, weight, mixed, _, *refs):
    grad_hidden, sums, grad_mixed, term_own, term_other, grad_attend = refs
    core, team = info[3 * TEAM], info[3 * TEAM + 1]
    sums[...] = jnp.zeros_like(sums)

    def rows(chunk):
        grad_normed = back_sum[chunk, :].astype(jnp.float32)
        attended = part_out[chunk, :]
        unit, scaling = norm_parts(frames[chunk, :].astype(jnp.float32) + vec[4:5, :] * attended)
        grad = cotangent[chunk, :].astype(jnp.float32) + norm_back(
            grad_normed, unit, scaling, vec[2:3, :]
        )
        grad_hidden[chunk, :] = grad
        grad_attend[chunk, :] = (grad * vec[4:5, :]).astype(jnp.bfloat16)
        sums[0:1, :] += jnp.sum(grad_normed * unit, axis=0, keepdims=True)
        sums[1:2, :] += jnp.sum(grad_normed, axis=0, keepdims=True)
        sums[2:3, :] += jnp.sum(grad * attended, axis=0, keepdims=True)

    row_chunks(frames.shape[0], 256, rows)
    grads = dot(grad_attend[...], weight[...]).astype(jnp.bfloat16)
    terms = dot_rows(grad_attend[...], mixed[...]).astype(jnp.bfloat16)
    for k in range(TEAM):
        for j in range(CORES):
            s = k * CORES + j
            columns = slice(s * WIDTH_DEV, (s + 1) * WIDTH_DEV)
            grad_mixed[(team ^ k) * CORES + (core ^ j)] = grads[:, columns]
            (term_other if j else term_own)[team ^ k] = terms[:, columns]


def attend_backward(first, info, *refs):
    grad_mixed, frames, normed, rows_in, win, cosines, sines, _ = refs[:8]
    term, sums, keep, send, joint, key_total, value_total, back = refs[8:]
    step = pl.program_id(0)
    core = info[3 * TEAM]
    k = info[3 * TEAM + 1] ^ (first + step)
    tokens = frames.shape[1]
    group = CORES * tokens
    width = WIDTH_DEV
    key_total[...] = jnp.zeros_like(key_total)
    value_total[...] = jnp.zeros_like(value_total)
    blocks = range(group // WINDOW)
    tiles = [(block, head) for block in blocks for head in range(HEADS_DEV)]
    masks = [span_mask(info, k, block, group) for block in blocks]

    def products(block, head):
        low, high = key_span(block, group)
        query = head_lanes(rows_in[0, block * WINDOW : (block + 1) * WINDOW, :width], head)
        half, begin = divmod(block * WINDOW, tokens)
        grad = head_lanes(grad_mixed[half, begin : begin + WINDOW, :], head)
        scores = dot_last(query, rows_in[0, low:high, width : 2 * width])
        return query, grad, scores, dot_last(grad, rows_in[0, low:high, 2 * width :])

    def unrotated(x, rows):
        return (x * cosines[0, rows, :] - half_swap(x) * sines[0, rows, :]).astype(jnp.bfloat16)

    ahead = products(*tiles[0])
    outs = []
    for i, (block, head) in enumerate(tiles):
        query, grad, scores, grad_probability = ahead
        if i + 1 < len(tiles):
            ahead = products(*tiles[i + 1])
        low, high = key_span(block, group)
        probability = softmax_rows(scores, masks[block])
        delta = jnp.sum(probability * grad_probability, axis=-1, keepdims=True)
        grad_scores = (probability * (grad_probability - delta)).astype(jnp.bfloat16)
        outs.append(dot(grad_scores, rows_in[0, low:high, width : 2 * width]))
        key_total[low:high, :] += dot_rows(grad_scores, query)
        value_total[low:high, :] += dot_rows(probability.astype(jnp.bfloat16), grad)
        if head == HEADS_DEV - 1:
            rows = slice(block * WINDOW, (block + 1) * WINDOW)
            joint[rows, :width] = unrotated(pick_heads(outs) * SCORE_SCALE, rows)
            outs = []
    for half in range(CORES):
        rows = slice(half * tokens, (half + 1) * tokens)
        joint[rows, width : 2 * width] = unrotated(key_total[rows, :] * SCORE_SCALE, rows)
        joint[rows, 2 * width :] = value_total[rows, :].astype(jnp.bfloat16)

    @pl.when(step == 0)
    def _():
        term[...] = jnp.zeros_like(term)
        sums[...] = jnp.zeros_like(sums)

    both = jnp.concatenate([normed[half] for half in range(CORES)], axis=0)
    term[...] += dot_rows(both, joint[...])
    back[...] = dot_last(joint[...], win[...])
    for half in range(CORES):

        def rows(chunk, half=half):
            part = back[pl.ds(chunk.start + half * tokens, chunk.size), :]
            unit, _ = norm_parts(frames[half, chunk, :].astype(jnp.float32))
            sums[0:1, :] += jnp.sum(part * unit, axis=0, keepdims=True)
            sums[1:2, :] += jnp.sum(part, axis=0, keepdims=True)

        row_chunks(tokens, 256, rows)
    keep[0] = back[pl.ds(pl.multiple_of(core * tokens, tokens), tokens), :]
    send[0] = back[pl.ds(pl.multiple_of((1 - core) * tokens, tokens), tokens), :].astype(jnp.bfloat16)


def join_terms(far, near, parts, *refs):
    out = refs[-1]

    def rows(chunk):
        for part in range(3):
            columns = slice(part * WIDTH_DEV, (part + 1) * WIDTH_DEV)
            out[part, chunk, :] = (far[chunk, columns] + near[chunk, columns]).astype(jnp.bfloat16)
        total = parts[0, chunk, :].astype(jnp.float32)
        for p in range(1, TEAM):
            total = total + parts[p, chunk, :].astype(jnp.float32)
        out[3, chunk, :] = total.astype(jnp.bfloat16)

    row_chunks(D, 128, rows)


def own_sums(last, late, _, grad_in, grad_out, grad_expand, grad_contract, grad_gains, squares):
    rows = grad_in.shape[0]
    devices = last.shape[0]
    total = jnp.zeros((rows, 128), jnp.float32)
    for p in range(SLOTS):
        for part in range(4):
            band = slice(part * rows, (part + 1) * rows)
            value = last[p, band, :].astype(jnp.float32)
            for r in range(1, devices // SLOTS):
                value = value + last[r * SLOTS + p, band, :].astype(jnp.float32)
            total = total + value * value
            begin = p * WIDTH_DEV
            if part < 3:
                grad_in[:, part * D + begin : part * D + begin + WIDTH_DEV] = value
            else:
                grad_out[:, begin : begin + WIDTH_DEV] = value
        for f in range(3 * FF_DEV // 128):
            value = late[p, :, f * 128 : (f + 1) * 128].astype(jnp.float32)
            total = total + value * value
            which, begin = divmod(f * 128, FF_DEV)
            begin += p * FF_DEV
            if which < 2:
                grad_expand[:, which * FF + begin : which * FF + begin + 128] = value
            else:
                grad_contract[:, begin : begin + 128] = value
    value = last[0, 4 * rows : 4 * rows + 16, :].astype(jnp.float32)
    for d in range(1, devices):
        value = value + last[d, 4 * rows : 4 * rows + 16, :].astype(jnp.float32)
    value = value[:8]
    grad_gains[...] = value
    whole = jnp.sum(total) + jnp.sum(value * value)
    squares[...] = jnp.full(squares.shape, whole, jnp.float32)


def adam_all(rates, squares_in, *refs):
    grads, weights, means, squares = refs[:4], refs[4:8], refs[8:12], refs[12:16]
    gain_grads, gains, gain_means, gain_squares = refs[16:20]
    norm_out = refs[21]
    outs, gain_outs = refs[22:38], refs[38:]
    norm = jnp.sqrt(jnp.sum(squares_in[:, 0:1, 0:1]))
    factor = CLIP_NORM / jnp.maximum(norm, CLIP_NORM)
    norm_out[0, 0] = norm

    def update(weight, mean, square, grad, rate, new):
        mean_new, square_new, moved = adam_step(weight, mean, square, grad, factor, rate)
        new[0][...] = mean_new
        new[1][...] = square_new
        new[2][...] = moved
        new[3][...] = moved.astype(jnp.bfloat16)

    for i in range(4):
        update(
            weights[i][...], means[i][...], squares[i][...], grads[i][...], rates[i], outs[i::4]
        )
    count, width = gains.shape
    update(
        gains[...],
        gain_means[...],
        gain_squares[...],
        gain_grads[:count, :width],
        VECTOR_RATE,
        gain_outs,
    )


def frames_back(*refs):
    pieces = refs[: TEAM + 1]
    frames, grad_hidden, vec, _, out = refs[TEAM + 1 :]

    def rows(chunk):
        grad_normed = add_pieces(pieces, chunk)
        unit, scaling = norm_parts(frames[chunk, :].astype(jnp.float32))
        out[chunk, :] = grad_hidden[chunk, :] + norm_back(grad_normed, unit, scaling, vec[0:1, :])

    row_chunks(frames.shape[0], 256, rows)


def frames_out(*refs):
    pieces = refs[:TEAM]
    frames, part_out, vec, _, out = refs[TEAM:]

    def rows(chunk):
        branch = add_pieces(pieces, chunk)
        hidden = frames[chunk, :].astype(jnp.float32) + vec[4:5, :] * part_out[chunk, :]
        out[chunk, :] = (hidden + vec[5:6, :] * branch).astype(jnp.bfloat16)

    row_chunks(frames.shape[0], 256, rows)


def per_device(
    frames,
    clip_lengths,
    cotangent,
    attend_in,
    attend_out,
    expand,
    contract,
    gains,
    prior_mean_attend_in,
    prior_mean_attend_out,
    prior_mean_expand,
    prior_mean_contract,
    prior_mean_gains,
    prior_square_attend_in,
    prior_square_attend_out,
    prior_square_expand,
    prior_square_contract,
    prior_square_gains,
):
    bf16 = jnp.bfloat16
    f32 = jnp.float32
    tokens = frames.shape[0]
    group = tokens * CORES
    rows = attend_in.shape[0]
    gain_width = gains.shape[1]
    reps = lax.axis_size("rep")
    devices = reps * SLOTS
    rep = lax.axis_index("rep")
    team = lax.axis_index("team")
    core = lax.axis_index("tm")

    frames_team = lax.all_gather(frames, MEMBERS, axis=0, tiled=False)

    tail_rows = 16
    lanes = 128
    parts = attend_in.astype(bf16).reshape(rows, 3, SLOTS, WIDTH_DEV).transpose(2, 1, 0, 3)
    parts = jnp.concatenate(
        [parts, attend_out.astype(bf16).reshape(rows, 1, SLOTS, WIDTH_DEV).transpose(2, 1, 0, 3)],
        axis=1,
    ).reshape(SLOTS, 4 * rows, lanes)
    small = jnp.zeros((tail_rows, lanes), f32)
    small = small.at[:6, :gain_width].set(gains)
    small = small.at[6, :3].set((clip_lengths[0] // 16).astype(f32))
    small = small.at[7, :3].set((clip_lengths[0] % 16).astype(f32))
    small = jnp.broadcast_to(small.astype(bf16)[None], (SLOTS, tail_rows, lanes))
    parts = jnp.concatenate([parts, small], axis=1)
    parts = jnp.broadcast_to(parts[None], (reps,) + parts.shape)
    spread = lax.all_to_all(
        parts.reshape(devices, 4 * rows + tail_rows, lanes), ALL, 0, 0, tiled=True
    )
    part_in = spread[:, : 3 * rows].reshape(devices, 3, rows, lanes).transpose(0, 2, 1, 3)
    part_in = part_in.reshape(D, 3 * WIDTH_DEV)
    part_out = spread[:, 3 * rows : 4 * rows].reshape(D, WIDTH_DEV)
    small = spread[:, 4 * rows : 4 * rows + 8].astype(f32)
    vectors = small[:, :6, :gain_width].transpose(1, 0, 2).reshape(6, D)
    vectors = jnp.pad(vectors, ((0, 2), (0, 0)))
    lengths = lax.dynamic_index_in_dim(
        small[:, 6:, :3].reshape(reps, TEAM, CORES, 2, 3)[:, :, 0], rep, 0, keepdims=False
    )
    lengths = (lengths[:, 0] * 16 + lengths[:, 1]).astype(jnp.int32)
    info = jnp.concatenate([lengths.reshape(-1), jnp.stack([core, team])])

    mlp_pack = jnp.concatenate(
        [
            expand.astype(bf16).reshape(rows, 2, SLOTS, FF_DEV).transpose(2, 0, 1, 3).reshape(
                SLOTS, rows, 2 * FF_DEV
            ),
            contract.astype(bf16).reshape(rows, SLOTS, FF_DEV).transpose(1, 0, 2),
        ],
        axis=2,
    )
    mlp_cols = exchange_team(after(mlp_pack, spread[0, :16])).reshape(SLOTS * rows, 3 * FF_DEV)
    outs_team = gather_team(part_out)
    cot_blocks = jnp.broadcast_to(cotangent[None], (TEAM, tokens, D))
    cots_own = lax.all_to_all(after(cot_blocks, mlp_cols[:16, :128]), "team", 0, 0, tiled=True)

    places = jnp.arange(group, dtype=jnp.int32)
    ends = jnp.cumsum(lengths, axis=1)
    starts = ends - lengths
    begin = jnp.max(
        jnp.where(starts[:, None, :] <= places[None, :, None], starts[:, None, :], 0), axis=2
    )
    offsets = (places[None] - begin).astype(f32)
    freqs = np.power(10000.0, -2.0 * np.arange(HEAD // 2) / HEAD)
    lane_freqs = jnp.asarray(np.tile(freqs, WIDTH_DEV // (HEAD // 2)), dtype=f32)
    angles = offsets[:, :, None] * lane_freqs
    signs = jnp.asarray(np.where(np.arange(WIDTH_DEV) % HEAD < HEAD // 2, -1.0, 1.0), dtype=f32)
    cosines = jnp.cos(angles)
    sines = jnp.sin(angles) * signs
    mlp_weight = lax.all_gather(after(mlp_cols, sines[0, :8], frames_team[0, :16, :128]), "rep", axis=0, tiled=True)

    by_frames = (CORES, tokens, D)
    by_heads = (CORES, tokens, WIDTH_DEV)
    by_rows = (1, group, 3 * WIDTH_DEV)
    by_angles = (1, group, WIDTH_DEV)
    normed_one, attend_rows, mixed = call_groups(
        attend_forward,
        info,
        [
            (in_hbm(frames_team), by_frames),
            (vectors, None),
            (part_in, None),
            (in_hbm(cosines), by_angles),
            (in_hbm(sines), by_angles),
        ],
        [
            ((SLOTS, tokens, D), bf16, by_frames, HBM_OUT),
            ((TEAM, group, 3 * WIDTH_DEV), bf16, by_rows, HBM_OUT),
            ((SLOTS, tokens, WIDTH_DEV), bf16, by_heads, PLAIN),
        ],
        name="attend_forward",
        micros=24,
    )

    cots_own = after(cots_own, mixed[0, :16])

    mixed_own = exchange_team(after(mixed, cots_own[0, :16, :128]))
    attend_part, normed_two, full_out, mixed_flat = call_kernel(
        attend_finish,
        [info, mixed_own, *outs_team, frames, vectors],
        [
            ((tokens, D), f32, HBM_OUT),
            ((TEAM, tokens, D), bf16),
            ((D, D), bf16, HBM_OUT),
            ((tokens, D), bf16, HBM_OUT),
        ],
        specs=[SMEM_SPEC] + [VMEM_SPEC] * (SLOTS + 3),
        far=(10,),
        name="attend_finish",
        micros=4,
    )

    weight_own = after(mlp_weight, normed_two[0, :16, :128])
    weight_other = other_core(weight_own)
    normed_team = lax.all_to_all(normed_two, "team", 0, 0, tiled=True)
    by_pairs = (TEAM // 2, tokens, D)
    inner, grads_up, pulls, back = call_groups(
        feed_forward,
        info,
        [
            (normed_team, by_pairs),
            (in_hbm(cots_own), by_pairs),
            (vectors, None),
            (weight_own, None),
            (weight_other, None),
        ],
        [
            ((TEAM, tokens, 2 * FF_DEV), bf16, (TEAM // 2, tokens, 2 * FF_DEV), HBM_OUT),
            ((TEAM, tokens, 4 * FF_DEV), bf16, (TEAM // 2, tokens, 4 * FF_DEV), HBM_OUT),
            ((TEAM, tokens, D), bf16, by_pairs, HBM_OUT),
            ((TEAM, tokens, D), bf16, by_pairs, HBM_OUT),
        ],
        steps=2,
        vmem=26,
        name="feed_forward",
        micros=20,
    )
    back_sum = lax.psum_scatter(back, "team", scatter_dimension=0, tiled=False)
    term_own, term_other = call_terms(normed_team, grads_up, pulls, inner)
    term_got = other_core(term_other)
    branch_keep, *branch_sends, sums_out = call_kernel(
        feed_branch,
        [info, inner, cots_own, weight_own, weight_other, term_own[:16, :128]],
        [((tokens, D), f32, HBM_OUT)] + [((tokens, D), bf16)] * 3 + [((8, D), f32)],
        scratch=[pltpu.VMEM((tokens, D), f32)],
        specs=[SMEM_SPEC] + [VMEM_SPEC] * 4 + [ANY_SPEC],
        far=(1, 2),
        name="feed_branch",
        micros=9,
    )
    term_got = after(term_got, sums_out)
    term_mlp = (term_own.astype(f32) + term_got.astype(f32)).astype(bf16)
    mlp_sum = lax.psum_scatter(term_mlp, "rep", scatter_dimension=0, tiled=True)

    loads = [attend_part, frames, cotangent, full_out, mixed_flat]
    grad_hidden, sums_two, grad_mixed, term_own, term_other = call_kernel(
        attend_back_start,
        [info, back_sum, vectors, *loads, sums_out],
        [
            ((tokens, D), f32, HBM_OUT),
            ((8, D), f32),
            ((SLOTS, tokens, WIDTH_DEV), bf16),
            ((TEAM, D, WIDTH_DEV), bf16),
            ((TEAM, D, WIDTH_DEV), bf16),
        ],
        scratch=[pltpu.VMEM((tokens, D), bf16)],
        specs=[SMEM_SPEC] + [VMEM_SPEC] * (len(loads) + 2) + [ANY_SPEC],
        far=(3, 4, 5, 6, 7),
        vmem=24,
        name="attend_back_start",
        micros=6,
    )
    grad_mixed = exchange_team(grad_mixed)
    out_sum = (term_own.astype(f32) + other_core(term_other).astype(f32)).astype(bf16)
    out_parts = lax.all_to_all(after(out_sum, grad_mixed[0, :16]), "team", 0, 0, tiled=True)
    branch_pieces = [branch_keep]
    branch_pieces += send_mates([after(x, out_sum[0, :16]) for x in branch_sends])

    halves = []
    for begin in (TEAM // 2, 0):
        token = after(vectors, out_sum[0, :16])
        if halves:
            token = halves[0][1]
        halves.append(
            call_groups(
                attend_backward,
                info,
                [
                    (grad_mixed, by_heads),
                    (in_hbm(frames_team), by_frames),
                    (in_hbm(normed_one), by_frames),
                    (in_hbm(attend_rows), by_rows),
                    (part_in, None),
                    (in_hbm(cosines), by_angles),
                    (in_hbm(sines), by_angles),
                    (token, None),
                ],
                [
                    ((D, 3 * WIDTH_DEV), f32, None, PLAIN),
                    ((8, D), f32, None, PLAIN),
                    ((TEAM // 2, tokens, D), f32, (1, tokens, D), HBM_OUT),
                    ((TEAM // 2, tokens, D), bf16, (1, tokens, D), HBM_OUT),
                ],
                scratch=[
                    pltpu.VMEM((group, 3 * WIDTH_DEV), bf16),
                    pltpu.VMEM((group, WIDTH_DEV), f32),
                    pltpu.VMEM((group, WIDTH_DEV), f32),
                    pltpu.VMEM((group, D), f32),
                ],
                mates=(begin, TEAM // 2),
                name="attend_backward",
                micros=17,
            )
        )
    (term_far, _, far_keep, far_send), (term_near, sums_near, near_keep, near_send) = halves
    sums_far = halves[0][1]
    late = exchange_team(after(mlp_sum.reshape(SLOTS, rows, 3 * FF_DEV), sums_far, out_parts[0, :16]))

    (out_frames,) = call_kernel(
        frames_out,
        [*branch_pieces, frames, attend_part, vectors, sums_near],
        [((tokens, D), bf16)],
        far=(0, 4, 5),
        name="frames_out",
        micros=3,
    )
    far_got, near_got = other_core(far_send), other_core(near_send)
    keeps = [near_keep[0], near_keep[1], far_keep[0], far_keep[1]]
    gots = [near_got[0], near_got[1], far_got[0], far_got[1]]
    one_pieces = [keeps[0], gots[0]] + send_mates(chip_sums(keeps, gots))
    (frames_grad,) = call_kernel(
        frames_back,
        [*one_pieces, frames, grad_hidden, vectors, vectors],
        [((tokens, D), f32)],
        specs=[VMEM_SPEC] * (TEAM + 4) + [ANY_SPEC],
        far=(5, 6),
        name="frames_back",
        micros=4,
    )
    (terms,) = call_kernel(
        join_terms,
        [term_far, term_near, out_parts, late[0, :16, :128]]
        + [x[:16, :128] for x in branch_pieces[1:]],
        [((4, D, WIDTH_DEV), bf16)],
        name="join_terms",
        micros=2,
    )
    term_gains = jnp.concatenate([sums_far[:2] + sums_near[:2], sums_two[:3], sums_out[:1]])
    gains_block = jnp.zeros((devices, tail_rows, lanes), bf16)
    gains_block = gains_block.at[:, :6, :gain_width].set(
        term_gains.astype(bf16).reshape(6, devices, gain_width).transpose(1, 0, 2)
    )
    terms = terms.reshape(4, devices, rows, lanes).transpose(1, 0, 2, 3)
    last = lax.all_to_all(
        jnp.concatenate([terms.reshape(devices, 4 * rows, lanes), gains_block], axis=1),
        ALL,
        0,
        0,
        tiled=True,
    )
    shapes = [(rows, 3 * D), (rows, D), (rows, 2 * FF), (rows, FF), (8, lanes)]
    if rows % 16 == 0:
        *owned, squares_out = call_kernel(
            own_sums,
            [last, late, out_frames[:16, :128]],
            [(shape, f32) for shape in shapes] + [((devices, 8, lanes), f32)],
            vmem=16,
            name="own_sums",
            micros=4,
        )
    else:
        last_sum = jnp.sum(
            last[:, : 4 * rows].reshape(reps, SLOTS, 4, rows, lanes).astype(f32), axis=0
        )
        late = late.astype(f32)
        owned = [
            last_sum[:, :3].transpose(2, 1, 0, 3).reshape(rows, 3 * D),
            last_sum[:, 3].transpose(1, 0, 2).reshape(rows, D),
            late[:, :, : 2 * FF_DEV]
            .reshape(SLOTS, rows, 2, FF_DEV)
            .transpose(1, 2, 0, 3)
            .reshape(rows, 2 * FF),
            late[:, :, 2 * FF_DEV :].transpose(1, 0, 2).reshape(rows, FF),
            jnp.sum(last[:, 4 * rows : 4 * rows + 8].astype(f32), axis=0),
        ]
        square_part = jnp.zeros((), f32)
        for grad in owned:
            square_part = square_part + jnp.sum(grad * grad)
        squares_out = jnp.full((devices, 8, lanes), square_part)
    squares_in = lax.all_to_all(squares_out, ALL, 0, 0, tiled=True)

    weights = [attend_in, attend_out, expand, contract]
    means = [prior_mean_attend_in, prior_mean_attend_out, prior_mean_expand, prior_mean_contract]
    squares = [
        prior_square_attend_in,
        prior_square_attend_out,
        prior_square_expand,
        prior_square_contract,
    ]
    rates = (RATE / math.sqrt(D), RATE / math.sqrt(D // 64), RATE / math.sqrt(D), RATE / math.sqrt(FF))
    steps = 4
    columns = [pl.BlockSpec((rows, x.shape[1] // steps), lambda i: (0, i)) for x in weights]
    whole = pl.BlockSpec(gains.shape, lambda i: (0, 0))
    out = pl.pallas_call(
        functools.partial(adam_all, rates),
        grid=(steps,),
        in_specs=[pl.BlockSpec(squares_in.shape, lambda i: (0, 0, 0))]
        + columns * 4
        + [pl.BlockSpec((8, lanes), lambda i: (0, 0))]
        + [whole] * 3
        + [ANY_SPEC],
        out_specs=[pl.BlockSpec(memory_space=pltpu.SMEM)] + columns * 4 + [whole] * 4,
        out_shape=[jax.ShapeDtypeStruct((1, 1), f32)]
        + [
            jax.ShapeDtypeStruct(x.shape, dtype) for dtype in (f32, f32, f32, bf16) for x in weights
        ]
        + [jax.ShapeDtypeStruct(gains.shape, dtype) for dtype in (f32, f32, f32, bf16)],
        compiler_params=pltpu.CompilerParams(vmem_limit_bytes=24 * MIB),
        cost_estimate=cost(8),
        name="adam_all",
    )(
        squares_in,
        *[in_hbm(x) for x in (*owned[:4], *weights, *means, *squares)],
        owned[4],
        gains,
        prior_mean_gains,
        prior_square_gains,
        frames_grad[:8, :128],
    )
    news = [out[1 + kind * 4 + which] for which in range(4) for kind in range(4)]
    return (out_frames, frames_grad, out[0][0, 0], *news, *out[17:])


def solution(mesh):
    teams = Mesh(
        mesh.devices.reshape(mesh.shape["dp"] // TEAM, TEAM, mesh.shape["tm"]), ALL
    )
    by_row = P(ALL, None)
    by_column = P(None, ALL)
    per_group = P(("rep", "team"), None)
    weights = (by_row, by_row, by_row, by_row, by_column)
    return jax.shard_map(
        per_device,
        mesh=teams,
        in_specs=(by_row, per_group, by_row) + weights * 3,
        out_specs=(by_row, by_row, P()) + (by_row,) * 16 + (by_column,) * 4,
        check_vma=False,
    )
```

```python
import functools
import math

import jax
import jax.numpy as jnp
import numpy as np
from jax import lax
from jax.experimental import pallas as pl
from jax.experimental.pallas import tpu as pltpu
from jax.sharding import Mesh
from jax.sharding import PartitionSpec as P

D = 1024
HEADS = 16
HEAD = 64
FF = 4096
WINDOW = 128
STEP = 10

EPS_NORM = 1e-05
NEG_FILL = -1e30
SCORE_SCALE = 0.125
BETA_ONE = 0.9
BETA_TWO = 0.999
ADAM_EPS = 1e-08
DECAY = 0.1
RATE = 3.0
VECTOR_RATE = 0.6
CLIP_NORM = 1.0

TEAM = 4
CORES = 2
SLOTS = TEAM * CORES
ALL = ("rep", "team", "tm")
MEMBERS = ("team", "tm")
ANY_SPEC = pl.BlockSpec(memory_space=pl.ANY)
SMEM_SPEC = pl.BlockSpec(memory_space=pltpu.SMEM)
VMEM_SPEC = pl.BlockSpec(memory_space=pltpu.VMEM)
MIB = 1 << 20
PLAIN, HBM_OUT = range(2)
HBM_SPEC = pl.BlockSpec(memory_space=pltpu.HBM)
LOG2_E = math.log2(math.e)
HEADS_DEV = HEADS // SLOTS
WIDTH_DEV = HEADS_DEV * HEAD
FF_DEV = FF // SLOTS


def swap_pairs(count, bit):
    return [(a, a ^ bit) for a in range(count)]


def other_core(x):
    return lax.ppermute(x, "tm", swap_pairs(CORES, 1))


def to_mate(x, bit):
    return lax.ppermute(x, "team", swap_pairs(TEAM, bit))


def gather_team(x):
    blocks = [x] + [to_mate(x, k) for k in range(1, TEAM)]
    parts = []
    for block in blocks:
        parts += [block, other_core(block)]
    return parts


def chip_sums(keep, got):
    return [
        (keep[k] + got[k].astype(jnp.float32)).astype(jnp.bfloat16) for k in range(1, TEAM)
    ]


def send_mates(chips):
    return [to_mate(chip, k + 1) for k, chip in enumerate(chips)]


def exchange_team(x):
    return lax.all_to_all(x, MEMBERS, 0, 0, tiled=True)


def after(x, *tokens):
    return pl.pallas_call(
        lambda *refs: None,
        out_shape=jax.ShapeDtypeStruct(x.shape, x.dtype),
        in_specs=[ANY_SPEC] * (1 + len(tokens)),
        out_specs=ANY_SPEC,
        input_output_aliases={0: 0},
        name="after",
    )(x, *tokens)


def norm_parts(values):
    centered = values - jnp.mean(values, axis=-1, keepdims=True)
    scaling = lax.rsqrt(jnp.mean(centered * centered, axis=-1, keepdims=True) + EPS_NORM)
    return (centered * scaling, scaling)


def norm_back(gradient, unit_rows, scaling, gain_row):
    scaled = gradient * gain_row
    return scaling * (
        scaled
        - jnp.mean(scaled, axis=-1, keepdims=True)
        - unit_rows * jnp.mean(scaled * unit_rows, axis=-1, keepdims=True)
    )


def dot_rows(left_side, right_side):
    return lax.dot_general(
        left_side, right_side, (((0,), (0,)), ((), ())), preferred_element_type=jnp.float32
    )


def dot_last(left_side, right_side):
    return lax.dot_general(
        left_side, right_side, (((1,), (1,)), ((), ())), preferred_element_type=jnp.float32
    )


def dot(left_side, right_side):
    return jnp.dot(left_side, right_side, preferred_element_type=jnp.float32)


def adam_step(weight, mean_old, square_old, gradient, factor, step_rate):
    clipped = gradient * factor
    mean_new = BETA_ONE * mean_old + (1.0 - BETA_ONE) * clipped
    square_new = BETA_TWO * square_old + (1.0 - BETA_TWO) * clipped * clipped
    mean_hat = mean_new / (1.0 - BETA_ONE**STEP)
    square_hat = square_new / (1.0 - BETA_TWO**STEP)
    moved = weight - step_rate * (mean_hat / (jnp.sqrt(square_hat) + ADAM_EPS) + DECAY * weight)
    return (mean_new, square_new, moved)


def in_hbm(x):
    return pltpu.with_memory_space_constraint(x, pltpu.HBM)


def cost(micros):
    return pl.CostEstimate(flops=int(micros * 1e9), transcendentals=0, bytes_accessed=int(micros * 1e6))


def call_kernel(
    kernel, ins, outs, scratch=(), specs=None, far=(), vmem=16, name=None, micros=2
):
    specs = list(specs or [VMEM_SPEC] * len(ins))
    ins = list(ins)
    buffers = [pltpu.VMEM(ins[i].shape, ins[i].dtype) for i in far]
    for i in far:
        specs[i] = HBM_SPEC
        ins[i] = in_hbm(ins[i])

    def loaded(*refs):
        refs = list(refs)
        if far:
            near, sems = refs[-1 - len(far) : -1], refs[-1]
            refs = refs[: -1 - len(far)]
            copies = [
                pltpu.make_async_copy(refs[i], b, sems.at[n]) for n, (i, b) in enumerate(zip(far, near))
            ]
            for copy in copies:
                copy.start()
            for copy in copies:
                copy.wait()
            for i, b in zip(far, near):
                refs[i] = b
        kernel(*refs)

    return pl.pallas_call(
        loaded,
        out_shape=[
            (pltpu.HBM if mode else jax.ShapeDtypeStruct)(shape, dtype) for shape, dtype, *mode in outs
        ],
        in_specs=specs,
        out_specs=[VMEM_SPEC] * len(outs),
        scratch_shapes=[
            *scratch,
            *buffers,
            *([pltpu.SemaphoreType.DMA((len(far),))] if far else []),
        ],
        compiler_params=pltpu.CompilerParams(vmem_limit_bytes=vmem * MIB),
        cost_estimate=cost(micros),
        name=name,
    )(*ins)


def call_terms(normed, grads, pulls, inner):
    count, tokens, _ = normed.shape
    step = 256
    by_rows = pl.BlockSpec((count, tokens, step), lambda r: (0, 0, r))

    def whole(x):
        return pl.BlockSpec(x.shape, lambda r: (0, 0, 0), pipeline_mode=pl.Buffered(1))

    return pl.pallas_call(
        feed_terms,
        grid=(D // step,),
        in_specs=[by_rows, whole(grads), by_rows, whole(inner)],
        out_specs=[pl.BlockSpec((step, 3 * FF_DEV), lambda r: (r, 0))] * 2,
        out_shape=[
            pltpu.HBM((D, 3 * FF_DEV), jnp.bfloat16),
            jax.ShapeDtypeStruct((D, 3 * FF_DEV), jnp.bfloat16),
        ],
        compiler_params=pltpu.CompilerParams(vmem_limit_bytes=24 * MIB),
        cost_estimate=cost(8),
        name="feed_terms",
    )(in_hbm(normed), in_hbm(grads), in_hbm(pulls), in_hbm(inner))


def call_groups(
    kernel, info, ins, outs, scratch=(), vmem=24, name=None, micros=20, mates=None, steps=TEAM
):
    def spec(shape, block, out):
        rest = (0,) * (len(shape) - 1)
        if block == "far":
            return HBM_SPEC
        if block is None:
            return pl.BlockSpec(
                shape, lambda g, info: (0, *rest), pipeline_mode=None if out else pl.Buffered(1)
            )
        if mates and not out:
            return pl.BlockSpec(block, lambda g, info: (info[3 * TEAM + 1] ^ (mates[0] + g), *rest))
        return pl.BlockSpec(block, lambda g, info: (g, *rest))

    return pl.pallas_call(
        functools.partial(kernel, mates[0] if mates else 0),
        grid_spec=pltpu.PrefetchScalarGridSpec(
            num_scalar_prefetch=1,
            grid=(mates[1] if mates else steps,),
            in_specs=[spec(x.shape, block, False) for x, block in ins],
            out_specs=[spec(shape, block, True) for shape, _, block, _ in outs],
            scratch_shapes=list(scratch),
        ),
        out_shape=[
            jax.ShapeDtypeStruct(shape, dtype) if mode == PLAIN else pltpu.HBM(shape, dtype)
            for shape, dtype, _, mode in outs
        ],
        compiler_params=pltpu.CompilerParams(vmem_limit_bytes=vmem * MIB),
        cost_estimate=cost(micros),
        name=name,
    )(info, *[x for x, _ in ins])


def row_chunks(count, size, body):
    def step(i, carry):
        body(pl.ds(pl.multiple_of(i * size, size), size))
        return carry

    lax.fori_loop(0, count // size, step, 0)


def lanes_of(x):
    return lax.broadcasted_iota(jnp.int32, (1, x.shape[-1]), 1)


def half_swap(x):
    width = x.shape[-1]
    half = HEAD // 2
    first = (lanes_of(x) & half) == 0
    return jnp.where(first, pltpu.roll(x, width - half, x.ndim - 1), pltpu.roll(x, half, x.ndim - 1))


def key_span(block, group):
    return max(0, (block - 1) * WINDOW), min(group, (block + 2) * WINDOW)


def span_mask(info, slot, block, group):
    low, high = key_span(block, group)
    first = info[3 * slot]
    second = first + info[3 * slot + 1]
    third = second + info[3 * slot + 2]
    place = block * WINDOW + lax.broadcasted_iota(jnp.int32, (WINDOW, 1), 0)
    start = jnp.where(
        place >= third,
        third,
        jnp.where(place >= second, second, jnp.where(place >= first, first, 0)),
    )
    end = jnp.where(
        place < first, first, jnp.where(place < second, second, jnp.where(place < third, third, group))
    )
    least = jnp.maximum(start, place - WINDOW)
    most = jnp.minimum(end, place + WINDOW + 1)
    key_place = low + lax.broadcasted_iota(jnp.int32, (1, high - low), 1)
    return (key_place >= least) & (key_place < most)


def head_lanes(x, head):
    lane = lanes_of(x)
    inside = (lane >= head * HEAD) & (lane < (head + 1) * HEAD)
    return jnp.where(inside, x, jnp.zeros_like(x))


def pick_heads(parts):
    out = parts[0]
    for head in range(1, len(parts)):
        out = jnp.where(lanes_of(out) >= head * HEAD, parts[head], out)
    return out


def softmax_rows(products, allowed):
    scores = jnp.where(allowed, products * (SCORE_SCALE * LOG2_E), NEG_FILL)
    exponent = jnp.exp2(scores - jnp.max(scores, axis=-1, keepdims=True))
    return exponent * (1.0 / jnp.sum(exponent, axis=-1, keepdims=True))


def attend_forward(_, info, frames, vec, win, cosines, sines, normed, rows_out, mixed):
    k = pl.program_id(0)
    tokens = frames.shape[1]
    group = CORES * tokens
    width = WIDTH_DEV
    for half in range(CORES):
        rows = slice(half * tokens, (half + 1) * tokens)

        def norm_rows(chunk, half=half):
            unit, _ = norm_parts(frames[half, chunk, :].astype(jnp.float32))
            normed[half, chunk, :] = (unit * vec[0:1, :] + vec[1:2, :]).astype(jnp.bfloat16)

        row_chunks(tokens, 256, norm_rows)
        joint = dot(normed[half], win[...])
        for part in range(2):
            x = joint[:, part * width : (part + 1) * width]
            rows_out[0, rows, part * width : (part + 1) * width] = (
                x * cosines[0, rows, :] + half_swap(x) * sines[0, rows, :]
            ).astype(jnp.bfloat16)
        rows_out[0, rows, 2 * width :] = joint[:, 2 * width :].astype(jnp.bfloat16)

    blocks = range(group // WINDOW)
    tiles = [(block, head) for block in blocks for head in range(HEADS_DEV)]
    masks = [span_mask(info, k, block, group) for block in blocks]

    def product(block, head):
        low, high = key_span(block, group)
        query = head_lanes(rows_out[0, block * WINDOW : (block + 1) * WINDOW, :width], head)
        return dot_last(query, rows_out[0, low:high, width : 2 * width])

    ahead = product(*tiles[0])
    outs = []
    for i, (block, head) in enumerate(tiles):
        now = ahead
        if i + 1 < len(tiles):
            ahead = product(*tiles[i + 1])
        low, high = key_span(block, group)
        probability = softmax_rows(now, masks[block]).astype(jnp.bfloat16)
        outs.append(dot(probability, rows_out[0, low:high, 2 * width :]))
        if head == HEADS_DEV - 1:
            half, begin = divmod(block * WINDOW, tokens)
            mixed[half, begin : begin + WINDOW, :] = pick_heads(outs).astype(jnp.bfloat16)
            outs = []


def attend_finish(info, mixed, *refs):
    outs = refs[:SLOTS]
    frames, vec = refs[SLOTS : SLOTS + 2]
    part_out, normed, weight, mixed_out = refs[-4:]
    core, team = info[3 * TEAM], info[3 * TEAM + 1]
    for k in range(TEAM):
        for j in range(CORES):
            s = k * CORES + j
            columns = slice(s * WIDTH_DEV, (s + 1) * WIDTH_DEV)
            weight[:, columns] = outs[s][...]
            mixed_out[:, columns] = mixed[(team ^ k) * CORES + (core ^ j)]
    part_out[...] = dot_last(mixed_out[...], weight[...])

    def rows(chunk):
        hidden = frames[chunk, :].astype(jnp.float32) + vec[4:5, :] * part_out[chunk, :]
        unit, _ = norm_parts(hidden)
        low = (unit * vec[2:3, :] + vec[3:4, :]).astype(jnp.bfloat16)
        for k in range(TEAM):
            normed[k, chunk, :] = low

    row_chunks(frames.shape[0], 256, rows)


def half_weight(weight, core, columns):
    return jnp.concatenate([weight[r, core, :, columns] for r in range(weight.shape[0])], axis=0)


def feed_forward(_, info, normed, vec, far_weight, *refs):
    far_cots = refs[:TEAM]
    inner, grads, pulls, back, weight, sems, cots, cot_sems = refs[TEAM:]
    count, tokens, _ = normed.shape
    half = FF_DEV // 2
    core = info[3 * TEAM]

    def flat(ref):
        return jnp.concatenate([ref[g] for g in range(count)], axis=0)

    def spread(ref, columns, value):
        low = value.astype(jnp.bfloat16)
        for g in range(count):
            ref[g, :, columns] = low[g * tokens : (g + 1) * tokens]

    first = pl.program_id(0) == 0
    copies = [
        [
            pltpu.make_async_copy(far_weight.at[r, core ^ w], weight.at[r, core ^ w], sems.at[w, r])
            for r in range(weight.shape[0])
        ]
        for w in range(CORES)
    ]

    cot_copies = [
        pltpu.make_async_copy(cot, cots.at[info[3 * TEAM + 1] ^ k], cot_sems.at[k])
        for k, cot in enumerate(far_cots)
    ]

    @pl.when(first)
    def _():
        for copy in cot_copies + copies[0] + copies[1]:
            copy.start()
        for copy in cot_copies:
            copy.wait()

    for g in range(count):
        cot = cots[count * pl.program_id(0) + g].astype(jnp.float32)
        pulls[g] = (cot * vec[5:6, :]).astype(jnp.bfloat16)
    for w in range(CORES):

        @pl.when(first)
        def _(w=w):
            for copy in copies[w]:
                copy.wait()

        for f in range(2):
            begin = f * half
            gate_cols = slice(begin, begin + half)
            up_cols = slice(FF_DEV + begin, FF_DEV + begin + half)
            out_cols = slice(2 * FF_DEV + begin, 2 * FF_DEV + begin + half)
            gate = dot(flat(normed), half_weight(weight, core ^ w, gate_cols))
            up = dot(flat(normed), half_weight(weight, core ^ w, up_cols))
            grad_inner = dot(flat(pulls), half_weight(weight, core ^ w, out_cols))
            sigmoid = jax.nn.sigmoid(gate)
            silu = gate * sigmoid
            inner_cols = slice(w * FF_DEV + begin, w * FF_DEV + begin + half)
            spread(inner, inner_cols, silu * up)
            slope = grad_inner * up * sigmoid * (1.0 + gate * (1.0 - sigmoid))
            shift = 2 * w * FF_DEV
            spread(grads, slice(shift + begin, shift + begin + half), slope)
            begin += shift + FF_DEV
            spread(grads, slice(begin, begin + half), grad_inner * silu)
    width = 2 * FF_DEV
    total = None
    for w in range(CORES):
        columns = slice(w * width, (w + 1) * width)
        part = dot_last(
            jnp.concatenate([grads[g, :, columns] for g in range(count)], axis=0),
            half_weight(weight, core ^ w, slice(0, width)),
        )
        total = part if total is None else total + part
    spread(back, slice(None), total)


def feed_branch(info, inner, weight, _, *refs):
    cots, (parts, sums) = refs[:TEAM], refs[TEAM:]
    core, team = info[3 * TEAM], info[3 * TEAM + 1]
    sums[...] = jnp.zeros_like(sums)
    columns = slice(2 * FF_DEV, 3 * FF_DEV)
    for k, cot in enumerate(cots):
        part = dot_last(
            inner[team ^ k, :, :FF_DEV], half_weight(weight, core, columns)
        ) + dot_last(inner[team ^ k, :, FF_DEV:], half_weight(weight, 1 - core, columns))
        sums[0:1, :] += jnp.sum(part * cot[...].astype(jnp.float32), axis=0, keepdims=True)
        parts[team ^ k] = part.astype(jnp.bfloat16)


def feed_terms(normed, grads, pulls, inner, own, other):
    def flat(ref, columns):
        return jnp.concatenate([ref[g, :, columns] for g in range(ref.shape[0])], axis=0)

    left, pull = flat(normed, slice(None)), flat(pulls, slice(None))
    for w, out in enumerate((own, other)):
        columns = slice(2 * w * FF_DEV, 2 * (w + 1) * FF_DEV)
        out[:, : 2 * FF_DEV] = dot_rows(left, flat(grads, columns)).astype(jnp.bfloat16)
        columns = slice(w * FF_DEV, (w + 1) * FF_DEV)
        out[:, 2 * FF_DEV :] = dot_rows(pull, flat(inner, columns)).astype(jnp.bfloat16)


def attend_back_start(info, back_sum, vec, part_out, frames, cotangent, weight, mixed, _, *refs):
    grad_hidden, sums, grad_mixed, term_own, term_other, grad_attend = refs
    core, team = info[3 * TEAM], info[3 * TEAM + 1]
    sums[...] = jnp.zeros_like(sums)

    def rows(chunk):
        grad_normed = back_sum[chunk, :].astype(jnp.float32)
        attended = part_out[chunk, :]
        unit, scaling = norm_parts(frames[chunk, :].astype(jnp.float32) + vec[4:5, :] * attended)
        grad = cotangent[chunk, :].astype(jnp.float32) + norm_back(
            grad_normed, unit, scaling, vec[2:3, :]
        )
        grad_hidden[chunk, :] = grad
        grad_attend[chunk, :] = (grad * vec[4:5, :]).astype(jnp.bfloat16)
        sums[0:1, :] += jnp.sum(grad_normed * unit, axis=0, keepdims=True)
        sums[1:2, :] += jnp.sum(grad_normed, axis=0, keepdims=True)
        sums[2:3, :] += jnp.sum(grad * attended, axis=0, keepdims=True)

    row_chunks(frames.shape[0], 256, rows)
    grads = dot(grad_attend[...], weight[...]).astype(jnp.bfloat16)
    terms = dot_rows(grad_attend[...], mixed[...]).astype(jnp.bfloat16)
    for k in range(TEAM):
        for j in range(CORES):
            s = k * CORES + j
            columns = slice(s * WIDTH_DEV, (s + 1) * WIDTH_DEV)
            grad_mixed[(team ^ k) * CORES + (core ^ j)] = grads[:, columns]
            (term_other if j else term_own)[team ^ k] = terms[:, columns]


def attend_backward(first, info, *refs):
    grad_mixed, frames, normed, rows_in, win, cosines, sines, _ = refs[:8]
    term, sums, keep, send, joint, key_total, value_total, back = refs[8:]
    step = pl.program_id(0)
    core = info[3 * TEAM]
    k = info[3 * TEAM + 1] ^ (first + step)
    tokens = frames.shape[1]
    group = CORES * tokens
    width = WIDTH_DEV
    key_total[...] = jnp.zeros_like(key_total)
    value_total[...] = jnp.zeros_like(value_total)
    blocks = range(group // WINDOW)
    tiles = [(block, head) for block in blocks for head in range(HEADS_DEV)]
    masks = [span_mask(info, k, block, group) for block in blocks]

    def products(block, head):
        low, high = key_span(block, group)
        query = head_lanes(rows_in[0, block * WINDOW : (block + 1) * WINDOW, :width], head)
        half, begin = divmod(block * WINDOW, tokens)
        grad = head_lanes(grad_mixed[half, begin : begin + WINDOW, :], head)
        scores = dot_last(query, rows_in[0, low:high, width : 2 * width])
        return query, grad, scores, dot_last(grad, rows_in[0, low:high, 2 * width :])

    def unrotated(x, rows):
        return (x * cosines[0, rows, :] - half_swap(x) * sines[0, rows, :]).astype(jnp.bfloat16)

    ahead = products(*tiles[0])
    outs = []
    for i, (block, head) in enumerate(tiles):
        query, grad, scores, grad_probability = ahead
        if i + 1 < len(tiles):
            ahead = products(*tiles[i + 1])
        low, high = key_span(block, group)
        probability = softmax_rows(scores, masks[block])
        delta = jnp.sum(probability * grad_probability, axis=-1, keepdims=True)
        grad_scores = (probability * (grad_probability - delta)).astype(jnp.bfloat16)
        outs.append(dot(grad_scores, rows_in[0, low:high, width : 2 * width]))
        key_total[low:high, :] += dot_rows(grad_scores, query)
        value_total[low:high, :] += dot_rows(probability.astype(jnp.bfloat16), grad)
        if head == HEADS_DEV - 1:
            rows = slice(block * WINDOW, (block + 1) * WINDOW)
            joint[rows, :width] = unrotated(pick_heads(outs) * SCORE_SCALE, rows)
            outs = []
    for half in range(CORES):
        rows = slice(half * tokens, (half + 1) * tokens)
        joint[rows, width : 2 * width] = unrotated(key_total[rows, :] * SCORE_SCALE, rows)
        joint[rows, 2 * width :] = value_total[rows, :].astype(jnp.bfloat16)

    @pl.when(step == 0)
    def _():
        term[...] = jnp.zeros_like(term)
        sums[...] = jnp.zeros_like(sums)

    both = jnp.concatenate([normed[half] for half in range(CORES)], axis=0)
    term[...] += dot_rows(both, joint[...])
    back[...] = dot_last(joint[...], win[...])
    for half in range(CORES):

        def rows(chunk, half=half):
            part = back[pl.ds(chunk.start + half * tokens, chunk.size), :]
            unit, _ = norm_parts(frames[half, chunk, :].astype(jnp.float32))
            sums[0:1, :] += jnp.sum(part * unit, axis=0, keepdims=True)
            sums[1:2, :] += jnp.sum(part, axis=0, keepdims=True)

        row_chunks(tokens, 256, rows)
    keep[0] = back[pl.ds(pl.multiple_of(core * tokens, tokens), tokens), :]
    send[0] = back[pl.ds(pl.multiple_of((1 - core) * tokens, tokens), tokens), :].astype(jnp.bfloat16)


def join_terms(term, parts, *refs):
    out = refs[-1]

    def rows(chunk):
        for part in range(3):
            columns = slice(part * WIDTH_DEV, (part + 1) * WIDTH_DEV)
            out[part, chunk, :] = term[chunk, columns].astype(jnp.bfloat16)
        total = parts[0, chunk, :].astype(jnp.float32)
        for p in range(1, TEAM):
            total = total + parts[p, chunk, :].astype(jnp.float32)
        out[3, chunk, :] = total.astype(jnp.bfloat16)

    row_chunks(D, 128, rows)


def own_sums(last, late, _, grad_in, grad_out, grad_expand, grad_contract, grad_gains, squares):
    rows = grad_in.shape[0]
    devices = last.shape[0]
    total = jnp.zeros((rows, 128), jnp.float32)
    for p in range(SLOTS):
        for part in range(4):
            band = slice(part * rows, (part + 1) * rows)
            value = last[p, band, :].astype(jnp.float32)
            for r in range(1, devices // SLOTS):
                value = value + last[r * SLOTS + p, band, :].astype(jnp.float32)
            total = total + value * value
            begin = p * WIDTH_DEV
            if part < 3:
                grad_in[:, part * D + begin : part * D + begin + WIDTH_DEV] = value
            else:
                grad_out[:, begin : begin + WIDTH_DEV] = value
        for f in range(3 * FF_DEV // 128):
            value = late[p, :, f * 128 : (f + 1) * 128].astype(jnp.float32)
            total = total + value * value
            which, begin = divmod(f * 128, FF_DEV)
            begin += p * FF_DEV
            if which < 2:
                grad_expand[:, which * FF + begin : which * FF + begin + 128] = value
            else:
                grad_contract[:, begin : begin + 128] = value
    value = last[0, 4 * rows : 4 * rows + 16, :].astype(jnp.float32)
    for d in range(1, devices):
        value = value + last[d, 4 * rows : 4 * rows + 16, :].astype(jnp.float32)
    value = value[:8]
    grad_gains[...] = value
    whole = jnp.sum(total) + jnp.sum(value * value)
    squares[...] = jnp.full(squares.shape, whole, jnp.float32)


def adam_all(rates, squares_in, *refs):
    grads, weights, means, squares = refs[:4], refs[4:8], refs[8:12], refs[12:16]
    gain_grads, gains, gain_means, gain_squares = refs[16:20]
    norm_out = refs[21]
    outs, gain_outs = refs[22:38], refs[38:]
    norm = jnp.sqrt(jnp.sum(squares_in[:, 0:1, 0:1]))
    factor = CLIP_NORM / jnp.maximum(norm, CLIP_NORM)
    norm_out[0, 0] = norm

    def update(weight, mean, square, grad, rate, new):
        mean_new, square_new, moved = adam_step(weight, mean, square, grad, factor, rate)
        new[0][...] = mean_new
        new[1][...] = square_new
        new[2][...] = moved
        new[3][...] = moved.astype(jnp.bfloat16)

    for i in range(4):
        update(
            weights[i][...], means[i][...], squares[i][...], grads[i][...], rates[i], outs[i::4]
        )
    count, width = gains.shape
    update(
        gains[...],
        gain_means[...],
        gain_squares[...],
        gain_grads[:count, :width],
        VECTOR_RATE,
        gain_outs,
    )


def frames_back(*refs):
    pieces = refs[: TEAM + 1]
    frames, grad_hidden, vec, out = refs[TEAM + 1 :]
    unit, scaling = norm_parts(frames[...].astype(jnp.float32))
    grad_normed = pieces[0][...]
    for piece in pieces[1:]:
        grad_normed = grad_normed + piece[...].astype(jnp.float32)
    out[...] = grad_hidden[...] + norm_back(grad_normed, unit, scaling, vec[0:1, :])


def frames_out(branch, frames, part_out, vec, _, out):
    hidden = frames[...].astype(jnp.float32) + vec[4:5, :] * part_out[...]
    out[...] = (hidden + vec[5:6, :] * branch[...].astype(jnp.float32)).astype(jnp.bfloat16)


def per_device(
    frames,
    clip_lengths,
    cotangent,
    attend_in,
    attend_out,
    expand,
    contract,
    gains,
    prior_mean_attend_in,
    prior_mean_attend_out,
    prior_mean_expand,
    prior_mean_contract,
    prior_mean_gains,
    prior_square_attend_in,
    prior_square_attend_out,
    prior_square_expand,
    prior_square_contract,
    prior_square_gains,
):
    bf16 = jnp.bfloat16
    f32 = jnp.float32
    tokens = frames.shape[0]
    group = tokens * CORES
    rows = attend_in.shape[0]
    gain_width = gains.shape[1]
    reps = lax.axis_size("rep")
    devices = reps * SLOTS
    rep = lax.axis_index("rep")
    team = lax.axis_index("team")
    core = lax.axis_index("tm")

    frames_team = lax.all_gather(frames, MEMBERS, axis=0, tiled=False)

    tail_rows = 16
    lanes = 128
    parts = attend_in.astype(bf16).reshape(rows, 3, SLOTS, WIDTH_DEV).transpose(2, 1, 0, 3)
    parts = jnp.concatenate(
        [parts, attend_out.astype(bf16).reshape(rows, 1, SLOTS, WIDTH_DEV).transpose(2, 1, 0, 3)],
        axis=1,
    ).reshape(SLOTS, 4 * rows, lanes)
    small = jnp.zeros((tail_rows, lanes), f32)
    small = small.at[:6, :gain_width].set(gains)
    small = small.at[6, :3].set((clip_lengths[0] // 16).astype(f32))
    small = small.at[7, :3].set((clip_lengths[0] % 16).astype(f32))
    small = jnp.broadcast_to(small.astype(bf16)[None], (SLOTS, tail_rows, lanes))
    parts = jnp.concatenate([parts, small], axis=1)
    parts = jnp.broadcast_to(parts[None], (reps,) + parts.shape)
    spread = lax.all_to_all(
        parts.reshape(devices, 4 * rows + tail_rows, lanes), ALL, 0, 0, tiled=True
    )
    part_in = spread[:, : 3 * rows].reshape(devices, 3, rows, lanes).transpose(0, 2, 1, 3)
    part_in = part_in.reshape(D, 3 * WIDTH_DEV)
    part_out = spread[:, 3 * rows : 4 * rows].reshape(D, WIDTH_DEV)
    small = spread[:, 4 * rows : 4 * rows + 8].astype(f32)
    vectors = small[:, :6, :gain_width].transpose(1, 0, 2).reshape(6, D)
    vectors = jnp.pad(vectors, ((0, 2), (0, 0)))
    lengths = lax.dynamic_index_in_dim(
        small[:, 6:, :3].reshape(reps, TEAM, CORES, 2, 3)[:, :, 0], rep, 0, keepdims=False
    )
    lengths = (lengths[:, 0] * 16 + lengths[:, 1]).astype(jnp.int32)
    info = jnp.concatenate([lengths.reshape(-1), jnp.stack([core, team])])

    mlp_pack = jnp.concatenate(
        [
            expand.astype(bf16).reshape(rows, 2, SLOTS, FF_DEV).transpose(2, 0, 1, 3).reshape(
                SLOTS, rows, 2 * FF_DEV
            ),
            contract.astype(bf16).reshape(rows, SLOTS, FF_DEV).transpose(1, 0, 2),
        ],
        axis=2,
    )
    mlp_cols = exchange_team(after(mlp_pack, spread)).reshape(SLOTS * rows, 3 * FF_DEV)
    outs_team = gather_team(part_out)
    cots = [cotangent] + send_mates([after(cotangent, mlp_cols)] * (TEAM - 1))

    places = jnp.arange(group, dtype=jnp.int32)
    ends = jnp.cumsum(lengths, axis=1)
    starts = ends - lengths
    begin = jnp.max(
        jnp.where(starts[:, None, :] <= places[None, :, None], starts[:, None, :], 0), axis=2
    )
    offsets = (places[None] - begin).astype(f32)
    freqs = np.power(10000.0, -2.0 * np.arange(HEAD // 2) / HEAD)
    lane_freqs = jnp.asarray(np.tile(freqs, WIDTH_DEV // (HEAD // 2)), dtype=f32)
    angles = offsets[:, :, None] * lane_freqs
    signs = jnp.asarray(np.where(np.arange(WIDTH_DEV) % HEAD < HEAD // 2, -1.0, 1.0), dtype=f32)
    cosines = jnp.cos(angles)
    sines = jnp.sin(angles) * signs
    mlp_weight = lax.all_gather(
        after(mlp_cols, sines, frames_team), ("rep", "tm"), axis=0, tiled=False
    ).reshape(reps, CORES, SLOTS * rows, 3 * FF_DEV)

    by_frames = (CORES, tokens, D)
    by_heads = (CORES, tokens, WIDTH_DEV)
    by_rows = (1, group, 3 * WIDTH_DEV)
    by_angles = (1, group, WIDTH_DEV)
    normed_one, attend_rows, mixed = call_groups(
        attend_forward,
        info,
        [
            (in_hbm(frames_team), by_frames),
            (vectors, None),
            (part_in, None),
            (in_hbm(cosines), by_angles),
            (in_hbm(sines), by_angles),
        ],
        [
            ((SLOTS, tokens, D), bf16, by_frames, HBM_OUT),
            ((TEAM, group, 3 * WIDTH_DEV), bf16, by_rows, HBM_OUT),
            ((SLOTS, tokens, WIDTH_DEV), bf16, by_heads, HBM_OUT),
        ],
        name="attend_forward",
        micros=24,
    )

    mixed_own = exchange_team(mixed)
    attend_part, normed_two, full_out, mixed_flat = call_kernel(
        attend_finish,
        [info, mixed_own, *outs_team, frames, vectors] + [x[:16, :128] for x in cots[1:]],
        [
            ((tokens, D), f32, HBM_OUT),
            ((TEAM, tokens, D), bf16),
            ((D, D), bf16, HBM_OUT),
            ((tokens, D), bf16, HBM_OUT),
        ],
        specs=[SMEM_SPEC] + [VMEM_SPEC] * (SLOTS + 3) + [ANY_SPEC] * (TEAM - 1),
        far=(10,),
        name="attend_finish",
        micros=4,
    )

    normed_team = lax.all_to_all(normed_two, "team", 0, 0, tiled=True)
    by_pairs = (TEAM // 2, tokens, D)
    inner, grads_up, pulls, back = call_groups(
        feed_forward,
        info,
        [
            (normed_team, by_pairs),
            (vectors, None),
            (in_hbm(mlp_weight), "far"),
            *[(in_hbm(x), "far") for x in cots],
        ],
        [
            ((TEAM, tokens, 2 * FF_DEV), bf16, (TEAM // 2, tokens, 2 * FF_DEV), HBM_OUT),
            ((TEAM, tokens, 4 * FF_DEV), bf16, (TEAM // 2, tokens, 4 * FF_DEV), HBM_OUT),
            ((TEAM, tokens, D), bf16, by_pairs, HBM_OUT),
            ((TEAM, tokens, D), bf16, by_pairs, HBM_OUT),
        ],
        scratch=[
            pltpu.VMEM(mlp_weight.shape, bf16),
            pltpu.SemaphoreType.DMA((CORES, mlp_weight.shape[0])),
            pltpu.VMEM((TEAM, tokens, D), bf16),
            pltpu.SemaphoreType.DMA((TEAM,)),
        ],
        steps=2,
        vmem=26,
        name="feed_forward",
        micros=20,
    )
    back_sum = lax.psum_scatter(back, "team", scatter_dimension=0, tiled=False)
    term_own, term_other = call_terms(normed_team, grads_up, pulls, inner)
    term_got = other_core(term_other)
    branch_parts, sums_out = call_kernel(
        feed_branch,
        [info, inner, mlp_weight, term_own[:16, :128], *cots],
        [((TEAM, tokens, D), bf16, HBM_OUT), ((8, D), f32)],
        specs=[SMEM_SPEC] + [VMEM_SPEC] * 2 + [ANY_SPEC] + [VMEM_SPEC] * TEAM,
        far=(1, 4, 5, 6, 7),
        name="feed_branch",
        micros=9,
    )
    branch_sum = lax.psum_scatter(branch_parts, "team", scatter_dimension=0, tiled=False)
    term_got = after(term_got, sums_out)
    term_mlp = (term_own.astype(f32) + term_got.astype(f32)).astype(bf16)
    mlp_sum = lax.psum_scatter(term_mlp, "rep", scatter_dimension=0, tiled=True)

    loads = [attend_part, frames, cotangent, full_out, mixed_flat]
    grad_hidden, sums_two, grad_mixed, term_own, term_other = call_kernel(
        attend_back_start,
        [info, back_sum, vectors, *loads, sums_out],
        [
            ((tokens, D), f32, HBM_OUT),
            ((8, D), f32),
            ((SLOTS, tokens, WIDTH_DEV), bf16),
            ((TEAM, D, WIDTH_DEV), bf16),
            ((TEAM, D, WIDTH_DEV), bf16),
        ],
        scratch=[pltpu.VMEM((tokens, D), bf16)],
        specs=[SMEM_SPEC] + [VMEM_SPEC] * (len(loads) + 2) + [ANY_SPEC],
        far=(1, 3, 4, 5, 6, 7),
        vmem=24,
        name="attend_back_start",
        micros=6,
    )
    grad_mixed = exchange_team(grad_mixed)
    out_sum = (term_own.astype(f32) + other_core(term_other).astype(f32)).astype(bf16)
    out_sum = after(out_sum, grad_mixed[0, :16])
    out_parts = lax.all_to_all(out_sum, "team", 0, 0, tiled=True)
    term_in, sums_one, one_keep, one_send = call_groups(
        attend_backward,
        info,
        [
            (grad_mixed, by_heads),
            (in_hbm(frames_team), by_frames),
            (in_hbm(normed_one), by_frames),
            (in_hbm(attend_rows), by_rows),
            (part_in, None),
            (in_hbm(cosines), by_angles),
            (in_hbm(sines), by_angles),
            (after(vectors, out_sum[0, :16]), None),
        ],
        [
            ((D, 3 * WIDTH_DEV), f32, None, PLAIN),
            ((8, D), f32, None, PLAIN),
            ((TEAM, tokens, D), f32, (1, tokens, D), HBM_OUT),
            ((TEAM, tokens, D), bf16, (1, tokens, D), HBM_OUT),
        ],
        scratch=[
            pltpu.VMEM((group, 3 * WIDTH_DEV), bf16),
            pltpu.VMEM((group, WIDTH_DEV), f32),
            pltpu.VMEM((group, WIDTH_DEV), f32),
            pltpu.VMEM((group, D), f32),
        ],
        mates=(0, TEAM),
        name="attend_backward",
        micros=25,
    )
    one_got = other_core(one_send)
    keeps, gots = list(one_keep), list(one_got)
    one_chips = chip_sums(keeps, gots)
    one_pieces = [keeps[0], gots[0]] + send_mates(one_chips)

    (terms,) = call_kernel(
        join_terms,
        [term_in, out_parts],
        [((4, D, WIDTH_DEV), bf16)],
        name="join_terms",
        micros=2,
    )
    term_gains = jnp.concatenate([sums_one[:2], sums_two[:3], sums_out[:1]])
    gains_block = jnp.zeros((devices, tail_rows, lanes), bf16)
    gains_block = gains_block.at[:, :6, :gain_width].set(
        term_gains.astype(bf16).reshape(6, devices, gain_width).transpose(1, 0, 2)
    )
    terms = terms.reshape(4, devices, rows, lanes).transpose(1, 0, 2, 3)
    last = lax.all_to_all(
        jnp.concatenate([terms.reshape(devices, 4 * rows, lanes), gains_block], axis=1),
        ALL,
        0,
        0,
        tiled=True,
    )
    late = exchange_team(after(mlp_sum.reshape(SLOTS, rows, 3 * FF_DEV), last[0, :16]))
    shapes = [(rows, 3 * D), (rows, D), (rows, 2 * FF), (rows, FF), (8, lanes)]
    if rows % 16 == 0:
        *owned, squares_out = call_kernel(
            own_sums,
            [last, late, one_chips[0][:16, :128]],
            [(shape, f32) for shape in shapes] + [((devices, 8, lanes), f32)],
            vmem=16,
            name="own_sums",
            micros=4,
        )
    else:
        last_sum = jnp.sum(
            last[:, : 4 * rows].reshape(reps, SLOTS, 4, rows, lanes).astype(f32), axis=0
        )
        late = late.astype(f32)
        owned = [
            last_sum[:, :3].transpose(2, 1, 0, 3).reshape(rows, 3 * D),
            last_sum[:, 3].transpose(1, 0, 2).reshape(rows, D),
            late[:, :, : 2 * FF_DEV]
            .reshape(SLOTS, rows, 2, FF_DEV)
            .transpose(1, 2, 0, 3)
            .reshape(rows, 2 * FF),
            late[:, :, 2 * FF_DEV :].transpose(1, 0, 2).reshape(rows, FF),
            jnp.sum(last[:, 4 * rows : 4 * rows + 8].astype(f32), axis=0),
        ]
        square_part = jnp.zeros((), f32)
        for grad in owned:
            square_part = square_part + jnp.sum(grad * grad)
        squares_out = jnp.full((devices, 8, lanes), square_part)
    squares_in = lax.all_to_all(squares_out, ALL, 0, 0, tiled=True)

    (frames_grad,) = call_kernel(
        frames_back,
        [*one_pieces, frames, grad_hidden, vectors],
        [((tokens, D), f32)],
        far=(5, 6),
        name="frames_back",
        micros=4,
    )

    weights = [attend_in, attend_out, expand, contract]
    means = [prior_mean_attend_in, prior_mean_attend_out, prior_mean_expand, prior_mean_contract]
    squares = [
        prior_square_attend_in,
        prior_square_attend_out,
        prior_square_expand,
        prior_square_contract,
    ]
    rates = (RATE / math.sqrt(D), RATE / math.sqrt(D // 64), RATE / math.sqrt(D), RATE / math.sqrt(FF))
    steps = 4
    columns = [pl.BlockSpec((rows, x.shape[1] // steps), lambda i: (0, i)) for x in weights]
    whole = pl.BlockSpec(gains.shape, lambda i: (0, 0))
    out = pl.pallas_call(
        functools.partial(adam_all, rates),
        grid=(steps,),
        in_specs=[pl.BlockSpec(squares_in.shape, lambda i: (0, 0, 0))]
        + columns * 4
        + [pl.BlockSpec((8, lanes), lambda i: (0, 0))]
        + [whole] * 3
        + [ANY_SPEC],
        out_specs=[pl.BlockSpec(memory_space=pltpu.SMEM)] + columns * 4 + [whole] * 4,
        out_shape=[jax.ShapeDtypeStruct((1, 1), f32)]
        + [
            jax.ShapeDtypeStruct(x.shape, dtype) for dtype in (f32, f32, f32, bf16) for x in weights
        ]
        + [jax.ShapeDtypeStruct(gains.shape, dtype) for dtype in (f32, f32, f32, bf16)],
        compiler_params=pltpu.CompilerParams(vmem_limit_bytes=24 * MIB),
        cost_estimate=cost(8),
        name="adam_all",
    )(
        squares_in,
        *[in_hbm(x) for x in (*owned[:4], *weights, *means, *squares)],
        owned[4],
        gains,
        prior_mean_gains,
        prior_square_gains,
        frames_grad[:8, :128],
    )
    (out_frames,) = call_kernel(
        frames_out,
        [branch_sum, frames, attend_part, vectors, out[-2]],
        [((tokens, D), bf16)],
        specs=[VMEM_SPEC] * 4 + [ANY_SPEC],
        far=(0, 1, 2),
        name="frames_out",
        micros=3,
    )

    news = [out[1 + kind * 4 + which] for which in range(4) for kind in range(4)]
    return (out_frames, frames_grad, out[0][0, 0], *news, *out[17:])


def solution(mesh):
    teams = Mesh(
        mesh.devices.reshape(mesh.shape["dp"] // TEAM, TEAM, mesh.shape["tm"]), ALL
    )
    by_row = P(ALL, None)
    by_column = P(None, ALL)
    per_group = P(("rep", "team"), None)
    weights = (by_row, by_row, by_row, by_row, by_column)
    return jax.shard_map(
        per_device,
        mesh=teams,
        in_specs=(by_row, per_group, by_row) + weights * 3,
        out_specs=(by_row, by_row, P()) + (by_row,) * 16 + (by_column,) * 4,
        check_vma=False,
    )
```

```python
import functools
import math

import jax
import jax.numpy as jnp
import numpy as np
from jax import lax
from jax.experimental import pallas as pl
from jax.experimental.pallas import tpu as pltpu
from jax.sharding import Mesh
from jax.sharding import PartitionSpec as P

D = 1024
HEADS = 16
HEAD = 64
FF = 4096
WINDOW = 128
STEP = 10

EPS_NORM = 1e-05
NEG_FILL = -1e30
SCORE_SCALE = 0.125
BETA_ONE = 0.9
BETA_TWO = 0.999
ADAM_EPS = 1e-08
DECAY = 0.1
RATE = 3.0
VECTOR_RATE = 0.6
CLIP_NORM = 1.0

TEAM = 4
CORES = 2
SLOTS = TEAM * CORES
ALL = ("rep", "team", "tm")
MEMBERS = ("team", "tm")
ANY_SPEC = pl.BlockSpec(memory_space=pl.ANY)
SMEM_SPEC = pl.BlockSpec(memory_space=pltpu.SMEM)
VMEM_SPEC = pl.BlockSpec(memory_space=pltpu.VMEM)
MIB = 1 << 20
PLAIN, HBM_OUT = range(2)
HBM_SPEC = pl.BlockSpec(memory_space=pltpu.HBM)
LOG2_E = math.log2(math.e)
HEADS_DEV = HEADS // SLOTS
WIDTH_DEV = HEADS_DEV * HEAD
FF_DEV = FF // SLOTS


def swap_pairs(count, bit):
    return [(a, a ^ bit) for a in range(count)]


def other_core(x):
    return lax.ppermute(x, "tm", swap_pairs(CORES, 1))


def to_mate(x, bit):
    return lax.ppermute(x, "team", swap_pairs(TEAM, bit))


def gather_team(x):
    blocks = [x] + [to_mate(x, k) for k in range(1, TEAM)]
    parts = []
    for block in blocks:
        parts += [block, other_core(block)]
    return parts


def chip_sums(keep, got):
    return [
        (keep[k] + got[k].astype(jnp.float32)).astype(jnp.bfloat16) for k in range(1, TEAM)
    ]


def send_mates(chips):
    return [to_mate(chip, k + 1) for k, chip in enumerate(chips)]


def exchange_team(x):
    return lax.all_to_all(x, MEMBERS, 0, 0, tiled=True)


def after(x, *tokens):
    return pl.pallas_call(
        lambda *refs: None,
        out_shape=jax.ShapeDtypeStruct(x.shape, x.dtype),
        in_specs=[ANY_SPEC] * (1 + len(tokens)),
        out_specs=ANY_SPEC,
        input_output_aliases={0: 0},
        name="after",
    )(x, *tokens)


def norm_parts(values):
    centered = values - jnp.mean(values, axis=-1, keepdims=True)
    scaling = lax.rsqrt(jnp.mean(centered * centered, axis=-1, keepdims=True) + EPS_NORM)
    return (centered * scaling, scaling)


def norm_back(gradient, unit_rows, scaling, gain_row):
    scaled = gradient * gain_row
    return scaling * (
        scaled
        - jnp.mean(scaled, axis=-1, keepdims=True)
        - unit_rows * jnp.mean(scaled * unit_rows, axis=-1, keepdims=True)
    )


def dot_rows(left_side, right_side):
    return lax.dot_general(
        left_side, right_side, (((0,), (0,)), ((), ())), preferred_element_type=jnp.float32
    )


def dot_last(left_side, right_side):
    return lax.dot_general(
        left_side, right_side, (((1,), (1,)), ((), ())), preferred_element_type=jnp.float32
    )


def dot(left_side, right_side):
    return jnp.dot(left_side, right_side, preferred_element_type=jnp.float32)


def adam_step(weight, mean_old, square_old, gradient, factor, step_rate):
    clipped = gradient * factor
    mean_new = BETA_ONE * mean_old + (1.0 - BETA_ONE) * clipped
    square_new = BETA_TWO * square_old + (1.0 - BETA_TWO) * clipped * clipped
    mean_hat = mean_new / (1.0 - BETA_ONE**STEP)
    square_hat = square_new / (1.0 - BETA_TWO**STEP)
    moved = weight - step_rate * (mean_hat / (jnp.sqrt(square_hat) + ADAM_EPS) + DECAY * weight)
    return (mean_new, square_new, moved)


def in_hbm(x):
    return pltpu.with_memory_space_constraint(x, pltpu.HBM)


def cost(micros):
    return pl.CostEstimate(flops=int(micros * 1e9), transcendentals=0, bytes_accessed=int(micros * 1e6))


def call_kernel(
    kernel, ins, outs, scratch=(), specs=None, far=(), vmem=16, name=None, micros=2
):
    specs = list(specs or [VMEM_SPEC] * len(ins))
    ins = list(ins)
    buffers = [pltpu.VMEM(ins[i].shape, ins[i].dtype) for i in far]
    for i in far:
        specs[i] = HBM_SPEC
        ins[i] = in_hbm(ins[i])

    def loaded(*refs):
        refs = list(refs)
        if far:
            near, sems = refs[-1 - len(far) : -1], refs[-1]
            refs = refs[: -1 - len(far)]
            copies = [
                pltpu.make_async_copy(refs[i], b, sems.at[n]) for n, (i, b) in enumerate(zip(far, near))
            ]
            for copy in copies:
                copy.start()
            for copy in copies:
                copy.wait()
            for i, b in zip(far, near):
                refs[i] = b
        kernel(*refs)

    return pl.pallas_call(
        loaded,
        out_shape=[
            (pltpu.HBM if mode else jax.ShapeDtypeStruct)(shape, dtype) for shape, dtype, *mode in outs
        ],
        in_specs=specs,
        out_specs=[VMEM_SPEC] * len(outs),
        scratch_shapes=[
            *scratch,
            *buffers,
            *([pltpu.SemaphoreType.DMA((len(far),))] if far else []),
        ],
        compiler_params=pltpu.CompilerParams(vmem_limit_bytes=vmem * MIB),
        cost_estimate=cost(micros),
        name=name,
    )(*ins)


def call_terms(normed, grads, pulls, inner):
    count, tokens, _ = normed.shape
    step = 256
    by_rows = pl.BlockSpec((count, tokens, step), lambda r: (0, 0, r))

    def whole(x):
        return pl.BlockSpec(x.shape, lambda r: (0, 0, 0), pipeline_mode=pl.Buffered(1))

    return pl.pallas_call(
        feed_terms,
        grid=(D // step,),
        in_specs=[by_rows, whole(grads), by_rows, whole(inner)],
        out_specs=[pl.BlockSpec((step, 3 * FF_DEV), lambda r: (r, 0))] * 2,
        out_shape=[
            pltpu.HBM((D, 3 * FF_DEV), jnp.bfloat16),
            jax.ShapeDtypeStruct((D, 3 * FF_DEV), jnp.bfloat16),
        ],
        compiler_params=pltpu.CompilerParams(vmem_limit_bytes=24 * MIB),
        cost_estimate=cost(8),
        name="feed_terms",
    )(in_hbm(normed), in_hbm(grads), in_hbm(pulls), in_hbm(inner))


def call_groups(
    kernel, info, ins, outs, scratch=(), vmem=24, name=None, micros=20, mates=None, steps=TEAM
):
    def spec(shape, block, out):
        rest = (0,) * (len(shape) - 1)
        if block == "far":
            return HBM_SPEC
        if block is None:
            return pl.BlockSpec(
                shape, lambda g, info: (0, *rest), pipeline_mode=None if out else pl.Buffered(1)
            )
        if mates and not out:
            return pl.BlockSpec(block, lambda g, info: (info[3 * TEAM + 1] ^ (mates[0] + g), *rest))
        return pl.BlockSpec(block, lambda g, info: (g, *rest))

    return pl.pallas_call(
        functools.partial(kernel, mates[0] if mates else 0),
        grid_spec=pltpu.PrefetchScalarGridSpec(
            num_scalar_prefetch=1,
            grid=(mates[1] if mates else steps,),
            in_specs=[spec(x.shape, block, False) for x, block in ins],
            out_specs=[spec(shape, block, True) for shape, _, block, _ in outs],
            scratch_shapes=list(scratch),
        ),
        out_shape=[
            jax.ShapeDtypeStruct(shape, dtype) if mode == PLAIN else pltpu.HBM(shape, dtype)
            for shape, dtype, _, mode in outs
        ],
        compiler_params=pltpu.CompilerParams(vmem_limit_bytes=vmem * MIB),
        cost_estimate=cost(micros),
        name=name,
    )(info, *[x for x, _ in ins])


def row_chunks(count, size, body):
    def step(i, carry):
        body(pl.ds(pl.multiple_of(i * size, size), size))
        return carry

    lax.fori_loop(0, count // size, step, 0)


def lanes_of(x):
    return lax.broadcasted_iota(jnp.int32, (1, x.shape[-1]), 1)


def half_swap(x):
    width = x.shape[-1]
    half = HEAD // 2
    first = (lanes_of(x) & half) == 0
    return jnp.where(first, pltpu.roll(x, width - half, x.ndim - 1), pltpu.roll(x, half, x.ndim - 1))


def key_span(block, group):
    return max(0, (block - 1) * WINDOW), min(group, (block + 2) * WINDOW)


def span_mask(info, slot, block, group):
    low, high = key_span(block, group)
    first = info[3 * slot]
    second = first + info[3 * slot + 1]
    third = second + info[3 * slot + 2]
    place = block * WINDOW + lax.broadcasted_iota(jnp.int32, (WINDOW, 1), 0)
    start = jnp.where(
        place >= third,
        third,
        jnp.where(place >= second, second, jnp.where(place >= first, first, 0)),
    )
    end = jnp.where(
        place < first, first, jnp.where(place < second, second, jnp.where(place < third, third, group))
    )
    least = jnp.maximum(start, place - WINDOW)
    most = jnp.minimum(end, place + WINDOW + 1)
    key_place = low + lax.broadcasted_iota(jnp.int32, (1, high - low), 1)
    return (key_place >= least) & (key_place < most)


def head_lanes(x, head):
    lane = lanes_of(x)
    inside = (lane >= head * HEAD) & (lane < (head + 1) * HEAD)
    return jnp.where(inside, x, jnp.zeros_like(x))


def pick_heads(parts):
    out = parts[0]
    for head in range(1, len(parts)):
        out = jnp.where(lanes_of(out) >= head * HEAD, parts[head], out)
    return out


def softmax_rows(products, allowed):
    scores = jnp.where(allowed, products * (SCORE_SCALE * LOG2_E), NEG_FILL)
    exponent = jnp.exp2(scores - jnp.max(scores, axis=-1, keepdims=True))
    return exponent * (1.0 / jnp.sum(exponent, axis=-1, keepdims=True))


def attend_forward(_, info, frames, vec, win, cosines, sines, normed, rows_out, mixed, stats):
    k = pl.program_id(0)
    tokens = frames.shape[1]
    group = CORES * tokens
    width = WIDTH_DEV
    for half in range(CORES):
        rows = slice(half * tokens, (half + 1) * tokens)

        def norm_rows(chunk, half=half):
            values = frames[half, chunk, :].astype(jnp.float32)
            mean = jnp.mean(values, axis=-1, keepdims=True)
            unit, scaling = norm_parts(values)
            stats[half, chunk, :] = jnp.where(lanes_of(stats) == 0, mean, scaling)
            normed[half, chunk, :] = (unit * vec[0:1, :] + vec[1:2, :]).astype(jnp.bfloat16)

        row_chunks(tokens, 256, norm_rows)
        joint = dot(normed[half], win[...])
        for part in range(2):
            x = joint[:, part * width : (part + 1) * width]
            rows_out[0, rows, part * width : (part + 1) * width] = (
                x * cosines[0, rows, :] + half_swap(x) * sines[0, rows, :]
            ).astype(jnp.bfloat16)
        rows_out[0, rows, 2 * width :] = joint[:, 2 * width :].astype(jnp.bfloat16)

    blocks = range(group // WINDOW)
    tiles = [(block, head) for block in blocks for head in range(HEADS_DEV)]
    masks = [span_mask(info, k, block, group) for block in blocks]

    def product(block, head):
        low, high = key_span(block, group)
        query = head_lanes(rows_out[0, block * WINDOW : (block + 1) * WINDOW, :width], head)
        return dot_last(query, rows_out[0, low:high, width : 2 * width])

    ahead = product(*tiles[0])
    outs = []
    for i, (block, head) in enumerate(tiles):
        now = ahead
        if i + 1 < len(tiles):
            ahead = product(*tiles[i + 1])
        low, high = key_span(block, group)
        probability = softmax_rows(now, masks[block]).astype(jnp.bfloat16)
        outs.append(dot(probability, rows_out[0, low:high, 2 * width :]))
        if head == HEADS_DEV - 1:
            half, begin = divmod(block * WINDOW, tokens)
            mixed[half, begin : begin + WINDOW, :] = pick_heads(outs).astype(jnp.bfloat16)
            outs = []


def attend_finish(info, mixed, *refs):
    outs = refs[:SLOTS]
    frames, vec = refs[SLOTS : SLOTS + 2]
    part_out, normed, weight, mixed_out = refs[-4:]
    core, team = info[3 * TEAM], info[3 * TEAM + 1]
    for k in range(TEAM):
        for j in range(CORES):
            s = k * CORES + j
            columns = slice(s * WIDTH_DEV, (s + 1) * WIDTH_DEV)
            weight[:, columns] = outs[s][...]
            mixed_out[:, columns] = mixed[(team ^ k) * CORES + (core ^ j)]
    part_out[...] = dot_last(mixed_out[...], weight[...])

    def rows(chunk):
        hidden = frames[chunk, :].astype(jnp.float32) + vec[4:5, :] * part_out[chunk, :]
        unit, _ = norm_parts(hidden)
        low = (unit * vec[2:3, :] + vec[3:4, :]).astype(jnp.bfloat16)
        for k in range(TEAM):
            normed[k, chunk, :] = low

    row_chunks(frames.shape[0], 256, rows)


def half_weight(weight, core, columns):
    return jnp.concatenate([weight[r, core, :, columns] for r in range(weight.shape[0])], axis=0)


def feed_forward(_, info, normed, vec, far_weight, *refs):
    far_cots = refs[:TEAM]
    inner, grads, pulls, back, weight, sems, cots, cot_sems = refs[TEAM:]
    count, tokens, _ = normed.shape
    half = FF_DEV // 2
    core = info[3 * TEAM]

    def flat(ref):
        return jnp.concatenate([ref[g] for g in range(count)], axis=0)

    def spread(ref, columns, value):
        low = value.astype(jnp.bfloat16)
        for g in range(count):
            ref[g, :, columns] = low[g * tokens : (g + 1) * tokens]

    first = pl.program_id(0) == 0
    copies = [
        [
            pltpu.make_async_copy(far_weight.at[r, core ^ w], weight.at[r, core ^ w], sems.at[w, r])
            for r in range(weight.shape[0])
        ]
        for w in range(CORES)
    ]

    cot_copies = [
        pltpu.make_async_copy(cot, cots.at[info[3 * TEAM + 1] ^ k], cot_sems.at[k])
        for k, cot in enumerate(far_cots)
    ]

    @pl.when(first)
    def _():
        for copy in copies[0] + cot_copies + copies[1]:
            copy.start()

    for w in range(CORES):

        @pl.when(first)
        def _(w=w):
            for copy in copies[w]:
                copy.wait()

        for f in range(2):
            begin = f * half
            gate_cols = slice(begin, begin + half)
            up_cols = slice(FF_DEV + begin, FF_DEV + begin + half)
            out_cols = slice(2 * FF_DEV + begin, 2 * FF_DEV + begin + half)
            gate = dot(flat(normed), half_weight(weight, core ^ w, gate_cols))
            up = dot(flat(normed), half_weight(weight, core ^ w, up_cols))
            if w == f == 0:

                @pl.when(first)
                def _():
                    for copy in cot_copies:
                        copy.wait()

                for g in range(count):
                    cot = cots[count * pl.program_id(0) + g].astype(jnp.float32)
                    pulls[g] = (cot * vec[5:6, :]).astype(jnp.bfloat16)
            grad_inner = dot(flat(pulls), half_weight(weight, core ^ w, out_cols))
            sigmoid = jax.nn.sigmoid(gate)
            silu = gate * sigmoid
            inner_cols = slice(w * FF_DEV + begin, w * FF_DEV + begin + half)
            spread(inner, inner_cols, silu * up)
            slope = grad_inner * up * sigmoid * (1.0 + gate * (1.0 - sigmoid))
            shift = 2 * w * FF_DEV
            spread(grads, slice(shift + begin, shift + begin + half), slope)
            begin += shift + FF_DEV
            spread(grads, slice(begin, begin + half), grad_inner * silu)
    both = jnp.concatenate(
        [half_weight(weight, core ^ w, slice(0, 2 * FF_DEV)) for w in range(CORES)], axis=1
    )
    total = dot_last(flat(grads), both)
    spread(back, slice(None), total)


def feed_branch(info, inner, weight, _, *refs):
    cots, (parts, sums) = refs[:TEAM], refs[TEAM:]
    core, team = info[3 * TEAM], info[3 * TEAM + 1]
    sums[...] = jnp.zeros_like(sums)
    columns = slice(2 * FF_DEV, 3 * FF_DEV)
    both = jnp.concatenate(
        [half_weight(weight, core ^ w, columns) for w in range(CORES)], axis=1
    )
    for k, cot in enumerate(cots):
        part = dot_last(inner[team ^ k], both)
        sums[0:1, :] += jnp.sum(part * cot[...].astype(jnp.float32), axis=0, keepdims=True)
        parts[team ^ k] = part.astype(jnp.bfloat16)


def feed_terms(normed, grads, pulls, inner, own, other):
    def flat(ref, columns):
        return jnp.concatenate([ref[g, :, columns] for g in range(ref.shape[0])], axis=0)

    left, pull = flat(normed, slice(None)), flat(pulls, slice(None))
    term = dot_rows(left, flat(grads, slice(None))).astype(jnp.bfloat16)
    term_out = dot_rows(pull, flat(inner, slice(None))).astype(jnp.bfloat16)
    for w, out in enumerate((own, other)):
        out[:, : 2 * FF_DEV] = term[:, 2 * w * FF_DEV : 2 * (w + 1) * FF_DEV]
        out[:, 2 * FF_DEV :] = term_out[:, w * FF_DEV : (w + 1) * FF_DEV]


def attend_back_start(info, back_sum, vec, part_out, frames, cotangent, weight, mixed, _, *refs):
    grad_hidden, sums, grad_mixed, term_own, term_other, grad_attend = refs
    core, team = info[3 * TEAM], info[3 * TEAM + 1]
    sums[...] = jnp.zeros_like(sums)

    def rows(chunk):
        grad_normed = back_sum[chunk, :].astype(jnp.float32)
        attended = part_out[chunk, :]
        unit, scaling = norm_parts(frames[chunk, :].astype(jnp.float32) + vec[4:5, :] * attended)
        grad = cotangent[chunk, :].astype(jnp.float32) + norm_back(
            grad_normed, unit, scaling, vec[2:3, :]
        )
        grad_hidden[chunk, :] = grad
        grad_attend[chunk, :] = (grad * vec[4:5, :]).astype(jnp.bfloat16)
        sums[0:1, :] += jnp.sum(grad_normed * unit, axis=0, keepdims=True)
        sums[1:2, :] += jnp.sum(grad_normed, axis=0, keepdims=True)
        sums[2:3, :] += jnp.sum(grad * attended, axis=0, keepdims=True)

    row_chunks(frames.shape[0], 256, rows)
    grads = dot(grad_attend[...], weight[...]).astype(jnp.bfloat16)
    terms = dot_rows(grad_attend[...], mixed[...]).astype(jnp.bfloat16)
    for k in range(TEAM):
        for j in range(CORES):
            s = k * CORES + j
            columns = slice(s * WIDTH_DEV, (s + 1) * WIDTH_DEV)
            grad_mixed[(team ^ k) * CORES + (core ^ j)] = grads[:, columns]
            (term_other if j else term_own)[team ^ k] = terms[:, columns]


def attend_backward(first, info, *refs):
    grad_mixed, frames, normed, rows_in, win, cosines, sines, _, stats = refs[:9]
    term, sums, keep, send, joint, key_total, value_total, back, total = refs[9:]
    step = pl.program_id(0)
    core = info[3 * TEAM]
    k = info[3 * TEAM + 1] ^ (first + step)
    tokens = frames.shape[1]
    group = CORES * tokens
    width = WIDTH_DEV
    key_total[...] = jnp.zeros_like(key_total)
    value_total[...] = jnp.zeros_like(value_total)
    blocks = range(group // WINDOW)
    tiles = [(block, head) for block in blocks for head in range(HEADS_DEV)]
    masks = [span_mask(info, k, block, group) for block in blocks]

    def products(block, head):
        low, high = key_span(block, group)
        query = head_lanes(rows_in[0, block * WINDOW : (block + 1) * WINDOW, :width], head)
        half, begin = divmod(block * WINDOW, tokens)
        grad = head_lanes(grad_mixed[half, begin : begin + WINDOW, :], head)
        scores = dot_last(query, rows_in[0, low:high, width : 2 * width])
        return query, grad, scores, dot_last(grad, rows_in[0, low:high, 2 * width :])

    def unrotated(x, rows):
        return (x * cosines[0, rows, :] - half_swap(x) * sines[0, rows, :]).astype(jnp.bfloat16)

    ahead = products(*tiles[0])
    outs = []
    for i, (block, head) in enumerate(tiles):
        query, grad, scores, grad_probability = ahead
        if i + 1 < len(tiles):
            ahead = products(*tiles[i + 1])
        low, high = key_span(block, group)
        probability = softmax_rows(scores, masks[block])
        delta = jnp.sum(probability * grad_probability, axis=-1, keepdims=True)
        grad_scores = (probability * (grad_probability - delta)).astype(jnp.bfloat16)
        outs.append(dot(grad_scores, rows_in[0, low:high, width : 2 * width]))
        key_total[low:high, :] += dot_rows(grad_scores, query)
        value_total[low:high, :] += dot_rows(probability.astype(jnp.bfloat16), grad)
        if head == HEADS_DEV - 1:
            rows = slice(block * WINDOW, (block + 1) * WINDOW)
            joint[rows, :width] = unrotated(pick_heads(outs) * SCORE_SCALE, rows)
            outs = []
    for half in range(CORES):
        rows = slice(half * tokens, (half + 1) * tokens)
        joint[rows, width : 2 * width] = unrotated(key_total[rows, :] * SCORE_SCALE, rows)
        joint[rows, 2 * width :] = value_total[rows, :].astype(jnp.bfloat16)

    @pl.when(step == 0)
    def _():
        total[...] = jnp.zeros_like(total)
        sums[...] = jnp.zeros_like(sums)

    both = jnp.concatenate([normed[half] for half in range(CORES)], axis=0)
    total[...] += dot_rows(both, joint[...])
    back[...] = dot_last(joint[...], win[...])
    for half in range(CORES):

        def rows(chunk, half=half):
            part = back[pl.ds(chunk.start + half * tokens, chunk.size), :]
            mean, scaling = stats[half, chunk, 0:1], stats[half, chunk, 1:2]
            unit = (frames[half, chunk, :].astype(jnp.float32) - mean) * scaling
            sums[0:1, :] += jnp.sum(part * unit, axis=0, keepdims=True)
            sums[1:2, :] += jnp.sum(part, axis=0, keepdims=True)

        row_chunks(tokens, 256, rows)
    keep[0] = back[pl.ds(pl.multiple_of(core * tokens, tokens), tokens), :]
    send[0] = back[pl.ds(pl.multiple_of((1 - core) * tokens, tokens), tokens), :].astype(jnp.bfloat16)

    @pl.when(step == TEAM - 1)
    def _():
        for part in range(3):
            term[part] = total[:, part * width : (part + 1) * width].astype(jnp.bfloat16)


def join_terms(parts, out):
    def rows(chunk):
        total = parts[0, chunk, :].astype(jnp.float32)
        for p in range(1, TEAM):
            total = total + parts[p, chunk, :].astype(jnp.float32)
        out[0, chunk, :] = total.astype(jnp.bfloat16)

    row_chunks(D, 256, rows)


def own_sums(last, late, _, grad_in, grad_out, grad_expand, grad_contract, grad_gains, squares):
    rows = grad_in.shape[0]
    devices = last.shape[0]
    total = jnp.zeros((rows, 128), jnp.float32)
    for p in range(SLOTS):
        for part in range(4):
            band = slice(part * rows, (part + 1) * rows)
            value = last[p, band, :].astype(jnp.float32)
            for r in range(1, devices // SLOTS):
                value = value + last[r * SLOTS + p, band, :].astype(jnp.float32)
            total = total + value * value
            begin = p * WIDTH_DEV
            if part < 3:
                grad_in[:, part * D + begin : part * D + begin + WIDTH_DEV] = value
            else:
                grad_out[:, begin : begin + WIDTH_DEV] = value
        for f in range(3 * FF_DEV // 128):
            value = late[p, :, f * 128 : (f + 1) * 128].astype(jnp.float32)
            total = total + value * value
            which, begin = divmod(f * 128, FF_DEV)
            begin += p * FF_DEV
            if which < 2:
                grad_expand[:, which * FF + begin : which * FF + begin + 128] = value
            else:
                grad_contract[:, begin : begin + 128] = value
    value = last[0, 4 * rows : 4 * rows + 16, :].astype(jnp.float32)
    for d in range(1, devices):
        value = value + last[d, 4 * rows : 4 * rows + 16, :].astype(jnp.float32)
    value = value[:8]
    grad_gains[...] = value
    whole = jnp.sum(total) + jnp.sum(value * value)
    squares[...] = jnp.full(squares.shape, whole, jnp.float32)


def adam_all(rates, squares_in, *refs):
    grads, weights, means, squares = refs[:4], refs[4:8], refs[8:12], refs[12:16]
    gain_grads, gains, gain_means, gain_squares = refs[16:20]
    norm_out = refs[21]
    outs, gain_outs = refs[22:38], refs[38:]
    norm = jnp.sqrt(jnp.sum(squares_in[:, 0:1, 0:1]))
    factor = CLIP_NORM / jnp.maximum(norm, CLIP_NORM)
    norm_out[0, 0] = norm

    def update(weight, mean, square, grad, rate, new):
        mean_new, square_new, moved = adam_step(weight, mean, square, grad, factor, rate)
        new[0][...] = mean_new
        new[1][...] = square_new
        new[2][...] = moved
        new[3][...] = moved.astype(jnp.bfloat16)

    for i in range(4):
        update(
            weights[i][...], means[i][...], squares[i][...], grads[i][...], rates[i], outs[i::4]
        )
    count, width = gains.shape
    update(
        gains[...],
        gain_means[...],
        gain_squares[...],
        gain_grads[:count, :width],
        VECTOR_RATE,
        gain_outs,
    )


def frames_back(*refs):
    pieces = refs[: TEAM + 1]
    frames, grad_hidden, vec, _, out = refs[TEAM + 1 :]
    unit, scaling = norm_parts(frames[...].astype(jnp.float32))
    grad_normed = pieces[0][...]
    for piece in pieces[1:]:
        grad_normed = grad_normed + piece[...].astype(jnp.float32)
    out[...] = grad_hidden[...] + norm_back(grad_normed, unit, scaling, vec[0:1, :])


def frames_out(branch, frames, part_out, vec, _, out):
    hidden = frames[...].astype(jnp.float32) + vec[4:5, :] * part_out[...]
    out[...] = (hidden + vec[5:6, :] * branch[...].astype(jnp.float32)).astype(jnp.bfloat16)


def per_device(
    frames,
    clip_lengths,
    cotangent,
    attend_in,
    attend_out,
    expand,
    contract,
    gains,
    prior_mean_attend_in,
    prior_mean_attend_out,
    prior_mean_expand,
    prior_mean_contract,
    prior_mean_gains,
    prior_square_attend_in,
    prior_square_attend_out,
    prior_square_expand,
    prior_square_contract,
    prior_square_gains,
):
    bf16 = jnp.bfloat16
    f32 = jnp.float32
    tokens = frames.shape[0]
    group = tokens * CORES
    rows = attend_in.shape[0]
    gain_width = gains.shape[1]
    reps = lax.axis_size("rep")
    devices = reps * SLOTS
    rep = lax.axis_index("rep")
    team = lax.axis_index("team")
    core = lax.axis_index("tm")

    frames_team = lax.all_gather(frames, MEMBERS, axis=0, tiled=False)

    tail_rows = 16
    lanes = 128
    parts = attend_in.astype(bf16).reshape(rows, 3, SLOTS, WIDTH_DEV).transpose(2, 1, 0, 3)
    parts = jnp.concatenate(
        [parts, attend_out.astype(bf16).reshape(rows, 1, SLOTS, WIDTH_DEV).transpose(2, 1, 0, 3)],
        axis=1,
    ).reshape(SLOTS, 4 * rows, lanes)
    small = jnp.zeros((tail_rows, lanes), f32)
    small = small.at[:6, :gain_width].set(gains)
    small = small.at[6, :3].set((clip_lengths[0] // 16).astype(f32))
    small = small.at[7, :3].set((clip_lengths[0] % 16).astype(f32))
    small = jnp.broadcast_to(small.astype(bf16)[None], (SLOTS, tail_rows, lanes))
    parts = jnp.concatenate([parts, small], axis=1)
    parts = jnp.broadcast_to(parts[None], (reps,) + parts.shape)
    spread = lax.all_to_all(
        parts.reshape(devices, 4 * rows + tail_rows, lanes), ALL, 0, 0, tiled=True
    )
    part_in = spread[:, : 3 * rows].reshape(devices, 3, rows, lanes).transpose(0, 2, 1, 3)
    part_in = part_in.reshape(D, 3 * WIDTH_DEV)
    part_out = spread[:, 3 * rows : 4 * rows].reshape(D, WIDTH_DEV)
    small = spread[:, 4 * rows : 4 * rows + 8].astype(f32)
    vectors = small[:, :6, :gain_width].transpose(1, 0, 2).reshape(6, D)
    vectors = jnp.pad(vectors, ((0, 2), (0, 0)))
    lengths = lax.dynamic_index_in_dim(
        small[:, 6:, :3].reshape(reps, TEAM, CORES, 2, 3)[:, :, 0], rep, 0, keepdims=False
    )
    lengths = (lengths[:, 0] * 16 + lengths[:, 1]).astype(jnp.int32)
    info = jnp.concatenate([lengths.reshape(-1), jnp.stack([core, team])])

    mlp_pack = jnp.concatenate(
        [
            expand.astype(bf16).reshape(rows, 2, SLOTS, FF_DEV).transpose(2, 0, 1, 3).reshape(
                SLOTS, rows, 2 * FF_DEV
            ),
            contract.astype(bf16).reshape(rows, SLOTS, FF_DEV).transpose(1, 0, 2),
        ],
        axis=2,
    )
    mlp_cols = exchange_team(after(mlp_pack, spread)).reshape(SLOTS * rows, 3 * FF_DEV)
    outs_team = gather_team(part_out)
    cots = [cotangent] + send_mates([after(cotangent, mlp_cols)] * (TEAM - 2))

    places = jnp.arange(group, dtype=jnp.int32)
    ends = jnp.cumsum(lengths, axis=1)
    starts = ends - lengths
    begin = jnp.max(
        jnp.where(starts[:, None, :] <= places[None, :, None], starts[:, None, :], 0), axis=2
    )
    offsets = (places[None] - begin).astype(f32)
    freqs = np.power(10000.0, -2.0 * np.arange(HEAD // 2) / HEAD)
    lane_freqs = jnp.asarray(np.tile(freqs, WIDTH_DEV // (HEAD // 2)), dtype=f32)
    angles = offsets[:, :, None] * lane_freqs
    signs = jnp.asarray(np.where(np.arange(WIDTH_DEV) % HEAD < HEAD // 2, -1.0, 1.0), dtype=f32)
    cosines = jnp.cos(angles)
    sines = jnp.sin(angles) * signs
    mlp_weight = lax.all_gather(
        after(mlp_cols, sines, frames_team), ("rep", "tm"), axis=0, tiled=False
    ).reshape(reps, CORES, SLOTS * rows, 3 * FF_DEV)

    by_frames = (CORES, tokens, D)
    by_heads = (CORES, tokens, WIDTH_DEV)
    by_rows = (1, group, 3 * WIDTH_DEV)
    by_angles = (1, group, WIDTH_DEV)
    normed_one, attend_rows, mixed, stats_one = call_groups(
        attend_forward,
        info,
        [
            (in_hbm(frames_team), by_frames),
            (vectors, None),
            (part_in, None),
            (in_hbm(cosines), by_angles),
            (in_hbm(sines), by_angles),
        ],
        [
            ((SLOTS, tokens, D), bf16, by_frames, HBM_OUT),
            ((TEAM, group, 3 * WIDTH_DEV), bf16, by_rows, HBM_OUT),
            ((SLOTS, tokens, WIDTH_DEV), bf16, by_heads, HBM_OUT),
            ((SLOTS, tokens, lanes), f32, (CORES, tokens, lanes), HBM_OUT),
        ],
        name="attend_forward",
        micros=24,
    )

    cots.append(to_mate(after(cotangent, mixed), TEAM - 1))
    mixed_own = exchange_team(mixed)
    attend_part, normed_two, full_out, mixed_flat = call_kernel(
        attend_finish,
        [info, mixed_own, *outs_team, frames, vectors] + [x[:16, :128] for x in cots[1:]],
        [
            ((tokens, D), f32, HBM_OUT),
            ((TEAM, tokens, D), bf16),
            ((D, D), bf16, HBM_OUT),
            ((tokens, D), bf16, HBM_OUT),
        ],
        specs=[SMEM_SPEC] + [VMEM_SPEC] * (SLOTS + 3) + [ANY_SPEC] * (TEAM - 1),
        far=(10,),
        name="attend_finish",
        micros=4,
    )

    normed_team = lax.all_to_all(normed_two, "team", 0, 0, tiled=True)
    by_pairs = (TEAM // 2, tokens, D)
    inner, grads_up, pulls, back = call_groups(
        feed_forward,
        info,
        [
            (normed_team, by_pairs),
            (vectors, None),
            (in_hbm(mlp_weight), "far"),
            *[(in_hbm(x), "far") for x in cots],
        ],
        [
            ((TEAM, tokens, 2 * FF_DEV), bf16, (TEAM // 2, tokens, 2 * FF_DEV), HBM_OUT),
            ((TEAM, tokens, 4 * FF_DEV), bf16, (TEAM // 2, tokens, 4 * FF_DEV), HBM_OUT),
            ((TEAM, tokens, D), bf16, by_pairs, HBM_OUT),
            ((TEAM, tokens, D), bf16, by_pairs, HBM_OUT),
        ],
        scratch=[
            pltpu.VMEM(mlp_weight.shape, bf16),
            pltpu.SemaphoreType.DMA((CORES, mlp_weight.shape[0])),
            pltpu.VMEM((TEAM, tokens, D), bf16),
            pltpu.SemaphoreType.DMA((TEAM,)),
        ],
        steps=2,
        vmem=26,
        name="feed_forward",
        micros=20,
    )
    back_sum = lax.psum_scatter(back, "team", scatter_dimension=0, tiled=False)
    term_own, term_other = call_terms(normed_team, grads_up, pulls, inner)
    term_got = other_core(term_other)
    branch_parts, sums_out = call_kernel(
        feed_branch,
        [info, inner, mlp_weight, term_own[:16, :128], *cots],
        [((TEAM, tokens, D), bf16, HBM_OUT), ((8, D), f32)],
        specs=[SMEM_SPEC] + [VMEM_SPEC] * 2 + [ANY_SPEC] + [VMEM_SPEC] * TEAM,
        far=(1, 4, 5, 6, 7),
        name="feed_branch",
        micros=9,
    )
    branch_sum = lax.psum_scatter(branch_parts, "team", scatter_dimension=0, tiled=False)
    term_got = after(term_got, sums_out)
    term_mlp = (term_own.astype(f32) + term_got.astype(f32)).astype(bf16)
    mlp_sum = lax.psum_scatter(term_mlp, "rep", scatter_dimension=0, tiled=True)

    loads = [attend_part, frames, cotangent, full_out, mixed_flat]
    grad_hidden, sums_two, grad_mixed, term_own, term_other = call_kernel(
        attend_back_start,
        [info, back_sum, vectors, *loads, sums_out],
        [
            ((tokens, D), f32, HBM_OUT),
            ((8, D), f32),
            ((SLOTS, tokens, WIDTH_DEV), bf16),
            ((TEAM, D, WIDTH_DEV), bf16),
            ((TEAM, D, WIDTH_DEV), bf16),
        ],
        scratch=[pltpu.VMEM((tokens, D), bf16)],
        specs=[SMEM_SPEC] + [VMEM_SPEC] * (len(loads) + 2) + [ANY_SPEC],
        far=(1, 3, 4, 5, 6, 7),
        vmem=24,
        name="attend_back_start",
        micros=6,
    )
    grad_mixed = exchange_team(grad_mixed)
    out_sum = (term_own.astype(f32) + other_core(term_other).astype(f32)).astype(bf16)
    out_sum = after(out_sum, grad_mixed[0, :16])
    out_parts = lax.all_to_all(out_sum, "team", 0, 0, tiled=True)
    term_in, sums_one, one_keep, one_send = call_groups(
        attend_backward,
        info,
        [
            (grad_mixed, by_heads),
            (in_hbm(frames_team), by_frames),
            (in_hbm(normed_one), by_frames),
            (in_hbm(attend_rows), by_rows),
            (part_in, None),
            (in_hbm(cosines), by_angles),
            (in_hbm(sines), by_angles),
            (after(vectors, out_sum), None),
            (in_hbm(stats_one), (CORES, tokens, lanes)),
        ],
        [
            ((3, D, WIDTH_DEV), bf16, None, HBM_OUT),
            ((8, D), f32, None, PLAIN),
            ((TEAM, tokens, D), f32, (1, tokens, D), HBM_OUT),
            ((TEAM, tokens, D), bf16, (1, tokens, D), HBM_OUT),
        ],
        scratch=[
            pltpu.VMEM((group, 3 * WIDTH_DEV), bf16),
            pltpu.VMEM((group, WIDTH_DEV), f32),
            pltpu.VMEM((group, WIDTH_DEV), f32),
            pltpu.VMEM((group, D), f32),
            pltpu.VMEM((D, 3 * WIDTH_DEV), f32),
        ],
        mates=(0, TEAM),
        name="attend_backward",
        micros=25,
    )
    one_got = other_core(one_send)
    keeps, gots = list(one_keep), list(one_got)
    one_chips = chip_sums(keeps, gots)
    one_pieces = [keeps[0], gots[0]] + send_mates(one_chips)

    (out_part,) = call_kernel(
        join_terms, [out_parts], [((1, D, WIDTH_DEV), bf16)], name="join_terms", micros=1
    )
    terms = jnp.concatenate([term_in, out_part], axis=0)
    term_gains = jnp.concatenate([sums_one[:2], sums_two[:3], sums_out[:1]])
    gains_block = jnp.zeros((devices, tail_rows, lanes), bf16)
    gains_block = gains_block.at[:, :6, :gain_width].set(
        term_gains.astype(bf16).reshape(6, devices, gain_width).transpose(1, 0, 2)
    )
    terms = terms.reshape(4, devices, rows, lanes).transpose(1, 0, 2, 3)
    last = lax.all_to_all(
        jnp.concatenate([terms.reshape(devices, 4 * rows, lanes), gains_block], axis=1),
        ALL,
        0,
        0,
        tiled=True,
    )
    late = exchange_team(after(mlp_sum.reshape(SLOTS, rows, 3 * FF_DEV), last[0, :16]))
    shapes = [(rows, 3 * D), (rows, D), (rows, 2 * FF), (rows, FF), (8, lanes)]
    if rows % 16 == 0:
        *owned, squares_out = call_kernel(
            own_sums,
            [last, late, one_chips[0][:16, :128]],
            [(shape, f32, HBM_OUT) for shape in shapes] + [((devices, 8, lanes), f32)],
            vmem=16,
            name="own_sums",
            micros=4,
        )
    else:
        last_sum = jnp.sum(
            last[:, : 4 * rows].reshape(reps, SLOTS, 4, rows, lanes).astype(f32), axis=0
        )
        late = late.astype(f32)
        owned = [
            last_sum[:, :3].transpose(2, 1, 0, 3).reshape(rows, 3 * D),
            last_sum[:, 3].transpose(1, 0, 2).reshape(rows, D),
            late[:, :, : 2 * FF_DEV]
            .reshape(SLOTS, rows, 2, FF_DEV)
            .transpose(1, 2, 0, 3)
            .reshape(rows, 2 * FF),
            late[:, :, 2 * FF_DEV :].transpose(1, 0, 2).reshape(rows, FF),
            jnp.sum(last[:, 4 * rows : 4 * rows + 8].astype(f32), axis=0),
        ]
        square_part = jnp.zeros((), f32)
        for grad in owned:
            square_part = square_part + jnp.sum(grad * grad)
        squares_out = jnp.full((devices, 8, lanes), square_part)
    squares_in = lax.all_to_all(squares_out, ALL, 0, 0, tiled=True)

    weights = [attend_in, attend_out, expand, contract]
    means = [prior_mean_attend_in, prior_mean_attend_out, prior_mean_expand, prior_mean_contract]
    squares = [
        prior_square_attend_in,
        prior_square_attend_out,
        prior_square_expand,
        prior_square_contract,
    ]
    rates = (RATE / math.sqrt(D), RATE / math.sqrt(D // 64), RATE / math.sqrt(D), RATE / math.sqrt(FF))
    steps = 4
    columns = [pl.BlockSpec((rows, x.shape[1] // steps), lambda i: (0, i)) for x in weights]
    whole = pl.BlockSpec(gains.shape, lambda i: (0, 0))
    out = pl.pallas_call(
        functools.partial(adam_all, rates),
        grid=(steps,),
        in_specs=[pl.BlockSpec(squares_in.shape, lambda i: (0, 0, 0))]
        + columns * 4
        + [pl.BlockSpec((8, lanes), lambda i: (0, 0))]
        + [whole] * 3
        + [ANY_SPEC],
        out_specs=[pl.BlockSpec(memory_space=pltpu.SMEM)] + columns * 4 + [whole] * 4,
        out_shape=[jax.ShapeDtypeStruct((1, 1), f32)]
        + [
            jax.ShapeDtypeStruct(x.shape, dtype) for dtype in (f32, f32, f32, bf16) for x in weights
        ]
        + [jax.ShapeDtypeStruct(gains.shape, dtype) for dtype in (f32, f32, f32, bf16)],
        compiler_params=pltpu.CompilerParams(vmem_limit_bytes=24 * MIB),
        cost_estimate=cost(8),
        name="adam_all",
    )(
        squares_in,
        *[in_hbm(x) for x in (*owned[:4], *weights, *means, *squares)],
        owned[4],
        gains,
        prior_mean_gains,
        prior_square_gains,
        one_pieces[2][:16, :128],
    )
    (out_frames,) = call_kernel(
        frames_out,
        [branch_sum, frames, attend_part, vectors, out[-2]],
        [((tokens, D), bf16)],
        specs=[VMEM_SPEC] * 4 + [ANY_SPEC],
        far=(0, 1, 2),
        name="frames_out",
        micros=3,
    )

    (frames_grad,) = call_kernel(
        frames_back,
        [*one_pieces, frames, grad_hidden, vectors, out[-2]],
        [((tokens, D), f32)],
        specs=[VMEM_SPEC] * (TEAM + 4) + [ANY_SPEC],
        name="frames_back",
        micros=4,
    )
    news = [out[1 + kind * 4 + which] for which in range(4) for kind in range(4)]
    return (out_frames, frames_grad, out[0][0, 0], *news, *out[17:])


def solution(mesh):
    teams = Mesh(
        mesh.devices.reshape(mesh.shape["dp"] // TEAM, TEAM, mesh.shape["tm"]), ALL
    )
    by_row = P(ALL, None)
    by_column = P(None, ALL)
    per_group = P(("rep", "team"), None)
    weights = (by_row, by_row, by_row, by_row, by_column)
    return jax.shard_map(
        per_device,
        mesh=teams,
        in_specs=(by_row, per_group, by_row) + weights * 3,
        out_specs=(by_row, by_row, P()) + (by_row,) * 16 + (by_column,) * 4,
        check_vma=False,
    )
```

```python
import functools
import math

import jax
import jax.numpy as jnp
import numpy as np
from jax import lax
from jax.experimental import pallas as pl
from jax.experimental.pallas import tpu as pltpu
from jax.sharding import Mesh
from jax.sharding import PartitionSpec as P

D = 1024
HEADS = 16
HEAD = 64
FF = 4096
WINDOW = 128
STEP = 10

EPS_NORM = 1e-05
NEG_FILL = -1e30
SCORE_SCALE = 0.125
BETA_ONE = 0.9
BETA_TWO = 0.999
ADAM_EPS = 1e-08
DECAY = 0.1
RATE = 3.0
VECTOR_RATE = 0.6
CLIP_NORM = 1.0

TEAM = 4
CORES = 2
SLOTS = TEAM * CORES
ALL = ("rep", "team", "tm")
MEMBERS = ("team", "tm")
ANY_SPEC = pl.BlockSpec(memory_space=pl.ANY)
SMEM_SPEC = pl.BlockSpec(memory_space=pltpu.SMEM)
VMEM_SPEC = pl.BlockSpec(memory_space=pltpu.VMEM)
MIB = 1 << 20
PLAIN, HBM_OUT = range(2)
HBM_SPEC = pl.BlockSpec(memory_space=pltpu.HBM)
LOG2_E = math.log2(math.e)
HEADS_DEV = HEADS // SLOTS
WIDTH_DEV = HEADS_DEV * HEAD
FF_DEV = FF // SLOTS


def swap_pairs(count, bit):
    return [(a, a ^ bit) for a in range(count)]


def other_core(x):
    return lax.ppermute(x, "tm", swap_pairs(CORES, 1))


def to_mate(x, bit):
    return lax.ppermute(x, "team", swap_pairs(TEAM, bit))


def gather_team(x):
    blocks = [x] + [to_mate(x, k) for k in range(1, TEAM)]
    parts = []
    for block in blocks:
        parts += [block, other_core(block)]
    return parts


def chip_sums(keep, got):
    return [
        (keep[k] + got[k].astype(jnp.float32)).astype(jnp.bfloat16) for k in range(1, TEAM)
    ]


def send_mates(chips):
    return [to_mate(chip, k + 1) for k, chip in enumerate(chips)]


def exchange_team(x):
    return lax.all_to_all(x, MEMBERS, 0, 0, tiled=True)


def after(x, *tokens):
    return pl.pallas_call(
        lambda *refs: None,
        out_shape=jax.ShapeDtypeStruct(x.shape, x.dtype),
        in_specs=[ANY_SPEC] * (1 + len(tokens)),
        out_specs=ANY_SPEC,
        input_output_aliases={0: 0},
        name="after",
    )(x, *tokens)


def norm_parts(values):
    centered = values - jnp.mean(values, axis=-1, keepdims=True)
    scaling = lax.rsqrt(jnp.mean(centered * centered, axis=-1, keepdims=True) + EPS_NORM)
    return (centered * scaling, scaling)


def norm_back(gradient, unit_rows, scaling, gain_row):
    scaled = gradient * gain_row
    return scaling * (
        scaled
        - jnp.mean(scaled, axis=-1, keepdims=True)
        - unit_rows * jnp.mean(scaled * unit_rows, axis=-1, keepdims=True)
    )


def dot_rows(left_side, right_side):
    return lax.dot_general(
        left_side, right_side, (((0,), (0,)), ((), ())), preferred_element_type=jnp.float32
    )


def dot_last(left_side, right_side):
    return lax.dot_general(
        left_side, right_side, (((1,), (1,)), ((), ())), preferred_element_type=jnp.float32
    )


def dot(left_side, right_side):
    return jnp.dot(left_side, right_side, preferred_element_type=jnp.float32)


def adam_step(weight, mean_old, square_old, gradient, factor, step_rate):
    clipped = gradient * factor
    mean_new = BETA_ONE * mean_old + (1.0 - BETA_ONE) * clipped
    square_new = BETA_TWO * square_old + (1.0 - BETA_TWO) * clipped * clipped
    mean_hat = mean_new / (1.0 - BETA_ONE**STEP)
    square_hat = square_new / (1.0 - BETA_TWO**STEP)
    moved = weight - step_rate * (mean_hat / (jnp.sqrt(square_hat) + ADAM_EPS) + DECAY * weight)
    return (mean_new, square_new, moved)


def in_hbm(x):
    return pltpu.with_memory_space_constraint(x, pltpu.HBM)


def cost(micros):
    return pl.CostEstimate(flops=int(micros * 1e9), transcendentals=0, bytes_accessed=int(micros * 1e6))


def call_kernel(
    kernel, ins, outs, scratch=(), specs=None, far=(), lazy=0, vmem=16, name=None, micros=2
):
    specs = list(specs or [VMEM_SPEC] * len(ins))
    ins = list(ins)
    buffers = [pltpu.VMEM(ins[i].shape, ins[i].dtype) for i in far]
    for i in far:
        specs[i] = HBM_SPEC
        ins[i] = in_hbm(ins[i])

    def loaded(*refs):
        refs = list(refs)
        if far:
            near, sems = refs[-1 - len(far) : -1], refs[-1]
            refs = refs[: -1 - len(far)]
            copies = [
                pltpu.make_async_copy(refs[i], b, sems.at[n]) for n, (i, b) in enumerate(zip(far, near))
            ]
            for copy in copies:
                copy.start()
            for copy in copies[: len(far) - lazy]:
                copy.wait()
            for i, b in zip(far, near):
                refs[i] = b
        if lazy:
            kernel(copies[len(far) - lazy :], *refs)
        else:
            kernel(*refs)

    return pl.pallas_call(
        loaded,
        out_shape=[
            (pltpu.HBM if mode else jax.ShapeDtypeStruct)(shape, dtype) for shape, dtype, *mode in outs
        ],
        in_specs=specs,
        out_specs=[VMEM_SPEC] * len(outs),
        scratch_shapes=[
            *scratch,
            *buffers,
            *([pltpu.SemaphoreType.DMA((len(far),))] if far else []),
        ],
        compiler_params=pltpu.CompilerParams(vmem_limit_bytes=vmem * MIB),
        cost_estimate=cost(micros),
        name=name,
    )(*ins)


def call_terms(normed, grads, pulls, inner):
    count, tokens, _ = normed.shape
    step = 256
    by_rows = pl.BlockSpec((count, tokens, step), lambda r: (0, 0, r))

    def whole(x):
        return pl.BlockSpec(x.shape, lambda r: (0, 0, 0), pipeline_mode=pl.Buffered(1))

    return pl.pallas_call(
        feed_terms,
        grid=(D // step,),
        in_specs=[by_rows, whole(grads), by_rows, whole(inner)],
        out_specs=[pl.BlockSpec((step, 3 * FF_DEV), lambda r: (r, 0))] * 2,
        out_shape=[
            pltpu.HBM((D, 3 * FF_DEV), jnp.bfloat16),
            jax.ShapeDtypeStruct((D, 3 * FF_DEV), jnp.bfloat16),
        ],
        compiler_params=pltpu.CompilerParams(vmem_limit_bytes=24 * MIB),
        cost_estimate=cost(8),
        name="feed_terms",
    )(in_hbm(normed), in_hbm(grads), in_hbm(pulls), in_hbm(inner))


def call_groups(
    kernel, info, ins, outs, scratch=(), vmem=24, name=None, micros=20, mates=None, steps=TEAM
):
    def spec(shape, block, out):
        rest = (0,) * (len(shape) - 1)
        if block == "far":
            return HBM_SPEC
        if block is None:
            return pl.BlockSpec(
                shape, lambda g, info: (0, *rest), pipeline_mode=None if out else pl.Buffered(1)
            )
        if mates and not out:
            return pl.BlockSpec(block, lambda g, info: (info[3 * TEAM + 1] ^ (mates[0] + g), *rest))
        return pl.BlockSpec(block, lambda g, info: (g, *rest))

    return pl.pallas_call(
        functools.partial(kernel, mates[0] if mates else 0),
        grid_spec=pltpu.PrefetchScalarGridSpec(
            num_scalar_prefetch=1,
            grid=(mates[1] if mates else steps,),
            in_specs=[spec(x.shape, block, False) for x, block in ins],
            out_specs=[spec(shape, block, True) for shape, _, block, _ in outs],
            scratch_shapes=list(scratch),
        ),
        out_shape=[
            jax.ShapeDtypeStruct(shape, dtype) if mode == PLAIN else pltpu.HBM(shape, dtype)
            for shape, dtype, _, mode in outs
        ],
        compiler_params=pltpu.CompilerParams(vmem_limit_bytes=vmem * MIB),
        cost_estimate=cost(micros),
        name=name,
    )(info, *[x for x, _ in ins])


def row_chunks(count, size, body):
    def step(i, carry):
        body(pl.ds(pl.multiple_of(i * size, size), size))
        return carry

    lax.fori_loop(0, count // size, step, 0)


def lanes_of(x):
    return lax.broadcasted_iota(jnp.int32, (1, x.shape[-1]), 1)


def half_swap(x):
    width = x.shape[-1]
    half = HEAD // 2
    first = (lanes_of(x) & half) == 0
    return jnp.where(first, pltpu.roll(x, width - half, x.ndim - 1), pltpu.roll(x, half, x.ndim - 1))


def key_span(block, group):
    return max(0, (block - 1) * WINDOW), min(group, (block + 2) * WINDOW)


def span_mask(info, slot, block, group):
    low, high = key_span(block, group)
    first = info[3 * slot]
    second = first + info[3 * slot + 1]
    third = second + info[3 * slot + 2]
    place = block * WINDOW + lax.broadcasted_iota(jnp.int32, (WINDOW, 1), 0)
    start = jnp.where(
        place >= third,
        third,
        jnp.where(place >= second, second, jnp.where(place >= first, first, 0)),
    )
    end = jnp.where(
        place < first, first, jnp.where(place < second, second, jnp.where(place < third, third, group))
    )
    least = jnp.maximum(start, place - WINDOW)
    most = jnp.minimum(end, place + WINDOW + 1)
    key_place = low + lax.broadcasted_iota(jnp.int32, (1, high - low), 1)
    return (key_place >= least) & (key_place < most)


def head_lanes(x, head):
    lane = lanes_of(x)
    inside = (lane >= head * HEAD) & (lane < (head + 1) * HEAD)
    return jnp.where(inside, x, jnp.zeros_like(x))


def pick_heads(parts):
    out = parts[0]
    for head in range(1, len(parts)):
        out = jnp.where(lanes_of(out) >= head * HEAD, parts[head], out)
    return out


def softmax_rows(products, allowed):
    scores = jnp.where(allowed, products * (SCORE_SCALE * LOG2_E), NEG_FILL)
    exponent = jnp.exp2(scores - jnp.max(scores, axis=-1, keepdims=True))
    return exponent * (1.0 / jnp.sum(exponent, axis=-1, keepdims=True))


def attend_forward(_, info, frames, vec, win, cosines, sines, normed, rows_out, mixed, stats):
    k = pl.program_id(0)
    tokens = frames.shape[1]
    group = CORES * tokens
    width = WIDTH_DEV
    for half in range(CORES):
        rows = slice(half * tokens, (half + 1) * tokens)

        def norm_rows(chunk, half=half):
            values = frames[half, chunk, :].astype(jnp.float32)
            mean = jnp.mean(values, axis=-1, keepdims=True)
            unit, scaling = norm_parts(values)
            stats[half, chunk, :] = jnp.where(lanes_of(stats) == 0, mean, scaling)
            normed[half, chunk, :] = (unit * vec[0:1, :] + vec[1:2, :]).astype(jnp.bfloat16)

        row_chunks(tokens, 256, norm_rows)
        joint = dot(normed[half], win[...])
        for part in range(2):
            x = joint[:, part * width : (part + 1) * width]
            rows_out[0, rows, part * width : (part + 1) * width] = (
                x * cosines[0, rows, :] + half_swap(x) * sines[0, rows, :]
            ).astype(jnp.bfloat16)
        rows_out[0, rows, 2 * width :] = joint[:, 2 * width :].astype(jnp.bfloat16)

    blocks = range(group // WINDOW)
    tiles = [(block, head) for block in blocks for head in range(HEADS_DEV)]
    masks = [span_mask(info, k, block, group) for block in blocks]

    def product(block, head):
        low, high = key_span(block, group)
        query = head_lanes(rows_out[0, block * WINDOW : (block + 1) * WINDOW, :width], head)
        return dot_last(query, rows_out[0, low:high, width : 2 * width])

    ahead = product(*tiles[0])
    outs = []
    for i, (block, head) in enumerate(tiles):
        now = ahead
        if i + 1 < len(tiles):
            ahead = product(*tiles[i + 1])
        low, high = key_span(block, group)
        probability = softmax_rows(now, masks[block]).astype(jnp.bfloat16)
        outs.append(dot(probability, rows_out[0, low:high, 2 * width :]))
        if head == HEADS_DEV - 1:
            half, begin = divmod(block * WINDOW, tokens)
            mixed[half, begin : begin + WINDOW, :] = pick_heads(outs).astype(jnp.bfloat16)
            outs = []


def attend_finish(info, mixed, *refs):
    outs = refs[:SLOTS]
    frames, vec = refs[SLOTS : SLOTS + 2]
    part_out, normed, weight, mixed_out = refs[-4:]
    core, team = info[3 * TEAM], info[3 * TEAM + 1]
    for k in range(TEAM):
        for j in range(CORES):
            s = k * CORES + j
            columns = slice(s * WIDTH_DEV, (s + 1) * WIDTH_DEV)
            weight[:, columns] = outs[s][...]
            mixed_out[:, columns] = mixed[(team ^ k) * CORES + (core ^ j)]
    part_out[...] = dot_last(mixed_out[...], weight[...])

    def rows(chunk):
        hidden = frames[chunk, :].astype(jnp.float32) + vec[4:5, :] * part_out[chunk, :]
        unit, _ = norm_parts(hidden)
        low = (unit * vec[2:3, :] + vec[3:4, :]).astype(jnp.bfloat16)
        for k in range(TEAM):
            normed[k, chunk, :] = low

    row_chunks(frames.shape[0], 256, rows)


def half_weight(weight, core, columns):
    return jnp.concatenate([weight[r, core, :, columns] for r in range(weight.shape[0])], axis=0)


def feed_forward(_, info, normed, vec, far_weight, *refs):
    far_cots = refs[:TEAM]
    inner, grads, pulls, back, weight, sems, cots, cot_sems = refs[TEAM:]
    count, tokens, _ = normed.shape
    half = FF_DEV // 2
    core = info[3 * TEAM]

    def flat(ref):
        return jnp.concatenate([ref[g] for g in range(count)], axis=0)

    def spread(ref, columns, value):
        low = value.astype(jnp.bfloat16)
        for g in range(count):
            ref[g, :, columns] = low[g * tokens : (g + 1) * tokens]

    first = pl.program_id(0) == 0
    copies = [
        [
            pltpu.make_async_copy(far_weight.at[r, core ^ w], weight.at[r, core ^ w], sems.at[w, r])
            for r in range(weight.shape[0])
        ]
        for w in range(CORES)
    ]

    cot_copies = [
        pltpu.make_async_copy(cot, cots.at[info[3 * TEAM + 1] ^ k], cot_sems.at[k])
        for k, cot in enumerate(far_cots)
    ]

    @pl.when(first)
    def _():
        for copy in copies[0] + cot_copies + copies[1]:
            copy.start()

    for w in range(CORES):

        @pl.when(first)
        def _(w=w):
            for copy in copies[w]:
                copy.wait()

        for f in range(2):
            begin = f * half
            gate_cols = slice(begin, begin + half)
            up_cols = slice(FF_DEV + begin, FF_DEV + begin + half)
            out_cols = slice(2 * FF_DEV + begin, 2 * FF_DEV + begin + half)
            gate = dot(flat(normed), half_weight(weight, core ^ w, gate_cols))
            up = dot(flat(normed), half_weight(weight, core ^ w, up_cols))
            if w == f == 0:

                @pl.when(first)
                def _():
                    for copy in cot_copies:
                        copy.wait()

                for g in range(count):
                    cot = cots[count * pl.program_id(0) + g].astype(jnp.float32)
                    pulls[g] = (cot * vec[5:6, :]).astype(jnp.bfloat16)
            grad_inner = dot(flat(pulls), half_weight(weight, core ^ w, out_cols))
            sigmoid = jax.nn.sigmoid(gate)
            silu = gate * sigmoid
            inner_cols = slice(w * FF_DEV + begin, w * FF_DEV + begin + half)
            spread(inner, inner_cols, silu * up)
            slope = grad_inner * up * sigmoid * (1.0 + gate * (1.0 - sigmoid))
            shift = 2 * w * FF_DEV
            spread(grads, slice(shift + begin, shift + begin + half), slope)
            begin += shift + FF_DEV
            spread(grads, slice(begin, begin + half), grad_inner * silu)
    both = jnp.concatenate(
        [half_weight(weight, core ^ w, slice(0, 2 * FF_DEV)) for w in range(CORES)], axis=1
    )
    total = dot_last(flat(grads), both)
    spread(back, slice(None), total)


def feed_branch(info, inner, weight, _, *refs):
    cots, (parts, sums) = refs[:TEAM], refs[TEAM:]
    core, team = info[3 * TEAM], info[3 * TEAM + 1]
    sums[...] = jnp.zeros_like(sums)
    columns = slice(2 * FF_DEV, 3 * FF_DEV)
    both = jnp.concatenate(
        [half_weight(weight, core ^ w, columns) for w in range(CORES)], axis=1
    )
    for k, cot in enumerate(cots):
        part = dot_last(inner[team ^ k], both)
        sums[0:1, :] += jnp.sum(part * cot[...].astype(jnp.float32), axis=0, keepdims=True)
        parts[team ^ k] = part.astype(jnp.bfloat16)


def feed_terms(normed, grads, pulls, inner, own, other):
    def flat(ref, columns):
        return jnp.concatenate([ref[g, :, columns] for g in range(ref.shape[0])], axis=0)

    left, pull = flat(normed, slice(None)), flat(pulls, slice(None))
    term = dot_rows(left, flat(grads, slice(None))).astype(jnp.bfloat16)
    term_out = dot_rows(pull, flat(inner, slice(None))).astype(jnp.bfloat16)
    for w, out in enumerate((own, other)):
        out[:, : 2 * FF_DEV] = term[:, 2 * w * FF_DEV : 2 * (w + 1) * FF_DEV]
        out[:, 2 * FF_DEV :] = term_out[:, w * FF_DEV : (w + 1) * FF_DEV]


def attend_back_start(copies, info, back_sum, vec, part_out, frames, cotangent, weight, mixed, _, *refs):
    grad_hidden, sums, grad_mixed, term_own, term_other, grad_attend = refs
    core, team = info[3 * TEAM], info[3 * TEAM + 1]
    sums[...] = jnp.zeros_like(sums)

    def rows(chunk):
        grad_normed = back_sum[chunk, :].astype(jnp.float32)
        attended = part_out[chunk, :]
        unit, scaling = norm_parts(frames[chunk, :].astype(jnp.float32) + vec[4:5, :] * attended)
        grad = cotangent[chunk, :].astype(jnp.float32) + norm_back(
            grad_normed, unit, scaling, vec[2:3, :]
        )
        grad_hidden[chunk, :] = grad
        grad_attend[chunk, :] = (grad * vec[4:5, :]).astype(jnp.bfloat16)
        sums[0:1, :] += jnp.sum(grad_normed * unit, axis=0, keepdims=True)
        sums[1:2, :] += jnp.sum(grad_normed, axis=0, keepdims=True)
        sums[2:3, :] += jnp.sum(grad * attended, axis=0, keepdims=True)

    row_chunks(frames.shape[0], 256, rows)
    for copy in copies:
        copy.wait()
    grads = dot(grad_attend[...], weight[...]).astype(jnp.bfloat16)
    terms = dot_rows(grad_attend[...], mixed[...]).astype(jnp.bfloat16)
    for k in range(TEAM):
        for j in range(CORES):
            s = k * CORES + j
            columns = slice(s * WIDTH_DEV, (s + 1) * WIDTH_DEV)
            grad_mixed[(team ^ k) * CORES + (core ^ j)] = grads[:, columns]
            (term_other if j else term_own)[team ^ k] = terms[:, columns]


def attend_backward(first, info, *refs):
    grad_mixed, frames, normed, rows_in, win, cosines, sines, _, stats = refs[:9]
    term, sums, keep, send, joint, key_total, value_total, back, total = refs[9:]
    step = pl.program_id(0)
    core = info[3 * TEAM]
    k = info[3 * TEAM + 1] ^ (first + step)
    tokens = frames.shape[1]
    group = CORES * tokens
    width = WIDTH_DEV
    key_total[...] = jnp.zeros_like(key_total)
    value_total[...] = jnp.zeros_like(value_total)
    blocks = range(group // WINDOW)
    tiles = [(block, head) for block in blocks for head in range(HEADS_DEV)]
    masks = [span_mask(info, k, block, group) for block in blocks]

    def products(block, head):
        low, high = key_span(block, group)
        query = head_lanes(rows_in[0, block * WINDOW : (block + 1) * WINDOW, :width], head)
        half, begin = divmod(block * WINDOW, tokens)
        grad = head_lanes(grad_mixed[half, begin : begin + WINDOW, :], head)
        scores = dot_last(query, rows_in[0, low:high, width : 2 * width])
        return query, grad, scores, dot_last(grad, rows_in[0, low:high, 2 * width :])

    def unrotated(x, rows):
        return (x * cosines[0, rows, :] - half_swap(x) * sines[0, rows, :]).astype(jnp.bfloat16)

    ahead = products(*tiles[0])
    outs = []
    for i, (block, head) in enumerate(tiles):
        query, grad, scores, grad_probability = ahead
        if i + 1 < len(tiles):
            ahead = products(*tiles[i + 1])
        low, high = key_span(block, group)
        probability = softmax_rows(scores, masks[block])
        delta = jnp.sum(probability * grad_probability, axis=-1, keepdims=True)
        grad_scores = (probability * (grad_probability - delta)).astype(jnp.bfloat16)
        outs.append(dot(grad_scores, rows_in[0, low:high, width : 2 * width]))
        key_total[low:high, :] += dot_rows(grad_scores, query)
        value_total[low:high, :] += dot_rows(probability.astype(jnp.bfloat16), grad)
        if head == HEADS_DEV - 1:
            rows = slice(block * WINDOW, (block + 1) * WINDOW)
            joint[rows, :width] = unrotated(pick_heads(outs) * SCORE_SCALE, rows)
            outs = []
    for half in range(CORES):
        rows = slice(half * tokens, (half + 1) * tokens)
        joint[rows, width : 2 * width] = unrotated(key_total[rows, :] * SCORE_SCALE, rows)
        joint[rows, 2 * width :] = value_total[rows, :].astype(jnp.bfloat16)

    @pl.when(step == 0)
    def _():
        total[...] = jnp.zeros_like(total)
        sums[...] = jnp.zeros_like(sums)

    both = jnp.concatenate([normed[half] for half in range(CORES)], axis=0)
    total[...] += dot_rows(both, joint[...])
    back[...] = dot_last(joint[...], win[...])
    for half in range(CORES):

        def rows(chunk, half=half):
            part = back[pl.ds(chunk.start + half * tokens, chunk.size), :]
            mean, scaling = stats[half, chunk, 0:1], stats[half, chunk, 1:2]
            unit = (frames[half, chunk, :].astype(jnp.float32) - mean) * scaling
            sums[0:1, :] += jnp.sum(part * unit, axis=0, keepdims=True)
            sums[1:2, :] += jnp.sum(part, axis=0, keepdims=True)

        row_chunks(tokens, 256, rows)
    keep[0] = back[pl.ds(pl.multiple_of(core * tokens, tokens), tokens), :]
    send[0] = back[pl.ds(pl.multiple_of((1 - core) * tokens, tokens), tokens), :].astype(jnp.bfloat16)

    @pl.when(step == TEAM - 1)
    def _():
        for part in range(3):
            term[part] = total[:, part * width : (part + 1) * width].astype(jnp.bfloat16)


def join_terms(parts, out):
    def rows(chunk):
        total = parts[0, chunk, :].astype(jnp.float32)
        for p in range(1, TEAM):
            total = total + parts[p, chunk, :].astype(jnp.float32)
        out[0, chunk, :] = total.astype(jnp.bfloat16)

    row_chunks(D, 256, rows)


def own_sums(last, late, _, grad_in, grad_out, grad_expand, grad_contract, grad_gains, squares):
    rows = grad_in.shape[0]
    devices = last.shape[0]
    total = jnp.zeros((rows, 128), jnp.float32)
    for p in range(SLOTS):
        for part in range(4):
            band = slice(part * rows, (part + 1) * rows)
            value = last[p, band, :].astype(jnp.float32)
            for r in range(1, devices // SLOTS):
                value = value + last[r * SLOTS + p, band, :].astype(jnp.float32)
            total = total + value * value
            begin = p * WIDTH_DEV
            if part < 3:
                grad_in[:, part * D + begin : part * D + begin + WIDTH_DEV] = value
            else:
                grad_out[:, begin : begin + WIDTH_DEV] = value
        for f in range(3 * FF_DEV // 128):
            value = late[p, :, f * 128 : (f + 1) * 128].astype(jnp.float32)
            total = total + value * value
            which, begin = divmod(f * 128, FF_DEV)
            begin += p * FF_DEV
            if which < 2:
                grad_expand[:, which * FF + begin : which * FF + begin + 128] = value
            else:
                grad_contract[:, begin : begin + 128] = value
    value = last[0, 4 * rows : 4 * rows + 16, :].astype(jnp.float32)
    for d in range(1, devices):
        value = value + last[d, 4 * rows : 4 * rows + 16, :].astype(jnp.float32)
    value = value[:8]
    grad_gains[...] = value
    whole = jnp.sum(total) + jnp.sum(value * value)
    squares[...] = jnp.full(squares.shape, whole, jnp.float32)


def adam_all(rates, squares_in, *refs):
    grads, weights, means, squares = refs[:4], refs[4:8], refs[8:12], refs[12:16]
    gain_grads, gains, gain_means, gain_squares = refs[16:20]
    norm_out = refs[22]
    outs, gain_outs = refs[23:39], refs[39:]
    norm = jnp.sqrt(jnp.sum(squares_in[:, 0:1, 0:1]))
    factor = CLIP_NORM / jnp.maximum(norm, CLIP_NORM)
    norm_out[0, 0] = norm

    def update(weight, mean, square, grad, rate, new):
        mean_new, square_new, moved = adam_step(weight, mean, square, grad, factor, rate)
        new[0][...] = mean_new
        new[1][...] = square_new
        new[2][...] = moved
        new[3][...] = moved.astype(jnp.bfloat16)

    for i in range(4):
        update(
            weights[i][...], means[i][...], squares[i][...], grads[i][...], rates[i], outs[i::4]
        )
    count, width = gains.shape
    update(
        gains[...],
        gain_means[...],
        gain_squares[...],
        gain_grads[:count, :width],
        VECTOR_RATE,
        gain_outs,
    )


def frames_back(*refs):
    pieces = refs[: TEAM + 1]
    frames, grad_hidden, vec, _, out = refs[TEAM + 1 :]
    unit, scaling = norm_parts(frames[...].astype(jnp.float32))
    grad_normed = pieces[0][...]
    for piece in pieces[1:]:
        grad_normed = grad_normed + piece[...].astype(jnp.float32)
    out[...] = grad_hidden[...] + norm_back(grad_normed, unit, scaling, vec[0:1, :])


def frames_out(branch, frames, part_out, vec, _, out):
    hidden = frames[...].astype(jnp.float32) + vec[4:5, :] * part_out[...]
    out[...] = (hidden + vec[5:6, :] * branch[...].astype(jnp.float32)).astype(jnp.bfloat16)


def per_device(
    frames,
    clip_lengths,
    cotangent,
    attend_in,
    attend_out,
    expand,
    contract,
    gains,
    prior_mean_attend_in,
    prior_mean_attend_out,
    prior_mean_expand,
    prior_mean_contract,
    prior_mean_gains,
    prior_square_attend_in,
    prior_square_attend_out,
    prior_square_expand,
    prior_square_contract,
    prior_square_gains,
):
    bf16 = jnp.bfloat16
    f32 = jnp.float32
    tokens = frames.shape[0]
    group = tokens * CORES
    rows = attend_in.shape[0]
    gain_width = gains.shape[1]
    reps = lax.axis_size("rep")
    devices = reps * SLOTS
    rep = lax.axis_index("rep")
    team = lax.axis_index("team")
    core = lax.axis_index("tm")

    frames_team = lax.all_gather(frames, MEMBERS, axis=0, tiled=False)

    tail_rows = 16
    lanes = 128
    parts = attend_in.astype(bf16).reshape(rows, 3, SLOTS, WIDTH_DEV).transpose(2, 1, 0, 3)
    parts = jnp.concatenate(
        [parts, attend_out.astype(bf16).reshape(rows, 1, SLOTS, WIDTH_DEV).transpose(2, 1, 0, 3)],
        axis=1,
    ).reshape(SLOTS, 4 * rows, lanes)
    small = jnp.zeros((tail_rows, lanes), f32)
    small = small.at[:6, :gain_width].set(gains)
    small = small.at[6, :3].set((clip_lengths[0] // 16).astype(f32))
    small = small.at[7, :3].set((clip_lengths[0] % 16).astype(f32))
    small = jnp.broadcast_to(small.astype(bf16)[None], (SLOTS, tail_rows, lanes))
    parts = jnp.concatenate([parts, small], axis=1)
    parts = jnp.broadcast_to(parts[None], (reps,) + parts.shape)
    spread = lax.all_to_all(
        parts.reshape(devices, 4 * rows + tail_rows, lanes), ALL, 0, 0, tiled=True
    )
    part_in = spread[:, : 3 * rows].reshape(devices, 3, rows, lanes).transpose(0, 2, 1, 3)
    part_in = part_in.reshape(D, 3 * WIDTH_DEV)
    part_out = spread[:, 3 * rows : 4 * rows].reshape(D, WIDTH_DEV)
    small = spread[:, 4 * rows : 4 * rows + 8].astype(f32)
    vectors = small[:, :6, :gain_width].transpose(1, 0, 2).reshape(6, D)
    vectors = jnp.pad(vectors, ((0, 2), (0, 0)))
    lengths = lax.dynamic_index_in_dim(
        small[:, 6:, :3].reshape(reps, TEAM, CORES, 2, 3)[:, :, 0], rep, 0, keepdims=False
    )
    lengths = (lengths[:, 0] * 16 + lengths[:, 1]).astype(jnp.int32)
    info = jnp.concatenate([lengths.reshape(-1), jnp.stack([core, team])])

    mlp_pack = jnp.concatenate(
        [
            expand.astype(bf16).reshape(rows, 2, SLOTS, FF_DEV).transpose(2, 0, 1, 3).reshape(
                SLOTS, rows, 2 * FF_DEV
            ),
            contract.astype(bf16).reshape(rows, SLOTS, FF_DEV).transpose(1, 0, 2),
        ],
        axis=2,
    )
    mlp_cols = exchange_team(after(mlp_pack, spread)).reshape(SLOTS * rows, 3 * FF_DEV)
    outs_team = gather_team(part_out)
    cots = [cotangent] + send_mates([after(cotangent, mlp_cols)] * (TEAM - 2))

    places = jnp.arange(group, dtype=jnp.int32)
    ends = jnp.cumsum(lengths, axis=1)
    starts = ends - lengths
    begin = jnp.max(
        jnp.where(starts[:, None, :] <= places[None, :, None], starts[:, None, :], 0), axis=2
    )
    offsets = (places[None] - begin).astype(f32)
    freqs = np.power(10000.0, -2.0 * np.arange(HEAD // 2) / HEAD)
    lane_freqs = jnp.asarray(np.tile(freqs, WIDTH_DEV // (HEAD // 2)), dtype=f32)
    angles = offsets[:, :, None] * lane_freqs
    signs = jnp.asarray(np.where(np.arange(WIDTH_DEV) % HEAD < HEAD // 2, -1.0, 1.0), dtype=f32)
    cosines = jnp.cos(angles)
    sines = jnp.sin(angles) * signs
    mlp_weight = lax.all_gather(
        after(mlp_cols, sines, frames_team), ("rep", "tm"), axis=0, tiled=False
    ).reshape(reps, CORES, SLOTS * rows, 3 * FF_DEV)

    by_frames = (CORES, tokens, D)
    by_heads = (CORES, tokens, WIDTH_DEV)
    by_rows = (1, group, 3 * WIDTH_DEV)
    by_angles = (1, group, WIDTH_DEV)
    normed_one, attend_rows, mixed, stats_one = call_groups(
        attend_forward,
        info,
        [
            (in_hbm(frames_team), by_frames),
            (vectors, None),
            (part_in, None),
            (in_hbm(cosines), by_angles),
            (in_hbm(sines), by_angles),
        ],
        [
            ((SLOTS, tokens, D), bf16, by_frames, HBM_OUT),
            ((TEAM, group, 3 * WIDTH_DEV), bf16, by_rows, HBM_OUT),
            ((SLOTS, tokens, WIDTH_DEV), bf16, by_heads, HBM_OUT),
            ((SLOTS, tokens, lanes), f32, (CORES, tokens, lanes), HBM_OUT),
        ],
        name="attend_forward",
        micros=24,
    )

    cots.append(to_mate(after(cotangent, mixed), TEAM - 1))
    mixed_own = exchange_team(mixed)
    attend_part, normed_two, full_out, mixed_flat = call_kernel(
        attend_finish,
        [info, mixed_own, *outs_team, frames, vectors] + [x[:16, :128] for x in cots[1:]],
        [
            ((tokens, D), f32, HBM_OUT),
            ((TEAM, tokens, D), bf16),
            ((D, D), bf16, HBM_OUT),
            ((tokens, D), bf16, HBM_OUT),
        ],
        specs=[SMEM_SPEC] + [VMEM_SPEC] * (SLOTS + 3) + [ANY_SPEC] * (TEAM - 1),
        far=(10,),
        name="attend_finish",
        micros=4,
    )

    normed_team = lax.all_to_all(normed_two, "team", 0, 0, tiled=True)
    by_pairs = (TEAM // 2, tokens, D)
    inner, grads_up, pulls, back = call_groups(
        feed_forward,
        info,
        [
            (normed_team, by_pairs),
            (vectors, None),
            (in_hbm(mlp_weight), "far"),
            *[(in_hbm(x), "far") for x in cots],
        ],
        [
            ((TEAM, tokens, 2 * FF_DEV), bf16, (TEAM // 2, tokens, 2 * FF_DEV), HBM_OUT),
            ((TEAM, tokens, 4 * FF_DEV), bf16, (TEAM // 2, tokens, 4 * FF_DEV), HBM_OUT),
            ((TEAM, tokens, D), bf16, by_pairs, HBM_OUT),
            ((TEAM, tokens, D), bf16, by_pairs, HBM_OUT),
        ],
        scratch=[
            pltpu.VMEM(mlp_weight.shape, bf16),
            pltpu.SemaphoreType.DMA((CORES, mlp_weight.shape[0])),
            pltpu.VMEM((TEAM, tokens, D), bf16),
            pltpu.SemaphoreType.DMA((TEAM,)),
        ],
        steps=2,
        vmem=26,
        name="feed_forward",
        micros=20,
    )
    back_sum = lax.psum_scatter(back, "team", scatter_dimension=0, tiled=False)
    term_own, term_other = call_terms(normed_team, grads_up, pulls, inner)
    term_got = other_core(term_other)
    branch_parts, sums_out = call_kernel(
        feed_branch,
        [info, inner, mlp_weight, term_own[:16, :128], *cots],
        [((TEAM, tokens, D), bf16, HBM_OUT), ((8, D), f32)],
        specs=[SMEM_SPEC] + [VMEM_SPEC] * 2 + [ANY_SPEC] + [VMEM_SPEC] * TEAM,
        far=(1, 4, 5, 6, 7),
        name="feed_branch",
        micros=9,
    )
    branch_sum = lax.psum_scatter(branch_parts, "team", scatter_dimension=0, tiled=False)
    term_got = after(term_got, sums_out)
    term_mlp = (term_own.astype(f32) + term_got.astype(f32)).astype(bf16)
    mlp_sum = lax.psum_scatter(term_mlp, "rep", scatter_dimension=0, tiled=True)

    loads = [attend_part, frames, cotangent, full_out, mixed_flat]
    grad_hidden, sums_two, grad_mixed, term_own, term_other = call_kernel(
        attend_back_start,
        [info, back_sum, vectors, *loads, sums_out],
        [
            ((tokens, D), f32, HBM_OUT),
            ((8, D), f32),
            ((SLOTS, tokens, WIDTH_DEV), bf16),
            ((TEAM, D, WIDTH_DEV), bf16),
            ((TEAM, D, WIDTH_DEV), bf16),
        ],
        scratch=[pltpu.VMEM((tokens, D), bf16)],
        specs=[SMEM_SPEC] + [VMEM_SPEC] * (len(loads) + 2) + [ANY_SPEC],
        far=(1, 3, 4, 5, 6, 7),
        lazy=2,
        vmem=24,
        name="attend_back_start",
        micros=6,
    )
    grad_mixed = exchange_team(grad_mixed)
    out_sum = (term_own.astype(f32) + other_core(term_other).astype(f32)).astype(bf16)
    out_sum = after(out_sum, grad_mixed)
    out_parts = lax.all_to_all(out_sum, "team", 0, 0, tiled=True)
    term_in, sums_one, one_keep, one_send = call_groups(
        attend_backward,
        info,
        [
            (grad_mixed, by_heads),
            (in_hbm(frames_team), by_frames),
            (in_hbm(normed_one), by_frames),
            (in_hbm(attend_rows), by_rows),
            (part_in, None),
            (in_hbm(cosines), by_angles),
            (in_hbm(sines), by_angles),
            (in_hbm(out_sum), "far"),
            (in_hbm(stats_one), (CORES, tokens, lanes)),
        ],
        [
            ((3, D, WIDTH_DEV), bf16, None, HBM_OUT),
            ((8, D), f32, None, PLAIN),
            ((TEAM, tokens, D), f32, (1, tokens, D), HBM_OUT),
            ((TEAM, tokens, D), bf16, (1, tokens, D), HBM_OUT),
        ],
        scratch=[
            pltpu.VMEM((group, 3 * WIDTH_DEV), bf16),
            pltpu.VMEM((group, WIDTH_DEV), f32),
            pltpu.VMEM((group, WIDTH_DEV), f32),
            pltpu.VMEM((group, D), f32),
            pltpu.VMEM((D, 3 * WIDTH_DEV), f32),
        ],
        mates=(0, TEAM),
        name="attend_backward",
        micros=25,
    )
    one_got = other_core(one_send)
    keeps, gots = list(one_keep), list(one_got)
    one_chips = chip_sums(keeps, gots)
    one_pieces = [keeps[0], gots[0]] + send_mates(one_chips)

    (out_part,) = call_kernel(
        join_terms, [out_parts], [((1, D, WIDTH_DEV), bf16)], name="join_terms", micros=1
    )
    terms = jnp.concatenate([term_in, out_part], axis=0)
    term_gains = jnp.concatenate([sums_one[:2], sums_two[:3], sums_out[:1]])
    gains_block = jnp.zeros((devices, tail_rows, lanes), bf16)
    gains_block = gains_block.at[:, :6, :gain_width].set(
        term_gains.astype(bf16).reshape(6, devices, gain_width).transpose(1, 0, 2)
    )
    terms = terms.reshape(4, devices, rows, lanes).transpose(1, 0, 2, 3)
    last = lax.all_to_all(
        jnp.concatenate([terms.reshape(devices, 4 * rows, lanes), gains_block], axis=1),
        ALL,
        0,
        0,
        tiled=True,
    )
    late = exchange_team(after(mlp_sum.reshape(SLOTS, rows, 3 * FF_DEV), last[0, :16]))
    shapes = [(rows, 3 * D), (rows, D), (rows, 2 * FF), (rows, FF), (8, lanes)]
    if rows % 16 == 0:
        *owned, squares_out = call_kernel(
            own_sums,
            [last, late, one_chips[0][:16, :128]],
            [(shape, f32, HBM_OUT) for shape in shapes] + [((devices, 8, lanes), f32)],
            vmem=16,
            name="own_sums",
            micros=4,
        )
    else:
        last_sum = jnp.sum(
            last[:, : 4 * rows].reshape(reps, SLOTS, 4, rows, lanes).astype(f32), axis=0
        )
        late = late.astype(f32)
        owned = [
            last_sum[:, :3].transpose(2, 1, 0, 3).reshape(rows, 3 * D),
            last_sum[:, 3].transpose(1, 0, 2).reshape(rows, D),
            late[:, :, : 2 * FF_DEV]
            .reshape(SLOTS, rows, 2, FF_DEV)
            .transpose(1, 2, 0, 3)
            .reshape(rows, 2 * FF),
            late[:, :, 2 * FF_DEV :].transpose(1, 0, 2).reshape(rows, FF),
            jnp.sum(last[:, 4 * rows : 4 * rows + 8].astype(f32), axis=0),
        ]
        square_part = jnp.zeros((), f32)
        for grad in owned:
            square_part = square_part + jnp.sum(grad * grad)
        squares_out = jnp.full((devices, 8, lanes), square_part)
    squares_in = lax.all_to_all(squares_out, ALL, 0, 0, tiled=True)

    weights = [attend_in, attend_out, expand, contract]
    means = [prior_mean_attend_in, prior_mean_attend_out, prior_mean_expand, prior_mean_contract]
    squares = [
        prior_square_attend_in,
        prior_square_attend_out,
        prior_square_expand,
        prior_square_contract,
    ]
    rates = (RATE / math.sqrt(D), RATE / math.sqrt(D // 64), RATE / math.sqrt(D), RATE / math.sqrt(FF))
    steps = 2
    columns = [pl.BlockSpec((rows, x.shape[1] // steps), lambda i: (0, i)) for x in weights]
    whole = pl.BlockSpec(gains.shape, lambda i: (0, 0))
    out = pl.pallas_call(
        functools.partial(adam_all, rates),
        grid=(steps,),
        in_specs=[pl.BlockSpec(squares_in.shape, lambda i: (0, 0, 0))]
        + columns * 4
        + [pl.BlockSpec((8, lanes), lambda i: (0, 0))]
        + [whole] * 3
        + [ANY_SPEC] * 2,
        out_specs=[pl.BlockSpec(memory_space=pltpu.SMEM)] + columns * 4 + [whole] * 4,
        out_shape=[jax.ShapeDtypeStruct((1, 1), f32)]
        + [
            jax.ShapeDtypeStruct(x.shape, dtype) for dtype in (f32, f32, f32, bf16) for x in weights
        ]
        + [jax.ShapeDtypeStruct(gains.shape, dtype) for dtype in (f32, f32, f32, bf16)],
        compiler_params=pltpu.CompilerParams(vmem_limit_bytes=24 * MIB),
        cost_estimate=cost(8),
        name="adam_all",
    )(
        squares_in,
        *[in_hbm(x) for x in (*owned[:4], *weights, *means, *squares)],
        owned[4],
        gains,
        prior_mean_gains,
        prior_square_gains,
        one_pieces[2][:16, :128],
        one_pieces[3][:16, :128],
    )
    (out_frames,) = call_kernel(
        frames_out,
        [branch_sum, frames, attend_part, vectors, out[-2]],
        [((tokens, D), bf16)],
        specs=[VMEM_SPEC] * 4 + [ANY_SPEC],
        far=(0, 1, 2),
        name="frames_out",
        micros=3,
    )

    (frames_grad,) = call_kernel(
        frames_back,
        [*one_pieces, frames, grad_hidden, vectors, out[-2]],
        [((tokens, D), f32)],
        specs=[VMEM_SPEC] * (TEAM + 4) + [ANY_SPEC],
        name="frames_back",
        micros=4,
    )
    news = [out[1 + kind * 4 + which] for which in range(4) for kind in range(4)]
    return (out_frames, frames_grad, out[0][0, 0], *news, *out[17:])


def solution(mesh):
    teams = Mesh(
        mesh.devices.reshape(mesh.shape["dp"] // TEAM, TEAM, mesh.shape["tm"]), ALL
    )
    by_row = P(ALL, None)
    by_column = P(None, ALL)
    per_group = P(("rep", "team"), None)
    weights = (by_row, by_row, by_row, by_row, by_column)
    return jax.shard_map(
        per_device,
        mesh=teams,
        in_specs=(by_row, per_group, by_row) + weights * 3,
        out_specs=(by_row, by_row, P()) + (by_row,) * 16 + (by_column,) * 4,
        check_vma=False,
    )
```

```python
import functools
import math

import jax
import jax.numpy as jnp
import numpy as np
from jax import lax
from jax.experimental import pallas as pl
from jax.experimental.pallas import tpu as pltpu
from jax.sharding import Mesh
from jax.sharding import PartitionSpec as P

D = 1024
HEADS = 16
HEAD = 64
FF = 4096
WINDOW = 128
STEP = 10

EPS_NORM = 1e-05
NEG_FILL = -1e30
SCORE_SCALE = 0.125
BETA_ONE = 0.9
BETA_TWO = 0.999
ADAM_EPS = 1e-08
DECAY = 0.1
RATE = 3.0
VECTOR_RATE = 0.6
CLIP_NORM = 1.0

TEAM = 4
CORES = 2
SLOTS = TEAM * CORES
ALL = ("rep", "team", "tm")
MEMBERS = ("team", "tm")
ANY_SPEC = pl.BlockSpec(memory_space=pl.ANY)
SMEM_SPEC = pl.BlockSpec(memory_space=pltpu.SMEM)
VMEM_SPEC = pl.BlockSpec(memory_space=pltpu.VMEM)
MIB = 1 << 20
PLAIN, HBM_OUT = range(2)
HBM_SPEC = pl.BlockSpec(memory_space=pltpu.HBM)
LOG2_E = math.log2(math.e)
HEADS_DEV = HEADS // SLOTS
WIDTH_DEV = HEADS_DEV * HEAD
FF_DEV = FF // SLOTS


def swap_pairs(count, bit):
    return [(a, a ^ bit) for a in range(count)]


def other_core(x):
    return lax.ppermute(x, "tm", swap_pairs(CORES, 1))


def to_mate(x, bit):
    return lax.ppermute(x, "team", swap_pairs(TEAM, bit))


def gather_team(x):
    blocks = [x] + [to_mate(x, k) for k in range(1, TEAM)]
    parts = []
    for block in blocks:
        parts += [block, other_core(block)]
    return parts


def chip_sums(keep, got):
    return [
        (keep[k] + got[k].astype(jnp.float32)).astype(jnp.bfloat16) for k in range(1, TEAM)
    ]


def send_mates(chips):
    return [to_mate(chip, k + 1) for k, chip in enumerate(chips)]


def exchange_team(x):
    return lax.all_to_all(x, MEMBERS, 0, 0, tiled=True)


def after(x, *tokens):
    return pl.pallas_call(
        lambda *refs: None,
        out_shape=jax.ShapeDtypeStruct(x.shape, x.dtype),
        in_specs=[ANY_SPEC] * (1 + len(tokens)),
        out_specs=ANY_SPEC,
        input_output_aliases={0: 0},
        name="after",
    )(x, *tokens)


def norm_parts(values):
    centered = values - jnp.mean(values, axis=-1, keepdims=True)
    scaling = lax.rsqrt(jnp.mean(centered * centered, axis=-1, keepdims=True) + EPS_NORM)
    return (centered * scaling, scaling)


def norm_back(gradient, unit_rows, scaling, gain_row):
    scaled = gradient * gain_row
    return scaling * (
        scaled
        - jnp.mean(scaled, axis=-1, keepdims=True)
        - unit_rows * jnp.mean(scaled * unit_rows, axis=-1, keepdims=True)
    )


def dot_rows(left_side, right_side):
    return lax.dot_general(
        left_side, right_side, (((0,), (0,)), ((), ())), preferred_element_type=jnp.float32
    )


def dot_last(left_side, right_side):
    return lax.dot_general(
        left_side, right_side, (((1,), (1,)), ((), ())), preferred_element_type=jnp.float32
    )


def dot(left_side, right_side):
    return jnp.dot(left_side, right_side, preferred_element_type=jnp.float32)


def adam_step(weight, mean_old, square_old, gradient, factor, step_rate):
    clipped = gradient * factor
    mean_new = BETA_ONE * mean_old + (1.0 - BETA_ONE) * clipped
    square_new = BETA_TWO * square_old + (1.0 - BETA_TWO) * clipped * clipped
    mean_hat = mean_new / (1.0 - BETA_ONE**STEP)
    square_hat = square_new / (1.0 - BETA_TWO**STEP)
    moved = weight - step_rate * (mean_hat / (jnp.sqrt(square_hat) + ADAM_EPS) + DECAY * weight)
    return (mean_new, square_new, moved)


def in_hbm(x):
    return pltpu.with_memory_space_constraint(x, pltpu.HBM)


def cost(micros):
    return pl.CostEstimate(flops=int(micros * 1e9), transcendentals=0, bytes_accessed=int(micros * 1e6))


def call_kernel(
    kernel, ins, outs, scratch=(), specs=None, far=(), lazy=0, vmem=16, name=None, micros=2
):
    specs = list(specs or [VMEM_SPEC] * len(ins))
    ins = list(ins)
    buffers = [pltpu.VMEM(ins[i].shape, ins[i].dtype) for i in far]
    for i in far:
        specs[i] = HBM_SPEC
        ins[i] = in_hbm(ins[i])

    def loaded(*refs):
        refs = list(refs)
        if far:
            near, sems = refs[-1 - len(far) : -1], refs[-1]
            refs = refs[: -1 - len(far)]
            copies = [
                pltpu.make_async_copy(refs[i], b, sems.at[n]) for n, (i, b) in enumerate(zip(far, near))
            ]
            for copy in copies:
                copy.start()
            for copy in copies[: len(far) - lazy]:
                copy.wait()
            for i, b in zip(far, near):
                refs[i] = b
        if lazy:
            kernel(copies[len(far) - lazy :], *refs)
        else:
            kernel(*refs)

    return pl.pallas_call(
        loaded,
        out_shape=[
            (pltpu.HBM if mode else jax.ShapeDtypeStruct)(shape, dtype) for shape, dtype, *mode in outs
        ],
        in_specs=specs,
        out_specs=[VMEM_SPEC] * len(outs),
        scratch_shapes=[
            *scratch,
            *buffers,
            *([pltpu.SemaphoreType.DMA((len(far),))] if far else []),
        ],
        compiler_params=pltpu.CompilerParams(vmem_limit_bytes=vmem * MIB),
        cost_estimate=cost(micros),
        name=name,
    )(*ins)


def call_terms(normed, grads, pulls, inner):
    count, tokens, _ = normed.shape
    step = 256
    by_rows = pl.BlockSpec((count, tokens, step), lambda r: (0, 0, r))

    def whole(x):
        return pl.BlockSpec(x.shape, lambda r: (0, 0, 0), pipeline_mode=pl.Buffered(1))

    return pl.pallas_call(
        feed_terms,
        grid=(D // step,),
        in_specs=[by_rows, whole(grads), by_rows, whole(inner)],
        out_specs=[pl.BlockSpec((step, 3 * FF_DEV), lambda r: (r, 0))] * 2,
        out_shape=[
            pltpu.HBM((D, 3 * FF_DEV), jnp.bfloat16),
            jax.ShapeDtypeStruct((D, 3 * FF_DEV), jnp.bfloat16),
        ],
        compiler_params=pltpu.CompilerParams(vmem_limit_bytes=24 * MIB),
        cost_estimate=cost(8),
        name="feed_terms",
    )(in_hbm(normed), in_hbm(grads), in_hbm(pulls), in_hbm(inner))


def call_groups(
    kernel, info, ins, outs, scratch=(), vmem=24, name=None, micros=20, mates=None, steps=TEAM
):
    def spec(shape, block, out):
        rest = (0,) * (len(shape) - 1)
        if block == "far":
            return HBM_SPEC
        if block is None:
            return pl.BlockSpec(
                shape, lambda g, info: (0, *rest), pipeline_mode=None if out else pl.Buffered(1)
            )
        if mates and not out:
            return pl.BlockSpec(block, lambda g, info: (info[3 * TEAM + 1] ^ (mates[0] + g), *rest))
        return pl.BlockSpec(block, lambda g, info: (g, *rest))

    return pl.pallas_call(
        functools.partial(kernel, mates[0] if mates else 0),
        grid_spec=pltpu.PrefetchScalarGridSpec(
            num_scalar_prefetch=1,
            grid=(mates[1] if mates else steps,),
            in_specs=[spec(x.shape, block, False) for x, block in ins],
            out_specs=[spec(shape, block, True) for shape, _, block, _ in outs],
            scratch_shapes=list(scratch),
        ),
        out_shape=[
            jax.ShapeDtypeStruct(shape, dtype) if mode == PLAIN else pltpu.HBM(shape, dtype)
            for shape, dtype, _, mode in outs
        ],
        compiler_params=pltpu.CompilerParams(vmem_limit_bytes=vmem * MIB),
        cost_estimate=cost(micros),
        name=name,
    )(info, *[x for x, _ in ins])


def row_chunks(count, size, body):
    def step(i, carry):
        body(pl.ds(pl.multiple_of(i * size, size), size))
        return carry

    lax.fori_loop(0, count // size, step, 0)


def lanes_of(x):
    return lax.broadcasted_iota(jnp.int32, (1, x.shape[-1]), 1)


def half_swap(x):
    width = x.shape[-1]
    half = HEAD // 2
    first = (lanes_of(x) & half) == 0
    return jnp.where(first, pltpu.roll(x, width - half, x.ndim - 1), pltpu.roll(x, half, x.ndim - 1))


def key_span(block, group):
    return max(0, (block - 1) * WINDOW), min(group, (block + 2) * WINDOW)


def span_mask(info, slot, block, group):
    low, high = key_span(block, group)
    first = info[3 * slot]
    second = first + info[3 * slot + 1]
    third = second + info[3 * slot + 2]
    place = block * WINDOW + lax.broadcasted_iota(jnp.int32, (WINDOW, 1), 0)
    start = jnp.where(
        place >= third,
        third,
        jnp.where(place >= second, second, jnp.where(place >= first, first, 0)),
    )
    end = jnp.where(
        place < first, first, jnp.where(place < second, second, jnp.where(place < third, third, group))
    )
    least = jnp.maximum(start, place - WINDOW)
    most = jnp.minimum(end, place + WINDOW + 1)
    key_place = low + lax.broadcasted_iota(jnp.int32, (1, high - low), 1)
    return (key_place >= least) & (key_place < most)


def head_lanes(x, head):
    lane = lanes_of(x)
    inside = (lane >= head * HEAD) & (lane < (head + 1) * HEAD)
    return jnp.where(inside, x, jnp.zeros_like(x))


def pick_heads(parts):
    out = parts[0]
    for head in range(1, len(parts)):
        out = jnp.where(lanes_of(out) >= head * HEAD, parts[head], out)
    return out


def softmax_rows(products, allowed):
    scores = jnp.where(allowed, products * (SCORE_SCALE * LOG2_E), NEG_FILL)
    exponent = jnp.exp2(scores - jnp.max(scores, axis=-1, keepdims=True))
    return exponent * (1.0 / jnp.sum(exponent, axis=-1, keepdims=True))


def attend_forward(_, info, frames, vec, win, cosines, sines, normed, rows_out, mixed, stats):
    k = pl.program_id(0)
    tokens = frames.shape[1]
    group = CORES * tokens
    width = WIDTH_DEV
    for half in range(CORES):
        rows = slice(half * tokens, (half + 1) * tokens)

        def norm_rows(chunk, half=half):
            values = frames[half, chunk, :].astype(jnp.float32)
            mean = jnp.mean(values, axis=-1, keepdims=True)
            unit, scaling = norm_parts(values)
            stats[half, chunk, :] = jnp.where(lanes_of(stats) == 0, mean, scaling)
            normed[half, chunk, :] = (unit * vec[0:1, :] + vec[1:2, :]).astype(jnp.bfloat16)

        row_chunks(tokens, 256, norm_rows)
        joint = dot(normed[half], win[...])
        for part in range(2):
            x = joint[:, part * width : (part + 1) * width]
            rows_out[0, rows, part * width : (part + 1) * width] = (
                x * cosines[0, rows, :] + half_swap(x) * sines[0, rows, :]
            ).astype(jnp.bfloat16)
        rows_out[0, rows, 2 * width :] = joint[:, 2 * width :].astype(jnp.bfloat16)

    blocks = range(group // WINDOW)
    tiles = [(block, head) for block in blocks for head in range(HEADS_DEV)]
    masks = [span_mask(info, k, block, group) for block in blocks]

    def product(block, head):
        low, high = key_span(block, group)
        query = head_lanes(rows_out[0, block * WINDOW : (block + 1) * WINDOW, :width], head)
        return dot_last(query, rows_out[0, low:high, width : 2 * width])

    ahead = product(*tiles[0])
    outs = []
    for i, (block, head) in enumerate(tiles):
        now = ahead
        if i + 1 < len(tiles):
            ahead = product(*tiles[i + 1])
        low, high = key_span(block, group)
        probability = softmax_rows(now, masks[block]).astype(jnp.bfloat16)
        outs.append(dot(probability, rows_out[0, low:high, 2 * width :]))
        if head == HEADS_DEV - 1:
            half, begin = divmod(block * WINDOW, tokens)
            mixed[half, begin : begin + WINDOW, :] = pick_heads(outs).astype(jnp.bfloat16)
            outs = []


def attend_finish(info, mixed, *refs):
    outs = refs[:SLOTS]
    frames, vec = refs[SLOTS : SLOTS + 2]
    part_out, normed, weight, mixed_out = refs[-4:]
    core, team = info[3 * TEAM], info[3 * TEAM + 1]
    for k in range(TEAM):
        for j in range(CORES):
            s = k * CORES + j
            columns = slice(s * WIDTH_DEV, (s + 1) * WIDTH_DEV)
            weight[:, columns] = outs[s][...]
            mixed_out[:, columns] = mixed[(team ^ k) * CORES + (core ^ j)]
    part_out[...] = dot_last(mixed_out[...], weight[...])

    def rows(chunk):
        hidden = frames[chunk, :].astype(jnp.float32) + vec[4:5, :] * part_out[chunk, :]
        unit, _ = norm_parts(hidden)
        low = (unit * vec[2:3, :] + vec[3:4, :]).astype(jnp.bfloat16)
        for k in range(TEAM):
            normed[k, chunk, :] = low

    row_chunks(frames.shape[0], 256, rows)


def half_weight(weight, core, columns):
    return jnp.concatenate([weight[r, core, :, columns] for r in range(weight.shape[0])], axis=0)


def feed_forward(_, info, normed, vec, far_weight, *refs):
    far_cots = refs[:TEAM]
    inner, grads, pulls, back, weight, sems, cots, cot_sems = refs[TEAM:]
    count, tokens, _ = normed.shape
    half = FF_DEV // 2
    core = info[3 * TEAM]

    def flat(ref):
        return jnp.concatenate([ref[g] for g in range(count)], axis=0)

    def spread(ref, columns, value):
        low = value.astype(jnp.bfloat16)
        for g in range(count):
            ref[g, :, columns] = low[g * tokens : (g + 1) * tokens]

    first = pl.program_id(0) == 0
    copies = [
        [
            pltpu.make_async_copy(far_weight.at[r, core ^ w], weight.at[r, core ^ w], sems.at[w, r])
            for r in range(weight.shape[0])
        ]
        for w in range(CORES)
    ]

    cot_copies = [
        pltpu.make_async_copy(cot, cots.at[info[3 * TEAM + 1] ^ k], cot_sems.at[k])
        for k, cot in enumerate(far_cots)
    ]

    @pl.when(first)
    def _():
        for copy in copies[0] + cot_copies + copies[1]:
            copy.start()

    for w in range(CORES):

        @pl.when(first)
        def _(w=w):
            for copy in copies[w]:
                copy.wait()

        for f in range(2):
            begin = f * half
            gate_cols = slice(begin, begin + half)
            up_cols = slice(FF_DEV + begin, FF_DEV + begin + half)
            out_cols = slice(2 * FF_DEV + begin, 2 * FF_DEV + begin + half)
            gate = dot(flat(normed), half_weight(weight, core ^ w, gate_cols))
            up = dot(flat(normed), half_weight(weight, core ^ w, up_cols))
            if w == f == 0:

                @pl.when(first)
                def _():
                    for copy in cot_copies:
                        copy.wait()

                for g in range(count):
                    cot = cots[count * pl.program_id(0) + g].astype(jnp.float32)
                    pulls[g] = (cot * vec[5:6, :]).astype(jnp.bfloat16)
            grad_inner = dot(flat(pulls), half_weight(weight, core ^ w, out_cols))
            sigmoid = jax.nn.sigmoid(gate)
            silu = gate * sigmoid
            inner_cols = slice(w * FF_DEV + begin, w * FF_DEV + begin + half)
            spread(inner, inner_cols, silu * up)
            slope = grad_inner * up * sigmoid * (1.0 + gate * (1.0 - sigmoid))
            shift = 2 * w * FF_DEV
            spread(grads, slice(shift + begin, shift + begin + half), slope)
            begin += shift + FF_DEV
            spread(grads, slice(begin, begin + half), grad_inner * silu)
    both = jnp.concatenate(
        [half_weight(weight, core ^ w, slice(0, 2 * FF_DEV)) for w in range(CORES)], axis=1
    )
    total = dot_last(flat(grads), both)
    spread(back, slice(None), total)


def feed_branch(info, inner, weight, _, *refs):
    cots, (parts, sums) = refs[:TEAM], refs[TEAM:]
    core, team = info[3 * TEAM], info[3 * TEAM + 1]
    sums[...] = jnp.zeros_like(sums)
    columns = slice(2 * FF_DEV, 3 * FF_DEV)
    both = jnp.concatenate(
        [half_weight(weight, core ^ w, columns) for w in range(CORES)], axis=1
    )
    for k, cot in enumerate(cots):
        part = dot_last(inner[team ^ k], both)
        sums[0:1, :] += jnp.sum(part * cot[...].astype(jnp.float32), axis=0, keepdims=True)
        parts[team ^ k] = part.astype(jnp.bfloat16)


def feed_terms(normed, grads, pulls, inner, own, other):
    def flat(ref, columns):
        return jnp.concatenate([ref[g, :, columns] for g in range(ref.shape[0])], axis=0)

    left, pull = flat(normed, slice(None)), flat(pulls, slice(None))
    term = dot_rows(left, flat(grads, slice(None))).astype(jnp.bfloat16)
    term_out = dot_rows(pull, flat(inner, slice(None))).astype(jnp.bfloat16)
    for w, out in enumerate((own, other)):
        out[:, : 2 * FF_DEV] = term[:, 2 * w * FF_DEV : 2 * (w + 1) * FF_DEV]
        out[:, 2 * FF_DEV :] = term_out[:, w * FF_DEV : (w + 1) * FF_DEV]


def attend_back_start(copies, info, back_sum, vec, part_out, frames, cotangent, weight, mixed, _, *refs):
    grad_hidden, sums, grad_mixed, term_own, term_other, grad_attend = refs
    core, team = info[3 * TEAM], info[3 * TEAM + 1]
    sums[...] = jnp.zeros_like(sums)

    def rows(chunk):
        grad_normed = back_sum[chunk, :].astype(jnp.float32)
        attended = part_out[chunk, :]
        unit, scaling = norm_parts(frames[chunk, :].astype(jnp.float32) + vec[4:5, :] * attended)
        grad = cotangent[chunk, :].astype(jnp.float32) + norm_back(
            grad_normed, unit, scaling, vec[2:3, :]
        )
        grad_hidden[chunk, :] = grad
        grad_attend[chunk, :] = (grad * vec[4:5, :]).astype(jnp.bfloat16)
        sums[0:1, :] += jnp.sum(grad_normed * unit, axis=0, keepdims=True)
        sums[1:2, :] += jnp.sum(grad_normed, axis=0, keepdims=True)
        sums[2:3, :] += jnp.sum(grad * attended, axis=0, keepdims=True)

    row_chunks(frames.shape[0], 256, rows)
    for copy in copies:
        copy.wait()
    grads = dot(grad_attend[...], weight[...]).astype(jnp.bfloat16)
    terms = dot_rows(grad_attend[...], mixed[...]).astype(jnp.bfloat16)
    for k in range(TEAM):
        for j in range(CORES):
            s = k * CORES + j
            columns = slice(s * WIDTH_DEV, (s + 1) * WIDTH_DEV)
            grad_mixed[(team ^ k) * CORES + (core ^ j)] = grads[:, columns]
            (term_other if j else term_own)[team ^ k] = terms[:, columns]


def attend_backward(first, info, *refs):
    grad_mixed, frames, normed, rows_in, win, cosines, sines, _, stats = refs[:9]
    term, sums, keep, send, joint, key_total, value_total, back, total = refs[9:]
    step = pl.program_id(0)
    core = info[3 * TEAM]
    k = info[3 * TEAM + 1] ^ (first + step)
    tokens = frames.shape[1]
    group = CORES * tokens
    width = WIDTH_DEV
    key_total[...] = jnp.zeros_like(key_total)
    value_total[...] = jnp.zeros_like(value_total)
    blocks = range(group // WINDOW)
    tiles = [(block, head) for block in blocks for head in range(HEADS_DEV)]
    masks = [span_mask(info, k, block, group) for block in blocks]

    def products(block, head):
        low, high = key_span(block, group)
        query = head_lanes(rows_in[0, block * WINDOW : (block + 1) * WINDOW, :width], head)
        half, begin = divmod(block * WINDOW, tokens)
        grad = head_lanes(grad_mixed[half, begin : begin + WINDOW, :], head)
        scores = dot_last(query, rows_in[0, low:high, width : 2 * width])
        return query, grad, scores, dot_last(grad, rows_in[0, low:high, 2 * width :])

    def unrotated(x, rows):
        return (x * cosines[0, rows, :] - half_swap(x) * sines[0, rows, :]).astype(jnp.bfloat16)

    ahead = products(*tiles[0])
    outs = []
    for i, (block, head) in enumerate(tiles):
        query, grad, scores, grad_probability = ahead
        if i + 1 < len(tiles):
            ahead = products(*tiles[i + 1])
        low, high = key_span(block, group)
        probability = softmax_rows(scores, masks[block])
        delta = jnp.sum(probability * grad_probability, axis=-1, keepdims=True)
        grad_scores = (probability * (grad_probability - delta)).astype(jnp.bfloat16)
        outs.append(dot(grad_scores, rows_in[0, low:high, width : 2 * width]))
        key_total[low:high, :] += dot_rows(grad_scores, query)
        value_total[low:high, :] += dot_rows(probability.astype(jnp.bfloat16), grad)
        if head == HEADS_DEV - 1:
            rows = slice(block * WINDOW, (block + 1) * WINDOW)
            joint[rows, :width] = unrotated(pick_heads(outs) * SCORE_SCALE, rows)
            outs = []
    for half in range(CORES):
        rows = slice(half * tokens, (half + 1) * tokens)
        joint[rows, width : 2 * width] = unrotated(key_total[rows, :] * SCORE_SCALE, rows)
        joint[rows, 2 * width :] = value_total[rows, :].astype(jnp.bfloat16)

    @pl.when(step == 0)
    def _():
        total[...] = jnp.zeros_like(total)
        sums[...] = jnp.zeros_like(sums)

    both = jnp.concatenate([normed[half] for half in range(CORES)], axis=0)
    total[...] += dot_rows(both, joint[...])
    back[...] = dot_last(joint[...], win[...])
    for half in range(CORES):

        def rows(chunk, half=half):
            part = back[pl.ds(chunk.start + half * tokens, chunk.size), :]
            mean, scaling = stats[half, chunk, 0:1], stats[half, chunk, 1:2]
            unit = (frames[half, chunk, :].astype(jnp.float32) - mean) * scaling
            sums[0:1, :] += jnp.sum(part * unit, axis=0, keepdims=True)
            sums[1:2, :] += jnp.sum(part, axis=0, keepdims=True)

        row_chunks(tokens, 256, rows)
    keep[0] = back[pl.ds(pl.multiple_of(core * tokens, tokens), tokens), :]
    send[0] = back[pl.ds(pl.multiple_of((1 - core) * tokens, tokens), tokens), :].astype(jnp.bfloat16)

    @pl.when(step == TEAM - 1)
    def _():
        for part in range(3):
            term[part] = total[:, part * width : (part + 1) * width].astype(jnp.bfloat16)


def join_terms(parts, out):
    def rows(chunk):
        total = parts[0, chunk, :].astype(jnp.float32)
        for p in range(1, TEAM):
            total = total + parts[p, chunk, :].astype(jnp.float32)
        out[0, chunk, :] = total.astype(jnp.bfloat16)

    row_chunks(D, 256, rows)


def own_sums(last, late, _, grad_in, grad_out, grad_expand, grad_contract, grad_gains, squares):
    rows = grad_in.shape[0]
    devices = last.shape[0]
    total = jnp.zeros((rows, 128), jnp.float32)
    for p in range(SLOTS):
        for part in range(4):
            band = slice(part * rows, (part + 1) * rows)
            value = last[p, band, :].astype(jnp.float32)
            for r in range(1, devices // SLOTS):
                value = value + last[r * SLOTS + p, band, :].astype(jnp.float32)
            total = total + value * value
            begin = p * WIDTH_DEV
            if part < 3:
                grad_in[:, part * D + begin : part * D + begin + WIDTH_DEV] = value
            else:
                grad_out[:, begin : begin + WIDTH_DEV] = value
        for f in range(3 * FF_DEV // 128):
            value = late[p, :, f * 128 : (f + 1) * 128].astype(jnp.float32)
            total = total + value * value
            which, begin = divmod(f * 128, FF_DEV)
            begin += p * FF_DEV
            if which < 2:
                grad_expand[:, which * FF + begin : which * FF + begin + 128] = value
            else:
                grad_contract[:, begin : begin + 128] = value
    value = last[0, 4 * rows : 4 * rows + 16, :].astype(jnp.float32)
    for d in range(1, devices):
        value = value + last[d, 4 * rows : 4 * rows + 16, :].astype(jnp.float32)
    value = value[:8]
    grad_gains[...] = value
    whole = jnp.sum(total) + jnp.sum(value * value)
    squares[...] = jnp.full(squares.shape, whole, jnp.float32)


def adam_all(rates, squares_in, *refs):
    grads, weights, means, squares = refs[:4], refs[4:8], refs[8:12], refs[12:16]
    gain_grads, gains, gain_means, gain_squares = refs[16:20]
    norm_out = refs[23]
    outs, gain_outs = refs[24:40], refs[40:]
    norm = jnp.sqrt(jnp.sum(squares_in[:, 0:1, 0:1]))
    factor = CLIP_NORM / jnp.maximum(norm, CLIP_NORM)
    norm_out[0, 0] = norm

    def update(weight, mean, square, grad, rate, new):
        mean_new, square_new, moved = adam_step(weight, mean, square, grad, factor, rate)
        new[0][...] = mean_new
        new[1][...] = square_new
        new[2][...] = moved
        new[3][...] = moved.astype(jnp.bfloat16)

    for i in range(4):
        update(
            weights[i][...], means[i][...], squares[i][...], grads[i][...], rates[i], outs[i::4]
        )
    count, width = gains.shape
    update(
        gains[...],
        gain_means[...],
        gain_squares[...],
        gain_grads[:count, :width],
        VECTOR_RATE,
        gain_outs,
    )


def frames_back(*refs):
    pieces = refs[: TEAM + 1]
    frames, grad_hidden, vec, _, out = refs[TEAM + 1 :]
    unit, scaling = norm_parts(frames[...].astype(jnp.float32))
    grad_normed = pieces[0][...]
    for piece in pieces[1:]:
        grad_normed = grad_normed + piece[...].astype(jnp.float32)
    out[...] = grad_hidden[...] + norm_back(grad_normed, unit, scaling, vec[0:1, :])


def frames_out(branch, frames, part_out, vec, _, out):
    hidden = frames[...].astype(jnp.float32) + vec[4:5, :] * part_out[...]
    out[...] = (hidden + vec[5:6, :] * branch[...].astype(jnp.float32)).astype(jnp.bfloat16)


def per_device(
    frames,
    clip_lengths,
    cotangent,
    attend_in,
    attend_out,
    expand,
    contract,
    gains,
    prior_mean_attend_in,
    prior_mean_attend_out,
    prior_mean_expand,
    prior_mean_contract,
    prior_mean_gains,
    prior_square_attend_in,
    prior_square_attend_out,
    prior_square_expand,
    prior_square_contract,
    prior_square_gains,
):
    bf16 = jnp.bfloat16
    f32 = jnp.float32
    tokens = frames.shape[0]
    group = tokens * CORES
    rows = attend_in.shape[0]
    gain_width = gains.shape[1]
    reps = lax.axis_size("rep")
    devices = reps * SLOTS
    rep = lax.axis_index("rep")
    team = lax.axis_index("team")
    core = lax.axis_index("tm")

    frames_team = lax.all_gather(frames, MEMBERS, axis=0, tiled=False)

    tail_rows = 16
    lanes = 128
    parts = attend_in.astype(bf16).reshape(rows, 3, SLOTS, WIDTH_DEV).transpose(2, 1, 0, 3)
    parts = jnp.concatenate(
        [parts, attend_out.astype(bf16).reshape(rows, 1, SLOTS, WIDTH_DEV).transpose(2, 1, 0, 3)],
        axis=1,
    ).reshape(SLOTS, 4 * rows, lanes)
    small = jnp.zeros((tail_rows, lanes), f32)
    small = small.at[:6, :gain_width].set(gains)
    small = small.at[6, :3].set((clip_lengths[0] // 16).astype(f32))
    small = small.at[7, :3].set((clip_lengths[0] % 16).astype(f32))
    small = jnp.broadcast_to(small.astype(bf16)[None], (SLOTS, tail_rows, lanes))
    parts = jnp.concatenate([parts, small], axis=1)
    parts = jnp.broadcast_to(parts[None], (reps,) + parts.shape)
    spread = lax.all_to_all(
        parts.reshape(devices, 4 * rows + tail_rows, lanes), ALL, 0, 0, tiled=True
    )
    part_in = spread[:, : 3 * rows].reshape(devices, 3, rows, lanes).transpose(0, 2, 1, 3)
    part_in = part_in.reshape(D, 3 * WIDTH_DEV)
    part_out = spread[:, 3 * rows : 4 * rows].reshape(D, WIDTH_DEV)
    small = spread[:, 4 * rows : 4 * rows + 8].astype(f32)
    vectors = small[:, :6, :gain_width].transpose(1, 0, 2).reshape(6, D)
    vectors = jnp.pad(vectors, ((0, 2), (0, 0)))
    lengths = lax.dynamic_index_in_dim(
        small[:, 6:, :3].reshape(reps, TEAM, CORES, 2, 3)[:, :, 0], rep, 0, keepdims=False
    )
    lengths = (lengths[:, 0] * 16 + lengths[:, 1]).astype(jnp.int32)
    info = jnp.concatenate([lengths.reshape(-1), jnp.stack([core, team])])

    mlp_pack = jnp.concatenate(
        [
            expand.astype(bf16).reshape(rows, 2, SLOTS, FF_DEV).transpose(2, 0, 1, 3).reshape(
                SLOTS, rows, 2 * FF_DEV
            ),
            contract.astype(bf16).reshape(rows, SLOTS, FF_DEV).transpose(1, 0, 2),
        ],
        axis=2,
    )
    mlp_cols = exchange_team(after(mlp_pack, spread)).reshape(SLOTS * rows, 3 * FF_DEV)
    outs_team = gather_team(part_out)
    cots = [cotangent] + send_mates([after(cotangent, mlp_cols)] * (TEAM - 2))

    places = jnp.arange(group, dtype=jnp.int32)
    ends = jnp.cumsum(lengths, axis=1)
    starts = ends - lengths
    begin = jnp.max(
        jnp.where(starts[:, None, :] <= places[None, :, None], starts[:, None, :], 0), axis=2
    )
    offsets = (places[None] - begin).astype(f32)
    freqs = np.power(10000.0, -2.0 * np.arange(HEAD // 2) / HEAD)
    lane_freqs = jnp.asarray(np.tile(freqs, WIDTH_DEV // (HEAD // 2)), dtype=f32)
    angles = offsets[:, :, None] * lane_freqs
    signs = jnp.asarray(np.where(np.arange(WIDTH_DEV) % HEAD < HEAD // 2, -1.0, 1.0), dtype=f32)
    cosines = jnp.cos(angles)
    sines = jnp.sin(angles) * signs
    mlp_weight = lax.all_gather(
        after(mlp_cols, sines, frames_team), ("rep", "tm"), axis=0, tiled=False
    ).reshape(reps, CORES, SLOTS * rows, 3 * FF_DEV)

    by_frames = (CORES, tokens, D)
    by_heads = (CORES, tokens, WIDTH_DEV)
    by_rows = (1, group, 3 * WIDTH_DEV)
    by_angles = (1, group, WIDTH_DEV)
    normed_one, attend_rows, mixed, stats_one = call_groups(
        attend_forward,
        info,
        [
            (in_hbm(frames_team), by_frames),
            (vectors, None),
            (part_in, None),
            (in_hbm(cosines), by_angles),
            (in_hbm(sines), by_angles),
        ],
        [
            ((SLOTS, tokens, D), bf16, by_frames, HBM_OUT),
            ((TEAM, group, 3 * WIDTH_DEV), bf16, by_rows, HBM_OUT),
            ((SLOTS, tokens, WIDTH_DEV), bf16, by_heads, HBM_OUT),
            ((SLOTS, tokens, lanes), f32, (CORES, tokens, lanes), HBM_OUT),
        ],
        name="attend_forward",
        micros=24,
    )

    cots.append(to_mate(after(cotangent, mixed), TEAM - 1))
    mixed_own = exchange_team(mixed)
    attend_part, normed_two, full_out, mixed_flat = call_kernel(
        attend_finish,
        [info, mixed_own, *outs_team, frames, vectors] + [x[:16, :128] for x in cots[1:]],
        [
            ((tokens, D), f32, HBM_OUT),
            ((TEAM, tokens, D), bf16),
            ((D, D), bf16, HBM_OUT),
            ((tokens, D), bf16, HBM_OUT),
        ],
        specs=[SMEM_SPEC] + [VMEM_SPEC] * (SLOTS + 3) + [ANY_SPEC] * (TEAM - 1),
        far=(10,),
        name="attend_finish",
        micros=4,
    )

    normed_team = lax.all_to_all(normed_two, "team", 0, 0, tiled=True)
    by_pairs = (TEAM // 2, tokens, D)
    inner, grads_up, pulls, back = call_groups(
        feed_forward,
        info,
        [
            (normed_team, by_pairs),
            (vectors, None),
            (in_hbm(mlp_weight), "far"),
            *[(in_hbm(x), "far") for x in cots],
        ],
        [
            ((TEAM, tokens, 2 * FF_DEV), bf16, (TEAM // 2, tokens, 2 * FF_DEV), HBM_OUT),
            ((TEAM, tokens, 4 * FF_DEV), bf16, (TEAM // 2, tokens, 4 * FF_DEV), HBM_OUT),
            ((TEAM, tokens, D), bf16, by_pairs, HBM_OUT),
            ((TEAM, tokens, D), bf16, by_pairs, HBM_OUT),
        ],
        scratch=[
            pltpu.VMEM(mlp_weight.shape, bf16),
            pltpu.SemaphoreType.DMA((CORES, mlp_weight.shape[0])),
            pltpu.VMEM((TEAM, tokens, D), bf16),
            pltpu.SemaphoreType.DMA((TEAM,)),
        ],
        steps=2,
        vmem=26,
        name="feed_forward",
        micros=20,
    )
    back_sum = lax.psum_scatter(back, "team", scatter_dimension=0, tiled=False)
    term_own, term_other = call_terms(normed_team, grads_up, pulls, inner)
    term_got = other_core(term_other)
    branch_parts, sums_out = call_kernel(
        feed_branch,
        [info, inner, mlp_weight, term_own[:16, :128], *cots],
        [((TEAM, tokens, D), bf16, HBM_OUT), ((8, D), f32)],
        specs=[SMEM_SPEC] + [VMEM_SPEC] * 2 + [ANY_SPEC] + [VMEM_SPEC] * TEAM,
        far=(1, 4, 5, 6, 7),
        name="feed_branch",
        micros=9,
    )
    branch_sum = lax.psum_scatter(branch_parts, "team", scatter_dimension=0, tiled=False)
    term_got = after(term_got, sums_out)
    term_mlp = (term_own.astype(f32) + term_got.astype(f32)).astype(bf16)
    mlp_sum = lax.psum_scatter(term_mlp, "rep", scatter_dimension=0, tiled=True)

    loads = [attend_part, frames, cotangent, full_out, mixed_flat]
    grad_hidden, sums_two, grad_mixed, term_own, term_other = call_kernel(
        attend_back_start,
        [info, back_sum, vectors, *loads, sums_out],
        [
            ((tokens, D), f32, HBM_OUT),
            ((8, D), f32),
            ((SLOTS, tokens, WIDTH_DEV), bf16),
            ((TEAM, D, WIDTH_DEV), bf16),
            ((TEAM, D, WIDTH_DEV), bf16),
        ],
        scratch=[pltpu.VMEM((tokens, D), bf16)],
        specs=[SMEM_SPEC] + [VMEM_SPEC] * (len(loads) + 2) + [ANY_SPEC],
        far=(1, 3, 4, 5, 6, 7),
        lazy=2,
        vmem=24,
        name="attend_back_start",
        micros=6,
    )
    grad_mixed = exchange_team(grad_mixed)
    out_sum = (term_own.astype(f32) + other_core(term_other).astype(f32)).astype(bf16)
    out_sum = after(out_sum, grad_mixed)
    out_parts = lax.all_to_all(out_sum, "team", 0, 0, tiled=True)
    term_in, sums_one, one_keep, one_send = call_groups(
        attend_backward,
        info,
        [
            (grad_mixed, by_heads),
            (in_hbm(frames_team), by_frames),
            (in_hbm(normed_one), by_frames),
            (in_hbm(attend_rows), by_rows),
            (part_in, None),
            (in_hbm(cosines), by_angles),
            (in_hbm(sines), by_angles),
            (in_hbm(out_sum), "far"),
            (in_hbm(stats_one), (CORES, tokens, lanes)),
        ],
        [
            ((3, D, WIDTH_DEV), bf16, None, HBM_OUT),
            ((8, D), f32, None, PLAIN),
            ((TEAM, tokens, D), f32, (1, tokens, D), HBM_OUT),
            ((TEAM, tokens, D), bf16, (1, tokens, D), HBM_OUT),
        ],
        scratch=[
            pltpu.VMEM((group, 3 * WIDTH_DEV), bf16),
            pltpu.VMEM((group, WIDTH_DEV), f32),
            pltpu.VMEM((group, WIDTH_DEV), f32),
            pltpu.VMEM((group, D), f32),
            pltpu.VMEM((D, 3 * WIDTH_DEV), f32),
        ],
        mates=(0, TEAM),
        name="attend_backward",
        micros=25,
    )
    one_got = other_core(one_send)
    keeps, gots = list(one_keep), list(one_got)
    one_chips = chip_sums(keeps, gots)
    one_pieces = [keeps[0], gots[0]] + send_mates(one_chips)

    (out_part,) = call_kernel(
        join_terms, [out_parts], [((1, D, WIDTH_DEV), bf16)], name="join_terms", micros=1
    )
    terms = jnp.concatenate([term_in, out_part], axis=0)
    term_gains = jnp.concatenate([sums_one[:2], sums_two[:3], sums_out[:1]])
    gains_block = jnp.zeros((devices, tail_rows, lanes), bf16)
    gains_block = gains_block.at[:, :6, :gain_width].set(
        term_gains.astype(bf16).reshape(6, devices, gain_width).transpose(1, 0, 2)
    )
    terms = terms.reshape(4, devices, rows, lanes).transpose(1, 0, 2, 3)
    last = lax.all_to_all(
        jnp.concatenate([terms.reshape(devices, 4 * rows, lanes), gains_block], axis=1),
        ALL,
        0,
        0,
        tiled=True,
    )
    late = exchange_team(after(mlp_sum.reshape(SLOTS, rows, 3 * FF_DEV), last[0, :16]))
    shapes = [(rows, 3 * D), (rows, D), (rows, 2 * FF), (rows, FF), (8, lanes)]
    if rows % 16 == 0:
        *owned, squares_out = call_kernel(
            own_sums,
            [last, late, one_chips[0][:16, :128]],
            [(shape, f32, HBM_OUT) for shape in shapes] + [((devices, 8, lanes), f32)],
            vmem=16,
            name="own_sums",
            micros=4,
        )
    else:
        last_sum = jnp.sum(
            last[:, : 4 * rows].reshape(reps, SLOTS, 4, rows, lanes).astype(f32), axis=0
        )
        late = late.astype(f32)
        owned = [
            last_sum[:, :3].transpose(2, 1, 0, 3).reshape(rows, 3 * D),
            last_sum[:, 3].transpose(1, 0, 2).reshape(rows, D),
            late[:, :, : 2 * FF_DEV]
            .reshape(SLOTS, rows, 2, FF_DEV)
            .transpose(1, 2, 0, 3)
            .reshape(rows, 2 * FF),
            late[:, :, 2 * FF_DEV :].transpose(1, 0, 2).reshape(rows, FF),
            jnp.sum(last[:, 4 * rows : 4 * rows + 8].astype(f32), axis=0),
        ]
        square_part = jnp.zeros((), f32)
        for grad in owned:
            square_part = square_part + jnp.sum(grad * grad)
        squares_out = jnp.full((devices, 8, lanes), square_part)
    squares_in = lax.all_to_all(squares_out, ALL, 0, 0, tiled=True)

    (out_frames,) = call_kernel(
        frames_out,
        [branch_sum, frames, attend_part, vectors, squares_out],
        [((tokens, D), bf16)],
        specs=[VMEM_SPEC] * 4 + [ANY_SPEC],
        far=(0, 1, 2),
        name="frames_out",
        micros=3,
    )

    weights = [attend_in, attend_out, expand, contract]
    means = [prior_mean_attend_in, prior_mean_attend_out, prior_mean_expand, prior_mean_contract]
    squares = [
        prior_square_attend_in,
        prior_square_attend_out,
        prior_square_expand,
        prior_square_contract,
    ]
    rates = (RATE / math.sqrt(D), RATE / math.sqrt(D // 64), RATE / math.sqrt(D), RATE / math.sqrt(FF))
    steps = 2
    columns = [pl.BlockSpec((rows, x.shape[1] // steps), lambda i: (0, i)) for x in weights]
    whole = pl.BlockSpec(gains.shape, lambda i: (0, 0))
    out = pl.pallas_call(
        functools.partial(adam_all, rates),
        grid=(steps,),
        in_specs=[pl.BlockSpec(squares_in.shape, lambda i: (0, 0, 0))]
        + columns * 4
        + [pl.BlockSpec((8, lanes), lambda i: (0, 0))]
        + [whole] * 3
        + [ANY_SPEC] * 3,
        out_specs=[pl.BlockSpec(memory_space=pltpu.SMEM)] + columns * 4 + [whole] * 4,
        out_shape=[jax.ShapeDtypeStruct((1, 1), f32)]
        + [
            jax.ShapeDtypeStruct(x.shape, dtype) for dtype in (f32, f32, f32, bf16) for x in weights
        ]
        + [jax.ShapeDtypeStruct(gains.shape, dtype) for dtype in (f32, f32, f32, bf16)],
        compiler_params=pltpu.CompilerParams(vmem_limit_bytes=24 * MIB),
        cost_estimate=cost(8),
        name="adam_all",
    )(
        squares_in,
        *[in_hbm(x) for x in (*owned[:4], *weights, *means, *squares)],
        owned[4],
        gains,
        prior_mean_gains,
        prior_square_gains,
        one_pieces[2][:16, :128],
        one_pieces[3][:16, :128],
        out_frames,
    )
    (frames_grad,) = call_kernel(
        frames_back,
        [*one_pieces, frames, grad_hidden, vectors, out[-2]],
        [((tokens, D), f32)],
        specs=[VMEM_SPEC] * (TEAM + 4) + [ANY_SPEC],
        name="frames_back",
        micros=4,
    )
    news = [out[1 + kind * 4 + which] for which in range(4) for kind in range(4)]
    return (out_frames, frames_grad, out[0][0, 0], *news, *out[17:])


def solution(mesh):
    teams = Mesh(
        mesh.devices.reshape(mesh.shape["dp"] // TEAM, TEAM, mesh.shape["tm"]), ALL
    )
    by_row = P(ALL, None)
    by_column = P(None, ALL)
    per_group = P(("rep", "team"), None)
    weights = (by_row, by_row, by_row, by_row, by_column)
    return jax.shard_map(
        per_device,
        mesh=teams,
        in_specs=(by_row, per_group, by_row) + weights * 3,
        out_specs=(by_row, by_row, P()) + (by_row,) * 16 + (by_column,) * 4,
        check_vma=False,
    )
```
